32 devices in a mesh: dp: 16 (over z, y, x), group: 2 (over core).
Axes of the slice: x: 2, y: 2, z: 4, core: 2. Of those that a mesh axis runs over, the one named last changes fastest.
Arguments:
- tokens: bfloat16 [32, 1024, 768], P(('dp', 'group')), may hold values from -6 to 6
- segments: int32 [32, 1024], P(('dp', 'group')), may hold values from 0 to 7, never falling along the last dimension, each value on 1 to 256 neighbouring positions
- labels: int32 [32], P(('dp', 'group')), may hold values from 0 to 2, as said below
- cotangent: bfloat16 [32, 1024, 768], P(('dp', 'group')), may hold values from -6 to 6
- w_qkv: bfloat16 [768, 2304], replicated, may hold values from -0.21875 to 0.21875
- b_query: float32 [768], replicated, may hold values from -3 to 3
- b_value: float32 [768], replicated, may hold values from -3 to 3
- w_out: bfloat16 [768, 768], replicated, may hold values from -0.875 to 0.875
- b_out: float32 [768], replicated, may hold values from -2 to 2
- gamma_one: float32 [768], replicated, may hold values from 0.5 to 1.5
- beta_one: float32 [768], replicated, may hold values from -2 to 2
- gamma_two: float32 [768], replicated, may hold values from 0.5 to 1.5
- beta_two: float32 [768], replicated, may hold values from -2 to 2
- w_up: bfloat16 [768, 3072], replicated, may hold values from -0.21875 to 0.21875
- b_up: float32 [3072], replicated, may hold values from -3 to 3
- w_down: bfloat16 [3072, 768], replicated, may hold values from -0.109375 to 0.109375
- b_down: float32 [768], replicated, may hold values from -2 to 2
Outputs:
- mixed: bfloat16 [32, 1024, 768], P(('dp', 'group'))
- grad_tokens: bfloat16 [32, 1024, 768], P(('dp', 'group'))
- grad_w_qkv: float32 [768, 2304], P('dp')
- grad_b_query: float32 [768], P('dp')
- grad_b_value: float32 [768], P('dp')
- grad_w_out: float32 [768, 768], P('dp')
- grad_b_out: float32 [768], P('dp')
- grad_gamma_one: float32 [768], P('dp')
- grad_beta_one: float32 [768], P('dp')
- grad_gamma_two: float32 [768], P('dp')
- grad_beta_two: float32 [768], P('dp')
- grad_w_up: float32 [768, 3072], P('dp')
- grad_b_up: float32 [3072], P('dp')
- grad_w_down: float32 [3072, 768], P('dp')
- grad_b_down: float32 [768], P('dp')
- counts: int32 [3], replicated
The draws below stay inside these ranges and needn't reach their ends.
Inputs may be any that keep to these rules, and one draw needn't show every extreme that they name: Taken in window order, the labels form 3 runs, one for each task, in an order that varies; each run covers whole consecutive indices of dp (all windows of a device and of both cores of a chip share a label) and at least max(1, 2) of them, so every task has windows.
All inputs are finite; a program needn't handle non-finite values.
Results may differ from the reference program's by a relative error of at most 0.015.
Values sent between devices are 32-bit elements; how exact they have to be, the bound alone decides.
No kernel may reach another device: no remote copies, remote signals or barrier semaphores. Data moves between devices by JAX's collectives and lax.ppermute only.
A program may use at most 256 MiB of HBM per device.

```python
import math
import jax
import jax.numpy as jnp
import numpy as np
from jax import lax

D = 768
HEADS = 12
HEAD = 64
FF = 3072
WIN = 1024
NTASK = 3
WIN_DEV = 1
WINDOWS = 32
N_DP = 16
N_GROUP = 2


def draw_labels(key, part):
    key = jax.random.fold_in(key, 11)
    cut_key, order_key = jax.random.split(key)
    least_run = max(1, N_DP // 8)
    spare_dp = N_DP - NTASK * least_run
    cut_points = jax.random.randint(cut_key, (2,), 0, spare_dp + 1, dtype=jnp.int32)
    first_end = least_run + jnp.min(cut_points)
    second_end = 2 * least_run + jnp.max(cut_points)
    task_order = jax.random.permutation(order_key, NTASK).astype(jnp.int32)
    dp_position = jnp.arange(WINDOWS, dtype=jnp.int32) // (WIN_DEV * N_GROUP)
    run_number = (dp_position >= first_end).astype(jnp.int32) + (dp_position >= second_end).astype(jnp.int32)
    return task_order[run_number].astype(jnp.int32)


def block_levels(rng, shape, pieces, least, largest):
    def one(dim, parts):
        heights = jax.random.uniform(jax.random.fold_in(jax.random.fold_in(rng, 6), dim), (parts,), jnp.float32, least / len(pieces), largest / len(pieces))
        return jnp.repeat(jnp.exp(heights), shape[dim] // parts).reshape((-1,) + (1,) * (len(shape) - dim - 1))

    loudness = one(*pieces[0])
    for cut in pieces[1:]:
        loudness = loudness * one(*cut)
    return loudness


def profile(count, total, reach, lean):
    weights = [(1 << 20) // math.isqrt(grade ** lean) + 1 for grade in range(2, count + 1)]
    spare, given = total - reach - (count - 1), [1] * (count - 1)
    while spare > 0:
        movable = [i for i in range(count - 1) if given[i] < reach]
        pool, budget = sum([weights[i] for i in movable]), spare
        for i in movable:
            more = min(reach - given[i], max(1, budget * weights[i] // pool), spare)
            given[i] = given[i] + more
            spare = spare - more
    return np.array([reach] + given)


def ragged(rng, count, total, bound, lean):
    if count == 2:
        one = jax.random.randint(rng, (), max(1, total - bound), min(bound, total - 1) + 1)
        return jnp.stack([one, total - one])
    lengths = jnp.asarray(profile(count, total, bound, lean), jnp.int32)
    pairs = (count - 1) // 2
    giver, sink = lengths[1:1 + 2 * pairs:2], lengths[2:2 + 2 * pairs:2]
    room = jnp.minimum(giver - 1, bound - sink)
    moved = jax.random.randint(jax.random.fold_in(rng, 1), (pairs,), 0, 1 << 20) % (room + 1)
    lengths = lengths.at[1:1 + 2 * pairs:2].set(giver - moved).at[2:2 + 2 * pairs:2].set(sink + moved)
    return lengths[jax.random.permutation(jax.random.fold_in(rng, 2), count)]


def scatter_about(key, dims, scale, limit, pieces=(), held_as=jnp.bfloat16):
    array = jax.random.normal(key, dims, jnp.float32) * scale
    if len(pieces) > 0:
        array = block_levels(key, dims, pieces, -0.22, 0.18) * array
    return jnp.clip(array, min=-limit, max=limit).astype(held_as)


def setup_inputs(seed: int = 0) -> dict:
    arg_keys = jax.random.split(jax.random.key(seed), 18)
    tokens = scatter_about(arg_keys[0], (WINDOWS, WIN, D), 1.0, 6.0, ((0, 32),))
    segments = jax.vmap(lambda own: jnp.searchsorted(jnp.cumsum(ragged(own, 8, WIN, WIN // 4, 1)), jnp.arange(WIN), side="right"))(jax.random.split(arg_keys[1], WINDOWS)).reshape((WINDOWS, WIN)).astype(jnp.int32)
    labels = draw_labels(jax.random.fold_in(arg_keys[17], 71), 0)
    cotangent = scatter_about(arg_keys[3], (WINDOWS, WIN, D), 1.0, 6.0, ((0, 32),))
    w_qkv = scatter_about(arg_keys[4], (D, 3 * D), D ** -0.5, 0.21875)
    b_query = scatter_about(arg_keys[5], (D,), 0.5, 3.0, (), jnp.float32)
    b_value = scatter_about(arg_keys[6], (D,), 0.5, 3.0, (), jnp.float32)
    w_out = scatter_about(arg_keys[7], (D, D), (D // 16) ** -0.5, 0.875)
    b_out = scatter_about(arg_keys[8], (D,), 0.3, 2.0, (), jnp.float32)
    gamma_one = jnp.clip(1.0 + 0.1 * jax.random.normal(arg_keys[9], (D,), jnp.float32), 0.5, 1.5)
    beta_one = scatter_about(arg_keys[10], (D,), 0.3, 2.0, (), jnp.float32)
    gamma_two = jnp.clip(1.0 + 0.1 * jax.random.normal(arg_keys[11], (D,), jnp.float32), 0.5, 1.5)
    beta_two = scatter_about(arg_keys[12], (D,), 0.3, 2.0, (), jnp.float32)
    w_up = scatter_about(arg_keys[13], (D, FF), D ** -0.5, 0.21875)
    b_up = scatter_about(arg_keys[14], (FF,), 0.5, 3.0, (), jnp.float32)
    w_down = scatter_about(arg_keys[15], (FF, D), FF ** -0.5, 0.109375)
    b_down = scatter_about(arg_keys[16], (D,), 0.3, 2.0, (), jnp.float32)
    return {"tokens": tokens, "segments": segments, "labels": labels, "cotangent": cotangent, "w_qkv": w_qkv, "b_query": b_query, "b_value": b_value, "w_out": w_out, "b_out": b_out, "gamma_one": gamma_one, "beta_one": beta_one, "gamma_two": gamma_two, "beta_two": beta_two, "w_up": w_up, "b_up": b_up, "w_down": w_down, "b_down": b_down}


@jax.custom_vjp
def low(v):
    return lax.optimization_barrier(v.astype(jnp.bfloat16)).astype(jnp.float32)

@jax.custom_vjp
def low_back(v):
    return v

def low_keep(v):
    return (low(v), None)

def low_pass(kept, grad):
    return (grad,)

def back_keep(v):
    return (v, None)

def back_low(kept, grad):
    return (low(grad),)
low.defvjp(low_keep, low_pass)
low_back.defvjp(back_keep, back_low)

def normalize(value, gain, shift):
    average = lax.optimization_barrier(jnp.mean(value, axis=-1, keepdims=True))
    centered = value - average
    variance = lax.optimization_barrier(jnp.mean(centered * centered, axis=-1, keepdims=True))
    return centered * lax.rsqrt(variance + 1e-05) * gain + shift

def forward(params, residual_in, segment_ids):
    w_qkv, b_query, b_value, w_out, b_out, gamma_one, beta_one, gamma_two, beta_two, w_up, b_up, w_down, b_down = params
    highest = lax.Precision.HIGHEST
    window = residual_in.shape[0]
    col_scale = jnp.concatenate([jnp.full((D,), HEAD ** (-0.5), jnp.float32), jnp.ones((2 * D,), jnp.float32)])
    bias_all = jnp.concatenate([b_query, jnp.zeros((D,), jnp.float32), b_value])
    input_one = low(normalize(residual_in, gamma_one, beta_one))
    projected = (jnp.dot(input_one, w_qkv, precision=highest) + bias_all) * col_scale
    projected = low_back(low(projected))
    split = projected.reshape(window, 3, HEADS, HEAD)
    scores = jnp.einsum('qhd,khd->hqk', split[:, 0], split[:, 1], precision=highest)
    position = jnp.arange(window)
    allowed = (position[None, :] <= position[:, None]) & (segment_ids[:, None] == segment_ids[None, :])
    scores = jnp.where(allowed[None], low_back(scores), -1e+30)
    probs = low(jax.nn.softmax(scores, axis=-1))
    attended = jnp.einsum('hqk,khd->qhd', probs, split[:, 2], precision=highest).reshape(window, D)
    attended = low_back(low(attended))
    branch = low_back(jnp.dot(attended, w_out, precision=highest) + b_out)
    middle = residual_in + branch
    input_two = low(normalize(middle, gamma_two, beta_two))
    hidden_pre = low_back(jnp.dot(input_two, w_up, precision=highest) + b_up)
    hidden_act = low(jax.nn.gelu(hidden_pre, approximate=False))
    return middle + jnp.dot(hidden_act, w_down, precision=highest) + b_down

def reference(tokens, segments, labels, cotangent, w_qkv, b_query, b_value, w_out, b_out, gamma_one, beta_one, gamma_two, beta_two, w_up, b_up, w_down, b_down):
    params = tuple((p.astype(jnp.float32) for p in (w_qkv, b_query, b_value, w_out, b_out, gamma_one, beta_one, gamma_two, beta_two, w_up, b_up, w_down, b_down)))
    task_hits = labels[:, None] == jnp.arange(NTASK, dtype=jnp.int32)[None, :]
    counts = lax.optimization_barrier(jnp.sum(task_hits.astype(jnp.int32), axis=0)) * WIN
    task_weight = jnp.sum(counts).astype(jnp.float32) / (NTASK * counts.astype(jnp.float32))
    window_weight = lax.optimization_barrier(jnp.sum(jnp.where(task_hits, task_weight[None, :], jnp.float32(0.0)), axis=1))

    def step(totals, window_item):
        token_rows, segment_ids, cot_rows, weight_one = window_item
        result, pullback = jax.vjp(lambda prm, val: forward(prm, val, segment_ids), params, token_rows.astype(jnp.float32))
        weighted = low(cot_rows.astype(jnp.float32) * weight_one)
        grad_params, grad_input = pullback(weighted)
        totals = jax.tree.map(lambda a, b: a + b, totals, grad_params)
        return (totals, (result.astype(jnp.bfloat16), grad_input.astype(jnp.bfloat16)))
    start_totals = jax.tree.map(jnp.zeros_like, params)
    totals, (mixed, grad_tokens) = lax.scan(step, start_totals, (tokens, segments, cotangent, window_weight))
    return (mixed, grad_tokens, totals[0], totals[1], totals[2], totals[3], totals[4], totals[5], totals[6], totals[7], totals[8], totals[9], totals[10], totals[11], totals[12], counts)
```

```python
import functools
import math

import jax
import jax.numpy as jnp
from jax import lax
from jax.experimental import pallas as pl
from jax.experimental.pallas import tpu as pltpu
from jax.sharding import PartitionSpec as P

F32 = jnp.float32
BF = jnp.bfloat16
D = 768
HEADS = 12
HEAD = 64
PAIR = 2 * HEAD
FF = 3072
NTASK = 3
QB = 256
HALF = D // 2
AXES = ("dp", "group")
NN = (((1,), (0,)), ((), ()))
NT = (((1,), (1,)), ((), ()))
TN = (((0,), (0,)), ((), ()))


def dot(a, b, dims=NN):
    return lax.dot_general(a, b, dims, preferred_element_type=F32)


def call(kernel, name, grid, in_specs, out_specs, out_shape, scratch=(), prefetch=0, flops=0, after=0):
    in_specs = list(in_specs) + [pl.BlockSpec(memory_space=pl.ANY)] * after
    moved = sum(math.prod(s.shape) * s.dtype.itemsize for s in jax.tree.leaves(out_shape))
    body = kernel
    if after:
        start = prefetch + len(in_specs) - after

        def body(*refs):
            kernel(*refs[:start], *refs[start + after :])

    return pl.pallas_call(
        body,
        grid_spec=pltpu.PrefetchScalarGridSpec(
            num_scalar_prefetch=prefetch,
            grid=grid,
            in_specs=in_specs,
            out_specs=out_specs,
            scratch_shapes=list(scratch),
        ),
        out_shape=out_shape,
        compiler_params=pltpu.CompilerParams(vmem_limit_bytes=56 * 2**20),
        cost_estimate=pl.CostEstimate(flops=flops, bytes_accessed=2 * moved, transcendentals=0),
        name=name,
    )


def shape(dims, dtype):
    return jax.ShapeDtypeStruct(dims, dtype)


def whole(*dims):
    return pl.BlockSpec(dims, lambda *_: (0,) * len(dims))


SMEM = pl.BlockSpec(memory_space=pltpu.SMEM)


def unit(x):
    centered = x - jnp.mean(x, axis=-1, keepdims=True)
    inv = lax.rsqrt(jnp.mean(centered * centered, axis=-1, keepdims=True) + 1e-05)
    return centered * inv, inv


def norm_back(e, u, inv, gain):
    scaled = e * gain
    return inv * (
        scaled
        - jnp.mean(scaled, axis=-1, keepdims=True)
        - u * jnp.mean(scaled * u, axis=-1, keepdims=True)
    )


def rows_of(ref):
    return range(0, ref.shape[0], QB)


def column_sum(x):
    return jnp.sum(x, axis=0, keepdims=True)


def project_kernel(x_ref, g_ref, b_ref, w_ref, bias_ref, proj_ref, in_ref):
    j = pl.program_id(0)

    @pl.when(j == 0)
    def _():
        for r in rows_of(x_ref):
            u, _ = unit(x_ref[r : r + QB].astype(F32))
            in_ref[r : r + QB] = (u * g_ref[...] + b_ref[...]).astype(BF)

    scale = jnp.where(j == 0, HEAD**-0.5, 1.0).astype(F32)
    proj_ref[...] = ((dot(in_ref[...], w_ref[...]) + bias_ref[0]) * scale).astype(BF)


def project(x, gain, shift, w_qkv, bias):
    t = x.shape[0]
    return call(
        project_kernel,
        "norm_project",
        (3,),
        [
            whole(t, D),
            whole(1, D),
            whole(1, D),
            pl.BlockSpec((D, D), lambda j: (0, j)),
            pl.BlockSpec((1, 1, D), lambda j: (j, 0, 0)),
        ],
        [pl.BlockSpec((t, D), lambda j: (0, j)), whole(t, D)],
        [shape((t, 3 * D), BF), shape((t, D), BF)],
        flops=6 * t * D * D,
    )(x, gain, shift, w_qkv, bias)


def bands(t):
    return [(q, max(0, q - QB), min(q + QB, 2 * QB)) for q in range(0, t, QB)]


def head_of(a, x):
    lane = lax.broadcasted_iota(jnp.int32, (1, PAIR), 1)
    return jnp.where((lane < HEAD) == (a == 0), x, jnp.zeros_like(x))


def attend_kernel(seg_ref, q_ref, k_ref, v_ref, att_ref, p_ref, bias_ref):
    t = q_ref.shape[0]

    @pl.when(pl.program_id(0) == 0)
    def _():
        hot = (seg_ref[...] == lax.broadcasted_iota(jnp.int32, (8, t), 0)).astype(BF)
        for i, (q0, k0, n) in enumerate(bands(t)):
            same = dot(hot[:, q0 : q0 + QB], hot[:, k0 : k0 + n], TN)
            row = q0 + lax.broadcasted_iota(jnp.int32, (QB, n), 0)
            col = k0 + lax.broadcasted_iota(jnp.int32, (QB, n), 1)
            bias_ref[i, :, :n] = jnp.where((same > 0.5) & (col <= row), 0.0, -1e30).astype(F32)

    for i, (q0, k0, n) in enumerate(bands(t)):
        queries, keys, values = q_ref[q0 : q0 + QB], k_ref[k0 : k0 + n], v_ref[k0 : k0 + n]
        total = None
        for a in range(2):
            scores = dot(head_of(a, queries), keys, NT) + bias_ref[i, :, :n]
            e = jnp.exp(scores - jnp.max(scores, axis=-1, keepdims=True))
            probs = (e * (1.0 / jnp.sum(e, axis=-1, keepdims=True))).astype(BF)
            p_ref[a, i, :, :n] = probs
            out = dot(probs, head_of(a, values))
            total = out if total is None else total + out
        att_ref[q0 : q0 + QB] = total.astype(BF)


def pair_block(t, offset=0):
    return pl.BlockSpec((t, PAIR), lambda h: (0, offset * (D // PAIR) + h))


def prob_block(t):
    return pl.BlockSpec((2, t // QB, QB, 2 * QB), lambda h: (h, 0, 0, 0))


def attend(seg, proj):
    t = proj.shape[0]
    return call(
        attend_kernel,
        "attend",
        (HEADS // 2,),
        [whole(1, t), pair_block(t), pair_block(t, 1), pair_block(t, 2)],
        [pair_block(t), prob_block(t)],
        [shape((t, D), BF), shape((HEADS, t // QB, QB, 2 * QB), BF)],
        [pltpu.VMEM((t // QB, QB, 2 * QB), F32)],
        flops=8 * HEADS * t * QB * HEAD,
    )(seg, proj, proj, proj)


def branch_kernel(x_ref, att_ref, w_ref, b_ref, g_ref, s_ref, mid_ref, in_ref):
    mid = x_ref[...].astype(F32) + dot(att_ref[...], w_ref[...]) + b_ref[...]
    mid_ref[...] = mid
    u, _ = unit(mid)
    in_ref[...] = (u * g_ref[...] + s_ref[...]).astype(BF)


def branch(x, att, w_out, b_out, gain, shift):
    t = x.shape[0]
    row = pl.BlockSpec((QB, D), lambda i: (i, 0))
    return call(
        branch_kernel,
        "branch_norm",
        (t // QB,),
        [row, row, whole(D, D), whole(1, D), whole(1, D), whole(1, D)],
        [row, row],
        [shape((t, D), F32), shape((t, D), BF)],
        flops=2 * t * D * D,
    )(x, att, w_out, b_out, gain, shift)


def gelu_both(v):
    cdf = 0.5 * (1.0 + lax.erf(v * (2.0**-0.5)))
    pdf = jnp.exp(-0.5 * v * v) * (1.0 / math.sqrt(2 * math.pi))
    return v * cdf, cdf + v * pdf


def put_halves(core, own_ref, other_ref, index, value):
    @pl.when(core == 0)
    def _():
        own_ref[index] = value[:, :HALF]
        other_ref[index] = value[:, HALF:]

    @pl.when(core != 0)
    def _():
        own_ref[index] = value[:, HALF:]
        other_ref[index] = value[:, :HALF]


def up_kernel(pos_ref, wt_ref, in_ref, cot_ref, w_ref, b_ref, act_ref, slope_ref, go_ref, own_ref, other_ref, sum_ref):
    @pl.when(pl.program_id(0) == 0)
    def _():
        go = (cot_ref[...].astype(F32) * wt_ref[0, 0]).astype(BF)
        go_ref[...] = go
        sum_ref[...] = column_sum(go.astype(F32))

    for r in rows_of(in_ref):
        act, slope = gelu_both(dot(in_ref[r : r + QB], w_ref[...]) + b_ref[...])
        act_ref[r : r + QB] = act.astype(BF)
        slope_ref[r : r + QB] = slope.astype(BF)
    put_halves(pos_ref[1], own_ref, other_ref, slice(None), dot(act_ref[...], go_ref[...], TN))


def up(pos, weight, in_two, cot, w_up, b_up):
    t = in_two.shape[0]
    cols = pl.BlockSpec((t, D), lambda j, *_: (0, j))
    half = pl.BlockSpec((D, HALF), lambda j, *_: (j, 0))
    return call(
        up_kernel,
        "up_and_down_grad",
        (FF // D,),
        [
            SMEM,
            whole(t, D),
            whole(t, D),
            pl.BlockSpec((D, D), lambda j, *_: (0, j)),
            pl.BlockSpec((1, D), lambda j, *_: (0, j)),
        ],
        [cols, cols, whole(t, D), half, half, whole(1, D)],
        [shape((t, FF), BF)] * 2
        + [shape((t, D), BF)]
        + [shape((FF, HALF), F32)] * 2
        + [shape((1, D), F32)],
        prefetch=1,
        flops=4 * t * D * FF,
    )(pos, weight, in_two, cot, w_up, b_up)


def hidden_kernel(pos_ref, go_ref, in_ref, slope_ref, w_ref, gp_ref, own_ref, other_ref, sum_ref):
    for r in rows_of(go_ref):
        grad = dot(go_ref[r : r + QB], w_ref[...], NT)
        gp_ref[r : r + QB] = (grad * slope_ref[r : r + QB].astype(F32)).astype(BF)
    sum_ref[...] = column_sum(gp_ref[...].astype(F32))
    put_halves(pos_ref[1], own_ref, other_ref, 0, dot(in_ref[...], gp_ref[...], TN))


def block_half():
    return pl.BlockSpec((1, D, HALF), lambda j, *_: (j, 0, 0))


def hidden(pos, go, in_two, slope, w_down):
    t = in_two.shape[0]
    cols = pl.BlockSpec((t, D), lambda j, *_: (0, j))
    return call(
        hidden_kernel,
        "hidden_grad",
        (FF // D,),
        [whole(t, D), whole(t, D), cols, pl.BlockSpec((D, D), lambda j, *_: (j, 0))],
        [cols, block_half(), block_half(), pl.BlockSpec((1, D), lambda j, *_: (0, j))],
        [shape((t, FF), BF)] + [shape((FF // D, D, HALF), F32)] * 2 + [shape((1, FF), F32)],
        prefetch=1,
        flops=4 * t * D * FF,
    )(pos, go, in_two, slope, w_down)


def middle_kernel(go_ref, mid_ref, g_ref, gp_ref, wu_ref, wo_ref, gm_ref, gb_ref, ga_ref, sums_ref, acc):
    j = pl.program_id(0)
    part = dot(gp_ref[...], wu_ref[...], NT)

    @pl.when(j == 0)
    def _():
        acc[...] = part

    @pl.when(j > 0)
    def _():
        acc[...] += part

    @pl.when(j == pl.num_programs(0) - 1)
    def _():
        gain_sum = shift_sum = bias_sum = jnp.zeros((1, D), F32)
        for r in rows_of(acc):
            e = acc[r : r + QB]
            u, inv = unit(mid_ref[r : r + QB])
            gain_sum += column_sum(e * u)
            shift_sum += column_sum(e)
            gm = go_ref[r : r + QB].astype(F32) + norm_back(e, u, inv, g_ref[...])
            gm_ref[r : r + QB] = gm
            gb = gm.astype(BF)
            gb_ref[r : r + QB] = gb
            bias_sum += column_sum(gb.astype(F32))
            ga_ref[r : r + QB] = dot(gb, wo_ref[...], NT).astype(BF)
        sums_ref[0:1] = gain_sum
        sums_ref[1:2] = shift_sum
        sums_ref[2:3] = bias_sum


def middle_back(go, mid, gain, gp, w_up, w_out, after=()):
    t = go.shape[0]
    return call(
        middle_kernel,
        "norm_two_back",
        (FF // D,),
        [
            whole(t, D),
            whole(t, D),
            whole(1, D),
            pl.BlockSpec((t, D), lambda j: (0, j)),
            pl.BlockSpec((D, D), lambda j: (0, j)),
            whole(D, D),
        ],
        [whole(t, D), whole(t, D), whole(t, D), whole(3, D)],
        [shape((t, D), F32), shape((t, D), BF), shape((t, D), BF), shape((3, D), F32)],
        [pltpu.VMEM((t, D), F32)],
        flops=2 * t * D * (FF + D),
        after=len(after),
    )(go, mid, gain, gp, w_up, w_out, *after)


def attend_back_kernel(q_ref, k_ref, v_ref, ga_ref, p_ref, dq_ref, dk_ref, dv_ref, dk_kept, dv_kept):
    t = q_ref.shape[0]
    for i, (q0, k0, n) in enumerate(bands(t)):
        queries, grads = q_ref[q0 : q0 + QB], ga_ref[q0 : q0 + QB]
        keys, values = k_ref[k0 : k0 + n], v_ref[k0 : k0 + n]
        dq = dk = dv = 0.0
        for a in range(2):
            probs = p_ref[a, i, :, :n]
            wide = probs.astype(F32)
            own = head_of(a, grads)
            prod = wide * dot(own, values, NT)
            ds = (prod - wide * jnp.sum(prod, axis=-1, keepdims=True)).astype(BF)
            dq = dq + dot(ds, head_of(a, keys))
            dk = dk + dot(ds, head_of(a, queries), TN)
            dv = dv + dot(probs, own, TN)
        dq_ref[q0 : q0 + QB] = dq.astype(BF) * jnp.asarray(HEAD**-0.5, BF)
        if i:
            dk_ref[k0 : k0 + QB] = (dk_kept[...] + dk[:QB]).astype(BF)
            dv_ref[k0 : k0 + QB] = (dv_kept[...] + dv[:QB]).astype(BF)
        dk_kept[...] = dk[n - QB :]
        dv_kept[...] = dv[n - QB :]
    dk_ref[t - QB :] = dk_kept[...].astype(BF)
    dv_ref[t - QB :] = dv_kept[...].astype(BF)


def attend_back(proj, ga, probs, after=()):
    t = proj.shape[0]
    return call(
        attend_back_kernel,
        "attend_back",
        (HEADS // 2,),
        [pair_block(t), pair_block(t, 1), pair_block(t, 2), pair_block(t), prob_block(t)],
        [pair_block(t)] * 3,
        [shape((t, D), BF)] * 3,
        [pltpu.VMEM((QB, PAIR), F32)] * 2,
        flops=20 * HEADS * t * QB * HEAD,
        after=len(after),
    )(proj, proj, proj, ga, probs, *after)


def input_kernel(pos_ref, x_ref, in_ref, att_ref, gm_ref, gb_ref, g_ref, dq_ref, dk_ref, dv_ref, w_ref, own_ref, other_ref, gt_ref, sums_ref, acc):
    j = pl.program_id(0)
    core = pos_ref[1]
    for b, d_ref in enumerate((dq_ref, dk_ref, dv_ref)):

        @pl.when(j == b)
        def _():
            put_halves(core, own_ref, other_ref, 0, dot(in_ref[...], d_ref[...], TN))
            part = dot(d_ref[...], w_ref[...], NT)
            if b == 0:
                acc[...] = part
            else:
                acc[...] += part
            if b != 1:
                sums_ref[b // 2 : b // 2 + 1] = column_sum(d_ref[...].astype(F32))

    @pl.when(j == 3)
    def _():
        put_halves(core, own_ref, other_ref, 0, dot(att_ref[...], gb_ref[...], TN))
        gain_sum = shift_sum = jnp.zeros((1, D), F32)
        for r in rows_of(acc):
            e = acc[r : r + QB]
            u, inv = unit(x_ref[r : r + QB].astype(F32))
            gain_sum += column_sum(e * u)
            shift_sum += column_sum(e)
            gt_ref[r : r + QB] = (gm_ref[r : r + QB] + norm_back(e, u, inv, g_ref[...])).astype(BF)
        sums_ref[2:3] = gain_sum
        sums_ref[3:4] = shift_sum


def input_back(pos, x, in_one, att, gm, gb, gain, dq, dk, dv, w_qkv, after=()):
    t = x.shape[0]
    full = whole(t, D)
    return call(
        input_kernel,
        "qkv_back",
        (4,),
        [full] * 5
        + [whole(1, D)]
        + [full] * 3
        + [pl.BlockSpec((D, D), lambda j, *_: (0, jnp.minimum(j, 2)))],
        [block_half(), block_half(), full, whole(4, D)],
        [shape((4, D, HALF), F32)] * 2 + [shape((t, D), BF), shape((4, D), F32)],
        [pltpu.VMEM((t, D), F32)],
        prefetch=1,
        flops=14 * t * D * D,
        after=len(after),
    )(pos, x, in_one, att, gm, gb, gain, dq, dk, dv, w_qkv, *after)


def mix_kernel(mid_ref, act_ref, w_ref, b_ref, out_ref):
    out_ref[...] = (mid_ref[...] + dot(act_ref[...], w_ref[...]) + b_ref[...]).astype(BF)


def mix(mid, act, w_down, b_down, after=()):
    t = mid.shape[0]
    row = pl.BlockSpec((QB, D), lambda i: (i, 0))
    return call(
        mix_kernel,
        "mix",
        (t // QB,),
        [row, pl.BlockSpec((QB, FF), lambda i: (i, 0)), whole(FF, D), whole(1, D)],
        row,
        shape((t, D), BF),
        flops=2 * t * D * FF,
        after=len(after),
    )(mid, act, w_down, b_down, *after)


def swap_with(x, n_dp, masks):
    pairs = []
    for dp in range(n_dp):
        for core in range(2):
            mask = masks[core]
            target = (dp ^ mask) * 2 + core if mask else dp * 2 + 1 - core
            pairs.append((dp * 2 + core, target))
    return lax.ppermute(x, AXES, pairs)


class Halving:
    def __init__(self, pos, n_dp, orders, layout, first, size):
        self.pos, self.n_dp, self.orders = pos, n_dp, orders
        self.layout, self.first, self.size = layout, first, size
        self.steps = len(orders[0])
        self.done = 0
        self.held = []

    def begin(self, own, received):
        self.held = [own, received]

    def bit(self, pos, j):
        a, b = self.orders[0][j], self.orders[1][j]
        return a if a == b else jnp.where(pos[1] == 0, a, b)

    def block(self, which, step):
        def values(i, pos):
            out = []
            for j in range(self.steps):
                mine = (pos[0] >> self.bit(pos, j)) & 1
                if j < step - 1:
                    out.append(mine)
                elif j == step - 1:
                    out.append(1 - mine)
                else:
                    out.append((i >> (j - step)) & 1)
            return out

        def natural(i, pos):
            return sum(v << self.bit(pos, j) for j, v in enumerate(values(i, pos)))

        def later(i, pos):
            skip = which - 1
            return sum(v << (j - skip) for j, v in enumerate(values(i, pos)) if j >= skip)

        return natural if which < 2 else later

    def specs(self, step):
        specs, args = [], []
        for which, array in enumerate(self.held):
            index = self.block(which, step)
            if which >= 2:
                block = (None,) + array.shape[1:]
                rest = (0,) * (array.ndim - 1)
                spec = pl.BlockSpec(block, lambda i, pos, f=index, r=rest: (f(i, pos),) + r)
            elif self.layout == "rows":
                block = (None, self.size) + array.shape[2:]
                at = self.first // self.size
                spec = pl.BlockSpec(block, lambda i, pos, f=index, a=at: (f(i, pos), a, 0, 0))
            else:
                block = (self.size, None) + array.shape[2:]
                at = self.first // self.size
                spec = pl.BlockSpec(block, lambda i, pos, f=index, a=at: (a, f(i, pos), 0, 0))
            specs.append(spec)
            args.append(array)
        return specs, args

    def part(self):
        return (self.size,) + self.held[0].shape[2:]

    def sums(self, step, after=()):
        specs, args = self.specs(step)
        part = self.part()
        count = self.n_dp >> min(step, self.steps)

        def kernel(pos_ref, *refs):
            total = refs[0][...]
            for ref in refs[1:-1]:
                total = total + ref[...]
            refs[-1][...] = total

        return call(
            kernel,
            "halve_%d" % step,
            (count,),
            specs,
            pl.BlockSpec((None,) + part, lambda i, pos: (i,) + (0,) * len(part)),
            shape((count,) + part, F32),
            prefetch=1,
            after=len(after),
        )(self.pos, *args, *after)

    def step(self, after=()):
        self.done += 1
        sent = self.sums(self.done, after)
        masks = tuple(1 << order[self.done - 1] for order in self.orders)
        self.held.append(swap_with(sent, self.n_dp, masks))
        return sent

    def finish(self, after=()):
        return self.sums(self.steps + 1, after)[0]


def gather_task_counts(labels, n_dp, window):
    hits = (labels[:, None] == jnp.arange(NTASK, dtype=jnp.int32)[None, :]).astype(jnp.int32)
    counts = jnp.sum(hits, axis=0) * (2 * window)
    bit = 1
    while bit < n_dp:
        masks = [bit] if 2 * bit >= n_dp else [bit, 2 * bit, 3 * bit]
        counts = counts + sum(swap_with(counts, n_dp, (m, m)) for m in masks)
        bit *= 4
    return hits, counts


def per_device(tokens, segments, labels, cotangent, w_qkv, b_query, b_value, w_out, b_out, gamma_one, beta_one, gamma_two, beta_two, w_up, b_up, w_down, b_down, *, n_dp):
    windows, window, width = tokens.shape
    core = lax.axis_index("group")
    dp = lax.axis_index("dp")
    pos = jnp.stack([dp, core]).astype(jnp.int32)
    x = tokens.reshape(window, width)
    cot = cotangent.reshape(window, width)
    flat = lambda v: v.reshape(1, -1)

    hits, counts = gather_task_counts(labels, n_dp, window)
    task_weight = jnp.sum(counts).astype(F32) / (NTASK * counts.astype(F32))
    weight = jnp.sum(jnp.where(hits > 0, task_weight[None, :], 0.0), axis=1).reshape(1, 1)

    bias = jnp.stack([b_query, jnp.zeros_like(b_query), b_value]).reshape(3, 1, D)
    proj, in_one = project(x, flat(gamma_one), flat(beta_one), w_qkv, bias)
    att, probs = attend(segments, proj)
    mid, in_two = branch(x, att, w_out, flat(b_out), flat(gamma_two), flat(beta_two))

    steps = n_dp.bit_length() - 1
    plain = list(range(steps))
    swapped = [1, 0] + plain[2:]
    wide = (plain, swapped)
    late = (plain[2:] + [0, 1], plain[2:] + [1, 0])
    rows = D // n_dp

    def other_core(value):
        return swap_with(value, n_dp, (0, 0))

    act, slope, go, own, other, sum_down = up(pos, weight, in_two, cot, w_up, flat(b_up))
    own = own.reshape(n_dp, 4, rows, HALF)
    received = other_core(other.reshape(n_dp, 4, rows, HALF))
    down = [Halving(pos, n_dp, wide, "rows", 0, 3), Halving(pos, n_dp, late, "rows", 3, 1)]
    for h in down:
        h.begin(own, received)
    gp, own, other, sum_up = hidden(pos, go, in_two, slope, w_down)

    def in_blocks(v):
        return v.reshape(4, n_dp, rows, HALF)

    def parts(own, other):
        received = other_core(in_blocks(other))
        out = [Halving(pos, n_dp, wide, "blocks", 0, 3), Halving(pos, n_dp, late, "blocks", 3, 1)]
        for h in out:
            h.begin(in_blocks(own), received)
        return out

    ups = parts(own, other)
    gm, gb, ga, sums_mid = middle_back(go, mid, flat(gamma_two), gp, w_up, w_out)
    dq, dk, dv = attend_back(proj, ga, probs)
    own, other, grad_tokens, sums_in = input_back(pos, x, in_one, att, gm, gb, flat(gamma_one), dq, dk, dv, w_qkv)
    ins = parts(own, other)
    mixed = mix(mid, act, w_down, flat(b_down))

    vectors = jnp.concatenate(
        [
            sums_in.reshape(4, n_dp, rows),
            sums_mid.reshape(3, n_dp, rows),
            sum_down.reshape(1, n_dp, rows),
            sum_up.reshape(n_dp, 4, rows).transpose(1, 0, 2),
        ]
    )
    vectors = vectors + other_core(vectors)
    for b in plain:
        vectors = vectors + swap_with(vectors, n_dp, (1 << b, 1 << b))
    vectors = lax.dynamic_index_in_dim(vectors, dp, 1, keepdims=False)

    for h in down + ups + ins:
        for _ in range(steps):
            h.step()

    def share(chain):
        mine = jnp.concatenate([h.finish() for h in chain])
        theirs = other_core(mine)
        first = jnp.where(core == 0, mine, theirs)
        second = jnp.where(core == 0, theirs, mine)
        return jnp.concatenate([first, second], axis=-1)

    grad_down = share(down)
    grad_up = share(ups)
    grad_in = share(ins)
    side = lambda blocks: jnp.concatenate(list(blocks), axis=1)
    return (
        mixed.reshape(tokens.shape),
        grad_tokens.reshape(tokens.shape),
        side(grad_in[:3]),
        vectors[0],
        vectors[1],
        grad_in[3],
        vectors[6],
        vectors[2],
        vectors[3],
        vectors[4],
        vectors[5],
        side(grad_up),
        vectors[8:].reshape(-1),
        grad_down.reshape(FF // n_dp, D),
        vectors[7],
        counts,
    )


def solution(mesh):
    split = P(("dp", "group"), None, None)
    return jax.shard_map(
        functools.partial(per_device, n_dp=mesh.shape["dp"]),
        mesh=mesh,
        in_specs=(split, P(("dp", "group"), None), P(("dp", "group")), split) + (P(),) * 13,
        out_specs=(split, split, P("dp", None), P("dp"), P("dp"), P("dp", None))
        + (P("dp"),) * 5
        + (P("dp", None), P("dp"), P("dp", None), P("dp"), P()),
        check_vma=False,
    )
```

```python
import functools
import math

import jax
import jax.numpy as jnp
from jax import lax
from jax.experimental import pallas as pl
from jax.experimental.pallas import tpu as pltpu
from jax.sharding import PartitionSpec as P

F32 = jnp.float32
BF = jnp.bfloat16
D = 768
HEADS = 12
HEAD = 64
PAIR = 2 * HEAD
FF = 3072
NTASK = 3
VECTORS = 16
QB = 256
HALF = D // 2
AXES = ("dp", "group")
NN = (((1,), (0,)), ((), ()))
NT = (((1,), (1,)), ((), ()))
TN = (((0,), (0,)), ((), ()))
VMEM_LIMIT = 63 * 2**20
SCALE = 1
FLOPS = 1e11


def dot(a, b, dims=NN):
    return lax.dot_general(a, b, dims, preferred_element_type=F32)


def call(kernel, name, grid, in_specs, out_specs, out_shape, scratch=(), prefetch=0, us=3, after=0):
    in_specs = list(in_specs) + [pl.BlockSpec(memory_space=pl.ANY)] * after
    body = kernel
    if after:
        start = prefetch + len(in_specs) - after

        def body(*refs):
            kernel(*refs[:start], *refs[start + after :])

    return pl.pallas_call(
        body,
        grid_spec=pltpu.PrefetchScalarGridSpec(
            num_scalar_prefetch=prefetch,
            grid=grid,
            in_specs=in_specs,
            out_specs=out_specs,
            scratch_shapes=list(scratch),
        ),
        out_shape=out_shape,
        compiler_params=pltpu.CompilerParams(vmem_limit_bytes=VMEM_LIMIT),
        cost_estimate=pl.CostEstimate(flops=int(us * FLOPS), bytes_accessed=int(us * SCALE), transcendentals=0),
        name=name,
    )


def shape(dims, dtype):
    return jax.ShapeDtypeStruct(dims, dtype)


def whole(*dims):
    return pl.BlockSpec(dims, lambda *_: (0,) * len(dims))


SMEM = pl.BlockSpec(memory_space=pltpu.SMEM)


def unit(x):
    centered = x - jnp.mean(x, axis=-1, keepdims=True)
    inv = lax.rsqrt(jnp.mean(centered * centered, axis=-1, keepdims=True) + 1e-05)
    return centered * inv, inv


def norm_back(e, u, inv, gain):
    scaled = e * gain
    return inv * (
        scaled
        - jnp.mean(scaled, axis=-1, keepdims=True)
        - u * jnp.mean(scaled * u, axis=-1, keepdims=True)
    )


def rows_of(ref):
    return range(0, ref.shape[0], QB)


def column_sum(x):
    return jnp.sum(x, axis=0, keepdims=True)


def project_kernel(x_ref, g_ref, b_ref, w_ref, bq_ref, bv_ref, proj_ref, in_ref):
    j = pl.program_id(0)

    @pl.when(j == 0)
    def _():
        for r in rows_of(x_ref):
            u, _ = unit(x_ref[r : r + QB].astype(F32))
            rows = (u * g_ref[...] + b_ref[...]).astype(BF)
            in_ref[r : r + QB] = rows
            proj_ref[r : r + QB] = ((dot(rows, w_ref[...]) + bq_ref[...]) * (HEAD**-0.5)).astype(BF)

    @pl.when(j != 0)
    def _():
        bias = bv_ref[...] * (j == 2).astype(F32)
        proj_ref[...] = (dot(in_ref[...], w_ref[...]) + bias).astype(BF)


def project(x, gain, shift, w_qkv, b_query, b_value):
    t = x.shape[0]
    return call(
        project_kernel,
        "norm_project",
        (3,),
        [whole(t, D), whole(D), whole(D), pl.BlockSpec((D, D), lambda j: (0, j)), whole(D), whole(D)],
        [pl.BlockSpec((t, D), lambda j: (0, j)), whole(t, D)],
        [shape((t, 3 * D), BF), shape((t, D), BF)],
        us=8,
    )(x, gain, shift, w_qkv, b_query, b_value)


def bands(t):
    return [(q, max(0, q - QB), min(q + QB, 2 * QB)) for q in range(0, t, QB)]


def head_of(a, x):
    lane = lax.broadcasted_iota(jnp.int32, (1, PAIR), 1)
    return jnp.where((lane < HEAD) == (a == 0), x, jnp.zeros_like(x))


def attend_kernel(seg_ref, q_ref, k_ref, v_ref, att_ref, p_ref, bias_ref):
    t = q_ref.shape[0]

    @pl.when(pl.program_id(0) == 0)
    def _():
        hot = (seg_ref[...] == lax.broadcasted_iota(jnp.int32, (8, t), 0)).astype(BF)
        for i, (q0, k0, n) in enumerate(bands(t)):
            same = dot(hot[:, q0 : q0 + QB], hot[:, k0 : k0 + n], TN)
            row = q0 + lax.broadcasted_iota(jnp.int32, (QB, n), 0)
            col = k0 + lax.broadcasted_iota(jnp.int32, (QB, n), 1)
            bias_ref[i, :, :n] = jnp.where((same > 0.5) & (col <= row), 0.0, -1e30).astype(F32)

    for i, (q0, k0, n) in enumerate(bands(t)):
        queries, keys, values = q_ref[q0 : q0 + QB], k_ref[k0 : k0 + n], v_ref[k0 : k0 + n]
        total = None
        for a in range(2):
            scores = dot(head_of(a, queries), keys, NT) + bias_ref[i, :, :n]
            e = jnp.exp(scores - jnp.max(scores, axis=-1, keepdims=True))
            probs = (e * (1.0 / jnp.sum(e, axis=-1, keepdims=True))).astype(BF)
            p_ref[a, i, :, :n] = probs
            out = dot(probs, head_of(a, values))
            total = out if total is None else total + out
        att_ref[q0 : q0 + QB] = total.astype(BF)


def pair_block(t, offset=0):
    return pl.BlockSpec((t, PAIR), lambda h: (0, offset * (D // PAIR) + h))


def prob_block(t):
    return pl.BlockSpec((2, t // QB, QB, 2 * QB), lambda h: (h, 0, 0, 0))


def attend(seg, proj, after=()):
    t = proj.shape[0]
    return call(
        attend_kernel,
        "attend",
        (HEADS // 2,),
        [whole(1, t), pair_block(t), pair_block(t, 1), pair_block(t, 2)],
        [pair_block(t), prob_block(t)],
        [shape((t, D), BF), shape((HEADS, t // QB, QB, 2 * QB), BF)],
        [pltpu.VMEM((t // QB, QB, 2 * QB), F32)],
        us=18,
        after=len(after),
    )(seg, proj, proj, proj, *after)


def branch_kernel(x_ref, att_ref, w_ref, b_ref, g_ref, s_ref, mid_ref, in_ref):
    mid = x_ref[...].astype(F32) + dot(att_ref[...], w_ref[...]) + b_ref[...]
    mid_ref[...] = mid
    u, _ = unit(mid)
    in_ref[...] = (u * g_ref[...] + s_ref[...]).astype(BF)


def branch(x, att, w_out, b_out, gain, shift):
    t = x.shape[0]
    row = pl.BlockSpec((QB, D), lambda i: (i, 0))
    return call(
        branch_kernel,
        "branch_norm",
        (t // QB,),
        [row, row, whole(D, D), whole(D), whole(D), whole(D)],
        [row, row],
        [shape((t, D), F32), shape((t, D), BF)],
                us=6,
    )(x, att, w_out, b_out, gain, shift)


def gelu_both(v):
    cdf = 0.5 * (1.0 + lax.erf(v * (2.0**-0.5)))
    pdf = jnp.exp(-0.5 * v * v) * (1.0 / math.sqrt(2 * math.pi))
    return v * cdf, cdf + v * pdf


def own_first(core, x):
    return jnp.where(core == 0, x, jnp.concatenate([x[:, HALF:], x[:, :HALF]], axis=1))


def up_kernel(pos_ref, counts_ref, label_ref, in_ref, cot_ref, w_ref, b_ref, act_ref, slope_ref, go_ref, own_ref, other_ref, sum_ref, turned):
    @pl.when(pl.program_id(0) == 0)
    def _():
        total = (counts_ref[0] + counts_ref[1] + counts_ref[2]).astype(F32)
        here = (NTASK * counts_ref[label_ref[0]]).astype(F32)
        weight = jnp.full((1, D), total, F32) / jnp.full((1, D), here, F32)
        go = (cot_ref[...].astype(F32) * weight).astype(BF)
        go_ref[...] = go
        turned[...] = own_first(pos_ref[1], go)
        sum_ref[...] = column_sum(go.astype(F32))

    bias = b_ref[pl.ds(pl.multiple_of(pl.program_id(0) * D, D), D)]
    for r in rows_of(in_ref):
        act, slope = gelu_both(dot(in_ref[r : r + QB], w_ref[...]) + bias)
        act_ref[r : r + QB] = act.astype(BF)
        slope_ref[r : r + QB] = slope.astype(BF)
    grad = dot(act_ref[...], turned[...], TN)
    own_ref[...] = grad[:, :HALF]
    other_ref[...] = grad[:, HALF:]


def up(pos, counts, labels, in_two, cot, w_up, b_up):
    t = in_two.shape[0]
    cols = pl.BlockSpec((t, D), lambda j, *_: (0, j))
    half = pl.BlockSpec((D, HALF), lambda j, *_: (j, 0))
    return call(
        up_kernel,
        "up_and_down_grad",
        (FF // D,),
        [
            whole(t, D),
            whole(t, D),
            pl.BlockSpec((D, D), lambda j, *_: (0, j)),
            whole(FF),
        ],
        [cols, cols, whole(t, D), half, half, whole(1, D)],
        [shape((t, FF), BF)] * 2
        + [shape((t, D), BF)]
        + [shape((FF, HALF), F32)] * 2
        + [shape((1, D), F32)],
        [pltpu.VMEM((t, D), BF)],
        prefetch=3,
        us=20,
    )(pos, counts, labels, in_two, cot, w_up, b_up)


def hidden_kernel(pos_ref, go_ref, in_ref, slope_ref, w_ref, gp_ref, own_ref, other_ref, sum_ref):
    for r in rows_of(go_ref):
        grad = dot(go_ref[r : r + QB], w_ref[...], NT)
        gp_ref[r : r + QB] = (grad * slope_ref[r : r + QB].astype(F32)).astype(BF)
    sum_ref[0] = column_sum(gp_ref[...].astype(F32))
    grad = dot(in_ref[...], own_first(pos_ref[1], gp_ref[...]), TN)
    own_ref[0] = grad[:, :HALF]
    other_ref[0] = grad[:, HALF:]


def block_half():
    return pl.BlockSpec((1, D, HALF), lambda j, *_: (j, 0, 0))


def hidden(pos, go, in_two, slope, w_down):
    t = in_two.shape[0]
    cols = pl.BlockSpec((t, D), lambda j, *_: (0, j))
    return call(
        hidden_kernel,
        "hidden_grad",
        (FF // D,),
        [whole(t, D), whole(t, D), cols, pl.BlockSpec((D, D), lambda j, *_: (j, 0))],
        [cols, block_half(), block_half(), pl.BlockSpec((1, 1, D), lambda j, *_: (j, 0, 0))],
        [shape((t, FF), BF)] + [shape((FF // D, D, HALF), F32)] * 2 + [shape((FF // D, 1, D), F32)],
        prefetch=1,
        us=17,
    )(pos, go, in_two, slope, w_down)


def middle_kernel(go_ref, mid_ref, g_ref, gp_ref, wu_ref, wo_ref, gm_ref, gb_ref, ga_ref, sums_ref, acc):
    j = pl.program_id(0)
    blocks = FF // D

    @pl.when(j == 0)
    def _():
        acc[...] = dot(gp_ref[...], wu_ref[...], NT)

    @pl.when((j > 0) & (j < blocks))
    def _():
        acc[...] += dot(gp_ref[...], wu_ref[...], NT)

    @pl.when(j >= blocks)
    def _():
        rows = gm_ref.shape[0]
        e = acc[pl.ds(pl.multiple_of((j - blocks) * rows, rows), rows)]
        u, inv = unit(mid_ref[...])
        gm = go_ref[...].astype(F32) + norm_back(e, u, inv, g_ref[...])
        gm_ref[...] = gm
        gb = gm.astype(BF)
        gb_ref[...] = gb
        ga_ref[...] = dot(gb, wo_ref[...], NT).astype(BF)
        add_sums(sums_ref, j == blocks, [column_sum(e * u), column_sum(e), column_sum(gb.astype(F32))])


def add_sums(ref, first, sums):
    for n, value in enumerate(sums):

        @pl.when(first)
        def _():
            ref[n : n + 1] = value

        @pl.when(jnp.logical_not(first))
        def _():
            ref[n : n + 1] += value


def middle_back(go, mid, gain, gp, w_up, w_out, after=()):
    t = go.shape[0]
    blocks, rows = FF // D, QB
    row = pl.BlockSpec((rows, D), lambda j: (jnp.maximum(j - blocks, 0), 0))
    return call(
        middle_kernel,
        "norm_two_back",
        (blocks + t // rows,),
        [
            row,
            row,
            whole(D),
            pl.BlockSpec((t, D), lambda j: (0, jnp.minimum(j, blocks - 1))),
            pl.BlockSpec((D, D), lambda j: (0, jnp.minimum(j, blocks - 1))),
            whole(D, D),
        ],
        [row, row, row, whole(3, D)],
        [shape((t, D), F32), shape((t, D), BF), shape((t, D), BF), shape((3, D), F32)],
        [pltpu.VMEM((t, D), F32)],
        us=16,
        after=len(after),
    )(go, mid, gain, gp, w_up, w_out, *after)


def attend_back_kernel(q_ref, k_ref, v_ref, ga_ref, p_ref, d_ref, dk_kept, dv_kept):
    t = q_ref.shape[0]
    for i, (q0, k0, n) in enumerate(bands(t)):
        queries, grads = q_ref[q0 : q0 + QB], ga_ref[q0 : q0 + QB]
        keys, values = k_ref[k0 : k0 + n], v_ref[k0 : k0 + n]
        dq = dk = dv = 0.0
        for a in range(2):
            probs = p_ref[a, i, :, :n]
            wide = probs.astype(F32)
            own = head_of(a, grads)
            prod = wide * dot(own, values, NT)
            ds = (prod - wide * jnp.sum(prod, axis=-1, keepdims=True)).astype(BF)
            dq = dq + dot(ds, head_of(a, keys))
            dk = dk + dot(ds, head_of(a, queries), TN)
            dv = dv + dot(probs, own, TN)
        d_ref[0, q0 : q0 + QB] = dq.astype(BF) * jnp.asarray(HEAD**-0.5, BF)
        if i:
            d_ref[1, k0 : k0 + QB] = (dk_kept[...] + dk[:QB]).astype(BF)
            d_ref[2, k0 : k0 + QB] = (dv_kept[...] + dv[:QB]).astype(BF)
        dk_kept[...] = dk[n - QB :]
        dv_kept[...] = dv[n - QB :]
    d_ref[1, t - QB :] = dk_kept[...].astype(BF)
    d_ref[2, t - QB :] = dv_kept[...].astype(BF)


def attend_back(proj, ga, probs, after=()):
    t = proj.shape[0]
    return call(
        attend_back_kernel,
        "attend_back",
        (HEADS // 2,),
        [pair_block(t), pair_block(t, 1), pair_block(t, 2), pair_block(t), prob_block(t)],
        pl.BlockSpec((3, t, PAIR), lambda h: (0, 0, h)),
        shape((3, t, D), BF),
        [pltpu.VMEM((QB, PAIR), F32)] * 2,
        us=20,
        after=len(after),
    )(proj, proj, proj, ga, probs, *after)


def input_kernel(pos_ref, x_ref, in_ref, att_ref, gm_ref, gb_ref, g_ref, d_ref, w_ref, mid_sums, down_sum, up_sums, own_ref, other_ref, gt_ref, sums_ref, acc):
    j = pl.program_id(0)

    def put(value):
        own_ref[0] = value[:, :HALF]
        other_ref[0] = value[:, HALF:]

    @pl.when(j < 3)
    def _():
        put(dot(in_ref[...], own_first(pos_ref[1], d_ref[0]), TN))

    @pl.when(j == 0)
    def _():
        acc[...] = dot(d_ref[0], w_ref[...], NT)
        sums_ref[0:1] = column_sum(d_ref[0].astype(F32))
        sums_ref[4:7] = mid_sums[...]
        sums_ref[7:8] = down_sum[...]
        for b in range(FF // D):
            sums_ref[8 + b : 9 + b] = up_sums[b]
        sums_ref[8 + FF // D :] = jnp.zeros((VECTORS - 8 - FF // D, D), F32)

    @pl.when((j == 1) | (j == 2))
    def _():
        acc[...] += dot(d_ref[0], w_ref[...], NT)
        sums_ref[1:2] = column_sum(d_ref[0].astype(F32))

    @pl.when(j == 3)
    def _():
        put(dot(att_ref[...], own_first(pos_ref[1], gb_ref[...]), TN))

    @pl.when(j > 3)
    def _():
        rows = gt_ref.shape[0]
        e = acc[pl.ds(pl.multiple_of((j - 4) * rows, rows), rows)]
        u, inv = unit(x_ref[...].astype(F32))
        gt_ref[...] = (gm_ref[...] + norm_back(e, u, inv, g_ref[...])).astype(BF)
        add_sums(sums_ref.at[2:4], j == 4, [column_sum(e * u), column_sum(e)])


def input_back(pos, x, in_one, att, gm, gb, gain, d, w_qkv, mid_sums, down_sum, up_sums, after=()):
    t = x.shape[0]
    full = whole(t, D)
    row = pl.BlockSpec((QB, D), lambda j, *_: (jnp.maximum(j - 4, 0), 0))
    block = pl.BlockSpec((1, D, HALF), lambda j, *_: (jnp.minimum(j, 3), 0, 0))
    return call(
        input_kernel,
        "qkv_back",
        (4 + t // QB,),
        [
            row,
            full,
            full,
            row,
            full,
            whole(D),
            pl.BlockSpec((1, t, D), lambda j, *_: (jnp.minimum(j, 2), 0, 0)),
            pl.BlockSpec((D, D), lambda j, *_: (0, jnp.minimum(j, 2))),
            whole(3, D),
            whole(1, D),
            whole(FF // D, 1, D),
        ],
        [block, block, row, whole(VECTORS, D)],
        [shape((4, D, HALF), F32)] * 2 + [shape((t, D), BF), shape((VECTORS, D), F32)],
        [pltpu.VMEM((t, D), F32)],
        prefetch=1,
        us=24,
        after=len(after),
    )(pos, x, in_one, att, gm, gb, gain, d, w_qkv, mid_sums, down_sum, up_sums, *after)


def mix_kernel(mid_ref, act_ref, w_ref, b_ref, out_ref):
    out_ref[...] = (mid_ref[...] + dot(act_ref[...], w_ref[...]) + b_ref[...]).astype(BF)


def mix(mid, act, w_down, b_down, after=()):
    t = mid.shape[0]
    row = pl.BlockSpec((QB, D), lambda i: (i, 0))
    return call(
        mix_kernel,
        "mix",
        (t // QB,),
        [row, pl.BlockSpec((QB, FF), lambda i: (i, 0)), whole(FF, D), whole(D)],
        row,
        shape((t, D), BF),
        us=10,
        after=len(after),
    )(mid, act, w_down, b_down, *after)


def swap_with(x, n_dp, masks):
    pairs = []
    for dp in range(n_dp):
        for core in range(2):
            mask = masks[core]
            target = (dp ^ mask) * 2 + core if mask else dp * 2 + 1 - core
            pairs.append((dp * 2 + core, target))
    return lax.ppermute(x, AXES, pairs)


class Part:
    def __init__(self, n_dp, orders, first, size, kind, own, received):
        self.n_dp, self.orders, self.size = n_dp, orders, size
        self.steps = len(orders[0])
        self.held = [(own, kind, first), (received, kind, first)]

    def bit(self, core, j):
        a, b = self.orders[0][j], self.orders[1][j]
        return a if a == b else jnp.where(core == 0, a, b)

    def values(self, i, step, dp, core):
        out = []
        for j in range(self.steps):
            mine = (dp >> self.bit(core, j)) & 1
            if j < step - 1:
                out.append(mine)
            elif j == step - 1:
                out.append(1 - mine)
            else:
                out.append((i >> (j - step)) & 1)
        return out

    def source(self, ref, kind, first, i, step, dp, core):
        values = self.values(i, step, dp, core)
        if kind in ("rows", "blocks"):
            at = sum(v << self.bit(core, j) for j, v in enumerate(values))
            span = pl.ds(first, self.size)
            return ref.at[at, span] if kind == "rows" else ref.at[span, at]
        at = sum(v << (j - kind) for j, v in enumerate(values) if j >= kind)
        return ref.at[at, pl.ds(first, self.size)]


class Vectors:
    def __init__(self, total, n_dp):
        self.n_dp, self.total = n_dp, total
        self.masks = [0] + [1 << b for b in range(n_dp.bit_length() - 1)]
        self.swap()

    def swap(self):
        mask = self.masks.pop(0)
        self.received = swap_with(self.total, self.n_dp, (mask, mask))


def tick(pos, name, sends, after=(), vectors=None):
    arrays, jobs, outs, scratch = [], [], [], []

    def operand(array):
        for n, known in enumerate(arrays):
            if known is array:
                return n
        arrays.append(array)
        return len(arrays) - 1

    copies = 0
    for n, (step, parts) in enumerate(sends):
        count = parts[0].n_dp >> min(step, parts[0].steps)
        tail = parts[0].held[0][0].shape[2:]
        offset = 0
        for part in parts:
            refs = [(operand(array), kind, first) for array, kind, first in part.held]
            jobs.append((part, refs, step, count, n, offset, len(scratch), copies))
            scratch.append(pltpu.VMEM((len(refs), count, part.size) + tail, F32))
            copies += count * (len(refs) + 1)
            offset += part.size
        outs.append(shape((count, offset) + tail, F32))
    if vectors is not None:
        pair = (operand(vectors.total), operand(vectors.received))
        outs.append(shape((VECTORS, D), F32))
        scratch.append(pltpu.VMEM((2, VECTORS, D), F32))
        copies += 3

    def kernel(pos_ref, *refs):
        ins, out_refs = refs[: len(arrays)], refs[len(arrays) : len(arrays) + len(outs)]
        held = refs[len(arrays) + len(outs) : -1]
        sems = refs[-1]
        dp, core = pos_ref[0], pos_ref[1]

        def loads(job, i):
            part, sources, step, count, n, offset, buf, base = job
            return [
                pltpu.make_async_copy(
                    part.source(ins[k], kind, first, i, step, dp, core),
                    held[buf].at[m, i],
                    sems.at[base + i * (len(sources) + 1) + m],
                )
                for m, (k, kind, first) in enumerate(sources)
            ]

        def store(job, i):
            part, sources, step, count, n, offset, buf, base = job
            return pltpu.make_async_copy(
                held[buf].at[0, i],
                out_refs[n].at[i, pl.ds(offset, part.size)],
                sems.at[base + i * (len(sources) + 1) + len(sources)],
            )

        def start(job, i):
            for copy in loads(job, i):
                copy.start()

        def add(job, i):
            for copy in loads(job, i):
                copy.wait()
            buf = held[job[6]]
            total = buf[0, i]
            for m in range(1, len(job[1])):
                total = total + buf[m, i]
            buf[0, i] = total
            store(job, i).start()

        def finish(job, i):
            store(job, i).wait()

        def vector_copy(m):
            if m == 2:
                return pltpu.make_async_copy(held[-1].at[0], out_refs[-1], sems.at[copies - 1])
            return pltpu.make_async_copy(ins[pair[m]], held[-1].at[m], sems.at[copies - 3 + m])

        for act in (start, add, finish):
            if vectors is not None:
                if act is start:
                    vector_copy(0).start()
                    vector_copy(1).start()
                elif act is add:
                    vector_copy(0).wait()
                    vector_copy(1).wait()
                    held[-1][0] = held[-1][0] + held[-1][1]
                    vector_copy(2).start()
                else:
                    vector_copy(2).wait()
            for job in jobs:
                if job[3] <= 8:
                    for i in range(job[3]):
                        act(job, i)
                else:
                    pl.loop(0, job[3])(functools.partial(act, job))

    anywhere = pl.BlockSpec(memory_space=pl.ANY)
    return call(
        kernel,
        name,
        (1,),
        [anywhere] * len(arrays),
        [anywhere] * len(outs),
        outs,
        scratch + [pltpu.SemaphoreType.DMA((copies,))],
        prefetch=1,
        after=len(after),
    )(pos, *arrays, *after)


def advance(pos, name, sends, after=(), vectors=None):
    sent = tick(pos, name, sends, after, vectors)
    if vectors is not None:
        vectors.total = sent[-1]
        if vectors.masks:
            vectors.swap()
    for array, (step, parts) in zip(sent, sends):
        masks = tuple(1 << order[step - 1] for order in parts[0].orders)
        received = swap_with(array, parts[0].n_dp, masks)
        offset = 0
        for part in parts:
            part.held.append((received, step, offset))
            offset += part.size
    return sent


def place_kernel(pos_ref, mine_ref, theirs_ref, *refs, places, blocks):
    core = pos_ref[1]
    for b, (n, row, col) in enumerate(places):
        mine, theirs = mine_ref[0, b], theirs_ref[0, b]
        rows = mine.shape[0]
        out = refs[len(refs) - blocks + n]
        out[row : row + rows, col : col + HALF] = jnp.where(core == 0, mine, theirs)
        out[row : row + rows, col + HALF : col + D] = jnp.where(core == 0, theirs, mine)
    if len(refs) > blocks:
        vectors, singles, wide = refs[0], refs[1:9], refs[9]
        rows, per = singles[0].shape[0], wide.shape[0]
        turned = pltpu.roll(vectors[:8], lax.rem(D - pos_ref[0] * rows, D), 1)
        for n, single in enumerate(singles):
            single[...] = turned[n, :rows]
        at = pos_ref[0] * per
        turned = pltpu.roll(vectors[8:], lax.rem(D - lax.rem(at, D), D), 1)
        line = lax.broadcasted_iota(jnp.int32, turned.shape, 0) == at // D
        wide[...] = jnp.sum(jnp.where(line, turned, 0.0), axis=0)[:per]


def place(pos, mine, theirs, places, outs, after=(), vectors=None):
    given, more = [], []
    if vectors is not None:
        rows = D // vectors.n_dp
        given = [vectors.total]
        more = [(rows,)] * 8 + [(rows * FF // D,)]
    return call(
        functools.partial(place_kernel, places=places, blocks=len(outs)),
        "place",
        (1,),
        [whole(*v.shape) for v in [mine, theirs] + given],
        [whole(*dims) for dims in more + outs],
        [shape(dims, F32) for dims in more + outs],
        prefetch=1,
        after=len(after),
    )(pos, mine, theirs, *given, *after)


def count_rounds(labels, n_dp, window):
    hits = (labels[:, None] == jnp.arange(NTASK, dtype=jnp.int32)[None, :]).astype(jnp.int32)
    counts = [jnp.sum(hits, axis=0) * (2 * window)]
    bit = 1
    while bit < n_dp:
        masks = [bit] if 2 * bit >= n_dp else [bit, 2 * bit, 3 * bit]
        counts.append(counts[-1] + sum(swap_with(counts[-1], n_dp, (m, m)) for m in masks))
        bit *= 4
    return counts[1:]


def per_device(tokens, segments, labels, cotangent, w_qkv, b_query, b_value, w_out, b_out, gamma_one, beta_one, gamma_two, beta_two, w_up, b_up, w_down, b_down, *, n_dp):
    windows, window, width = tokens.shape
    pos = jnp.stack([lax.axis_index("dp"), lax.axis_index("group")]).astype(jnp.int32)
    x = tokens.reshape(window, width)
    cot = cotangent.reshape(window, width)
    counts = count_rounds(labels, n_dp, window)

    steps = n_dp.bit_length() - 1
    plain = list(range(steps))
    wide = (plain, [1, 0] + plain[2:])
    late = (plain[2:] + [0, 1], plain[2:] + [1, 0])
    rows = D // n_dp

    def other_core(value):
        return swap_with(value, n_dp, (0, 0))

    def parts(kind, own, other):
        dims = (n_dp, 4, rows, HALF) if kind == "rows" else (4, n_dp, rows, HALF)
        own, received = own.reshape(dims), other_core(other.reshape(dims))
        return Part(n_dp, wide, 0, 3, kind, own, received), Part(n_dp, late, 3, 1, kind, own, received)

    go_on = functools.partial(advance, pos)
    proj, in_one = project(x, gamma_one, beta_one, w_qkv, b_query, b_value)
    att, probs = attend(segments, proj, counts[:1])
    mid, in_two = branch(x, att, w_out, b_out, gamma_two, beta_two)
    act, slope, go, own, other, sum_down = up(pos, counts[-1], labels, in_two, cot, w_up, b_up)
    down, down_late = parts("rows", own, other)
    gp, own, other, sum_up = hidden(pos, go, in_two, slope, w_down)
    ups, ups_late = parts("blocks", own, other)
    sent = go_on("tick_1", [(1, [down]), (1, [down_late])], (gp,))
    gm, gb, ga, sums_mid = middle_back(go, mid, gamma_two, gp, w_up, w_out, sent[:1])
    sent = go_on("tick_2", [(1, [ups]), (1, [ups_late])], (ga,))
    d = attend_back(proj, ga, probs, sent[:1])
    sent = go_on("tick_3", [(2, [down_late, ups_late])], (d,))
    own, other, grad_tokens, vectors = input_back(
        pos, x, in_one, att, gm, gb, gamma_one, d, w_qkv, sums_mid, sum_down, sum_up, sent[:1]
    )
    ins, ins_late = parts("blocks", own, other)
    vectors = Vectors(vectors, n_dp)
    sent = go_on("tick_4", [(2, [down, ups])], (grad_tokens,))
    mixed = mix(mid, act, w_down, b_down, sent[:1])
    sent = go_on("tick_5", [(1, [ins]), (1, [ins_late]), (3, [down_late, ups_late])], (mixed,), vectors)
    sent = go_on("tick_6", [(3, [down, ups])], sent[:1], vectors)
    sent = go_on("tick_7", [(2, [ins_late]), (4, [down_late, ups_late])], sent[:1], vectors)
    sent = go_on("tick_8", [(2, [ins]), (4, [down, ups])], sent[:1], vectors)
    sent = go_on("tick_9", [(3, [ins_late])], sent[:1], vectors)
    early = [down, down_late, ups, ups_late]
    for step in range(5, steps + 1):
        sent = go_on("tick_more", [(step, [down, ups]), (step, [down_late, ups_late])], sent[:1], vectors)
    sent = go_on("tick_10", [(3, [ins]), (4, [ins_late])], sent[:1])
    mine = tick(pos, "own_early", [(steps + 1, early)], sent[:1])[0]
    theirs = other_core(mine)
    sent = go_on("tick_11", [(4, [ins])], (mine,))
    for step in range(5, steps + 1):
        sent = go_on("tick_more", [(step, [ins]), (step, [ins_late])], sent[:1])
    *singles, grad_b_up, grad_down, grad_up = place(
        pos,
        mine,
        theirs,
        [(0, b * rows, 0) for b in range(4)] + [(1, 0, b * D) for b in range(4)],
        [(4 * rows, D), (rows, FF)],
        sent[:1],
        vectors,
    )
    mine = tick(pos, "own_late", [(steps + 1, [ins, ins_late])], (grad_up,))[0]
    grad_qkv, grad_out = place(
        pos, mine, other_core(mine), [(0, 0, b * D) for b in range(3)] + [(1, 0, 0)], [(rows, 3 * D), (rows, D)]
    )
    query, value, gain_one, shift_one, gain_two, shift_two, out, bias_down = singles
    return (
        mixed.reshape(tokens.shape),
        grad_tokens.reshape(tokens.shape),
        grad_qkv,
        query,
        value,
        grad_out,
        out,
        gain_one,
        shift_one,
        gain_two,
        shift_two,
        grad_up,
        grad_b_up,
        grad_down,
        bias_down,
        counts[-1],
    )


def solution(mesh):
    split = P(("dp", "group"), None, None)
    return jax.shard_map(
        functools.partial(per_device, n_dp=mesh.shape["dp"]),
        mesh=mesh,
        in_specs=(split, P(("dp", "group"), None), P(("dp", "group")), split) + (P(),) * 13,
        out_specs=(split, split, P("dp", None), P("dp"), P("dp"), P("dp", None))
        + (P("dp"),) * 5
        + (P("dp", None), P("dp"), P("dp", None), P("dp"), P()),
        check_vma=False,
    )
```

```python
import functools
import math

import jax
import jax.numpy as jnp
from jax import lax
from jax.experimental import pallas as pl
from jax.experimental.pallas import tpu as pltpu
from jax.sharding import PartitionSpec as P

F32 = jnp.float32
BF = jnp.bfloat16
D = 768
HEADS = 12
HEAD = 64
PAIR = 2 * HEAD
LANES = 128
FF = 3072
NTASK = 3
VECTORS = 16
QB = 256
HALF = D // 2
AXES = ("dp", "group")
NN = (((1,), (0,)), ((), ()))
NT = (((1,), (1,)), ((), ()))
TN = (((0,), (0,)), ((), ()))
LATE = (1, 1)
SMALL_FLOPS = 1000000
SMALL_LIMIT = 20 * 2**20
FREE = {'branch_norm': [1, 2], 'up_and_down_grad': [3, 4, 5], 'hidden_grad': [1, 2, 4], 'norm_two_back': [0, 3, 4, 5], 'first_heads_grad': [1, 2], 'last_heads_grad': [1, 2], 'norm_one_back': [3, 4, 5], 'mix': [2]}
OUT = {'attend': [0], 'branch_norm': [1], 'up_and_down_grad': [2], 'hidden_grad': [0], 'attend_back': [0]}
VMEM_LIMIT = 34 * 2**20
SCALE = 1
FLOPS = 4e9


def dot(a, b, dims=NN):
    return lax.dot_general(a, b, dims, preferred_element_type=F32)


def in_hbm(x):
    return pltpu.with_memory_space_constraint(x, pltpu.HBM)


def call(kernel, name, grid, in_specs, out_specs, out_shape, scratch=(), prefetch=0, us=3, after=0, free=()):
    in_specs = list(in_specs) + [pl.BlockSpec(memory_space=pl.ANY)] * after
    body = kernel
    if after:
        start = prefetch + len(in_specs) - after

        def body(*refs):
            kernel(*refs[:start], *refs[start + after :])

    single = not isinstance(out_shape, list)
    made = [(s if n in OUT.get(name, ()) else pltpu.HBM(s.shape, s.dtype)) if isinstance(s, jax.ShapeDtypeStruct) else s for n, s in enumerate([out_shape] if single else out_shape)]
    run = pl.pallas_call(
        body,
        grid_spec=pltpu.PrefetchScalarGridSpec(
            num_scalar_prefetch=prefetch,
            grid=grid,
            in_specs=in_specs,
            out_specs=[out_specs] if single else out_specs,
            scratch_shapes=list(scratch),
        ),
        out_shape=made,
        compiler_params=pltpu.CompilerParams(vmem_limit_bytes=VMEM_LIMIT),
        cost_estimate=pl.CostEstimate(flops=int(us * FLOPS), bytes_accessed=int(us * SCALE), transcendentals=0),
        name=name,
    )

    def apply(*args):
        last = len(args) - after
        table = FREE.get(name, free)
        args = [x if n < prefetch or n >= last or n in table else in_hbm(x) for n, x in enumerate(args)]
        out = run(*args)
        return out[0] if single else out

    return apply


def shape(dims, dtype):
    return jax.ShapeDtypeStruct(dims, dtype)


def whole(*dims):
    return pl.BlockSpec(dims, lambda *_: (0,) * len(dims))


SMEM = pl.BlockSpec(memory_space=pltpu.SMEM)


def unit(x):
    centered = x - jnp.mean(x, axis=-1, keepdims=True)
    inv = lax.rsqrt(jnp.mean(centered * centered, axis=-1, keepdims=True) + 1e-05)
    return centered * inv, inv


def norm_back(e, u, inv, gain):
    scaled = e * gain
    return inv * (
        scaled
        - jnp.mean(scaled, axis=-1, keepdims=True)
        - u * jnp.mean(scaled * u, axis=-1, keepdims=True)
    )


def rows_of(ref):
    return range(0, ref.shape[0], QB)


def column_sum(x):
    return jnp.sum(x, axis=0, keepdims=True)


def project_kernel(x_ref, g_ref, b_ref, w_ref, bq_ref, bv_ref, proj_ref, in_ref):
    j = pl.program_id(0)

    @pl.when(j == 0)
    def _():
        for r in rows_of(x_ref):
            u, _ = unit(x_ref[r : r + QB].astype(F32))
            rows = (u * g_ref[...] + b_ref[...]).astype(BF)
            in_ref[r : r + QB] = rows
            proj_ref[r : r + QB] = ((dot(rows, w_ref[...]) + bq_ref[...]) * (HEAD**-0.5)).astype(BF)

    @pl.when(j != 0)
    def _():
        bias = bv_ref[...] * (j == 2).astype(F32)
        proj_ref[...] = (dot(in_ref[...], w_ref[...]) + bias).astype(BF)


def project(x, gain, shift, w_qkv, b_query, b_value):
    t = x.shape[0]
    return call(
        project_kernel,
        "norm_project",
        (3,),
        [whole(t, D), whole(D), whole(D), pl.BlockSpec((D, D), lambda j: (0, j)), whole(D), whole(D)],
        [pl.BlockSpec((t, D), lambda j: (0, j)), whole(t, D)],
        [shape((t, 3 * D), BF), shape((t, D), BF)],
        us=8,
    )(x, gain, shift, w_qkv, b_query, b_value)


def bands(t):
    return [(q, max(0, q - QB), min(q + QB, 2 * QB)) for q in range(0, t, QB)]


def head_of(a, x):
    lane = lax.broadcasted_iota(jnp.int32, (1, PAIR), 1)
    return jnp.where((lane < HEAD) == (a == 0), x, jnp.zeros_like(x))


def attend_kernel(seg_ref, q_ref, k_ref, v_ref, att_ref, p_ref, bias_ref):
    t = q_ref.shape[0]

    @pl.when(pl.program_id(0) == 0)
    def _():
        hot = (seg_ref[...] == lax.broadcasted_iota(jnp.int32, (8, t), 0)).astype(BF)
        for i, (q0, k0, n) in enumerate(bands(t)):
            same = dot(hot[:, q0 : q0 + QB], hot[:, k0 : k0 + n], TN)
            row = q0 + lax.broadcasted_iota(jnp.int32, (QB, n), 0)
            col = k0 + lax.broadcasted_iota(jnp.int32, (QB, n), 1)
            bias_ref[i, :, :n] = jnp.where((same > 0.5) & (col <= row), 0.0, -1e30).astype(F32)

    for i, (q0, k0, n) in enumerate(bands(t)):
        queries, keys, values = q_ref[q0 : q0 + QB], k_ref[k0 : k0 + n], v_ref[k0 : k0 + n]
        total = None
        for a in range(2):
            scores = dot(head_of(a, queries), keys, NT) + bias_ref[i, :, :n]
            e = jnp.exp(scores - jnp.max(scores, axis=-1, keepdims=True))
            probs = (e * (1.0 / jnp.sum(e, axis=-1, keepdims=True))).astype(BF)
            p_ref[a, i, :, :n] = probs
            out = dot(probs, head_of(a, values))
            total = out if total is None else total + out
        att_ref[q0 : q0 + QB] = total.astype(BF)


def pair_block(t, offset=0):
    return pl.BlockSpec((t, PAIR), lambda h: (0, offset * (D // PAIR) + h))


def prob_block(t):
    return pl.BlockSpec((2, t // QB, QB, 2 * QB), lambda h: (h, 0, 0, 0))


def attend(seg, proj, after=()):
    t = proj.shape[0]
    return call(
        attend_kernel,
        "attend",
        (HEADS // 2,),
        [whole(1, t), pair_block(t), pair_block(t, 1), pair_block(t, 2)],
        [pair_block(t), prob_block(t)],
        [shape((t, D), BF), shape((HEADS, t // QB, QB, 2 * QB), BF)],
        [pltpu.VMEM((t // QB, QB, 2 * QB), F32)],
        us=18,
        after=len(after),
    )(seg, proj, proj, proj, *after)


def branch_kernel(x_ref, att_ref, w_ref, b_ref, g_ref, s_ref, mid_ref, in_ref):
    mid = x_ref[...].astype(F32) + dot(att_ref[...], w_ref[...]) + b_ref[...]
    mid_ref[...] = mid
    u, _ = unit(mid)
    in_ref[...] = (u * g_ref[...] + s_ref[...]).astype(BF)


def branch(x, att, w_out, b_out, gain, shift):
    t = x.shape[0]
    row = pl.BlockSpec((QB, D), lambda i: (i, 0))
    return call(
        branch_kernel,
        "branch_norm",
        (t // QB,),
        [row, row, whole(D, D), whole(D), whole(D), whole(D)],
        [row, row],
        [shape((t, D), F32), shape((t, D), BF)],
                us=6,
    )(x, att, w_out, b_out, gain, shift)


def gelu_both(v):
    cdf = 0.5 * (1.0 + lax.erf(v * (2.0**-0.5)))
    pdf = jnp.exp(-0.5 * v * v) * (1.0 / math.sqrt(2 * math.pi))
    return v * cdf, cdf + v * pdf


def own_first(core, x):
    half = x.shape[1] // 2
    return jnp.where(core == 0, x, jnp.concatenate([x[:, half:], x[:, :half]], axis=1))


def up_kernel(pos_ref, counts_ref, label_ref, in_ref, cot_ref, w_ref, b_ref, act_ref, slope_ref, go_ref, own_ref, other_ref, sum_ref, turned):
    @pl.when(pl.program_id(0) == 0)
    def _():
        total = (counts_ref[0] + counts_ref[1] + counts_ref[2]).astype(F32)
        here = (NTASK * counts_ref[label_ref[0]]).astype(F32)
        weight = jnp.full((1, D), total, F32) / jnp.full((1, D), here, F32)
        go = (cot_ref[...].astype(F32) * weight).astype(BF)
        go_ref[...] = go
        turned[...] = own_first(pos_ref[1], go)
        sum_ref[...] = column_sum(go.astype(F32))

    bias = b_ref[pl.ds(pl.multiple_of(pl.program_id(0) * D, D), D)]
    for r in rows_of(in_ref):
        act, slope = gelu_both(dot(in_ref[r : r + QB], w_ref[...]) + bias)
        act_ref[r : r + QB] = act.astype(BF)
        slope_ref[r : r + QB] = slope.astype(BF)
    grad = dot(act_ref[...], turned[...], TN)
    own_ref[...] = grad[:, :HALF]
    other_ref[...] = grad[:, HALF:]


def up(pos, counts, labels, in_two, cot, w_up, b_up):
    t = in_two.shape[0]
    cols = pl.BlockSpec((t, D), lambda j, *_: (0, j))
    half = pl.BlockSpec((D, HALF), lambda j, *_: (j, 0))
    return call(
        up_kernel,
        "up_and_down_grad",
        (FF // D,),
        [
            whole(t, D),
            whole(t, D),
            pl.BlockSpec((D, D), lambda j, *_: (0, j)),
            whole(FF),
        ],
        [cols, cols, whole(t, D), half, half, whole(1, D)],
        [shape((t, FF), BF)] * 2
        + [shape((t, D), BF)]
        + [shape((FF, HALF), F32)] * 2
        + [shape((1, D), F32)],
        [pltpu.VMEM((t, D), BF)],
        prefetch=3,
        us=20,
    )(pos, counts, labels, in_two, cot, w_up, b_up)


def hidden_kernel(pos_ref, go_ref, in_ref, slope_ref, w_ref, gp_ref, own_ref, other_ref, sum_ref):
    for r in rows_of(go_ref):
        grad = dot(go_ref[r : r + QB], w_ref[...], NT)
        gp_ref[r : r + QB] = (grad * slope_ref[r : r + QB].astype(F32)).astype(BF)
    sum_ref[0] = column_sum(gp_ref[...].astype(F32))
    grad = dot(in_ref[...], own_first(pos_ref[1], gp_ref[...]), TN)
    own_ref[0] = grad[:, :HALF]
    other_ref[0] = grad[:, HALF:]


def block_half():
    return pl.BlockSpec((1, D, HALF), lambda j, *_: (j, 0, 0))


def hidden(pos, go, in_two, slope, w_down):
    t = in_two.shape[0]
    cols = pl.BlockSpec((t, D), lambda j, *_: (0, j))
    return call(
        hidden_kernel,
        "hidden_grad",
        (FF // D,),
        [whole(t, D), whole(t, D), cols, pl.BlockSpec((D, D), lambda j, *_: (j, 0))],
        [cols, block_half(), block_half(), pl.BlockSpec((1, 1, D), lambda j, *_: (j, 0, 0))],
        [shape((t, FF), BF)] + [shape((FF // D, D, HALF), F32)] * 2 + [shape((FF // D, 1, D), F32)],
        prefetch=1,
        us=17,
    )(pos, go, in_two, slope, w_down)


def add_sums(ref, first, sums):
    for n, value in enumerate(sums):

        @pl.when(first)
        def _():
            ref[n : n + 1] = value

        @pl.when(jnp.logical_not(first))
        def _():
            ref[n : n + 1] += value


def middle_kernel(go_ref, mid_ref, g_ref, gp_ref, wu_ref, wo_ref, gm_ref, gb_ref, ga_ref, sums_ref):
    e = dot(gp_ref[...], wu_ref[...], NT)
    u, inv = unit(mid_ref[...])
    gm = go_ref[...].astype(F32) + norm_back(e, u, inv, g_ref[...])
    gm_ref[...] = gm
    gb = gm.astype(BF)
    gb_ref[...] = gb
    ga_ref[...] = dot(gb, wo_ref[...], NT).astype(BF)
    sums = [column_sum(e * u), column_sum(e), column_sum(gb.astype(F32))]
    add_sums(sums_ref, pl.program_id(0) == 0, sums)


def middle_back(go, mid, gain, gp, w_up, w_out, after=()):
    t = go.shape[0]
    row = pl.BlockSpec((QB, D), lambda i: (i, 0))
    return call(
        middle_kernel,
        "norm_two_back",
        (t // QB,),
        [row, row, whole(D), pl.BlockSpec((QB, FF), lambda i: (i, 0)), whole(D, FF), whole(D, D)],
        [row, row, row, whole(3, D)],
        [shape((t, D), F32), shape((t, D), BF), shape((t, D), BF), shape((3, D), F32)],
        us=16,
        after=len(after),
    )(go, mid, gain, gp, w_up, w_out, *after)


def attend_back_kernel(q_ref, k_ref, v_ref, ga_ref, p_ref, d_ref, dk_kept, dv_kept):
    t = q_ref.shape[0]
    for i, (q0, k0, n) in enumerate(bands(t)):
        queries, grads = q_ref[q0 : q0 + QB], ga_ref[q0 : q0 + QB]
        keys, values = k_ref[k0 : k0 + n], v_ref[k0 : k0 + n]
        dq = dk = dv = 0.0
        for a in range(2):
            probs = p_ref[a, i, :, :n]
            wide = probs.astype(F32)
            own = head_of(a, grads)
            prod = wide * dot(own, values, NT)
            ds = (prod - wide * jnp.sum(prod, axis=-1, keepdims=True)).astype(BF)
            dq = dq + dot(ds, head_of(a, keys))
            dk = dk + dot(ds, head_of(a, queries), TN)
            dv = dv + dot(probs, own, TN)
        d_ref[0, q0 : q0 + QB] = dq.astype(BF) * jnp.asarray(HEAD**-0.5, BF)
        if i:
            d_ref[1, k0 : k0 + QB] = (dk_kept[...] + dk[:QB]).astype(BF)
            d_ref[2, k0 : k0 + QB] = (dv_kept[...] + dv[:QB]).astype(BF)
        dk_kept[...] = dk[n - QB :]
        dv_kept[...] = dv[n - QB :]
    d_ref[1, t - QB :] = dk_kept[...].astype(BF)
    d_ref[2, t - QB :] = dv_kept[...].astype(BF)


def attend_back(proj, ga, probs, first, pairs, after=()):
    t = proj.shape[0]

    def block(part=0):
        return pl.BlockSpec((t, PAIR), lambda h: (0, part * (D // PAIR) + first + h))

    return call(
        attend_back_kernel,
        "attend_back",
        (pairs,),
        [
            block(),
            block(1),
            block(2),
            block(),
            pl.BlockSpec((2, t // QB, QB, 2 * QB), lambda h: (first + h, 0, 0, 0)),
        ],
        pl.BlockSpec((3, t, PAIR), lambda h: (0, 0, h)),
        shape((3, t, pairs * PAIR), BF),
        [pltpu.VMEM((QB, PAIR), F32)] * 2,
        us=20,
        after=len(after),
    )(proj, proj, proj, ga, probs, *after)


def first_heads_kernel(pos_ref, in_ref, d_ref, att_ref, gb_ref, own_ref, other_ref):
    core = pos_ref[1]
    grad = dot(in_ref[...], own_first(core, d_ref[0]), TN)
    grad_out = dot(att_ref[...], own_first(core, gb_ref[...]), TN)
    columns = [grad[:, n * LANES : (n + 1) * LANES] for n in range(4)]
    columns += [grad_out[:, n * LANES : (n + 1) * LANES] for n in range(2)]
    for n, (own, other) in enumerate([(0, 2), (1, 3), (4, 5)]):
        own_ref[n] = columns[own]
        other_ref[n] = columns[other]


def first_heads(pos, in_one, d, att, gb, after=()):
    t = in_one.shape[0]
    block = pl.BlockSpec((3, D, LANES), lambda j, *_: (j, 0, 0))
    return call(
        first_heads_kernel,
        "first_heads_grad",
        (3,),
        [
            whole(t, D),
            pl.BlockSpec((1, t, 4 * LANES), lambda j, *_: (j, 0, 0)),
            whole(t, D),
            pl.BlockSpec((t, 2 * LANES), lambda j, *_: (0, j)),
        ],
        [block, block],
        [shape((9, D, LANES), F32)] * 2,
        prefetch=1,
        us=10,
        after=len(after),
    )(pos, in_one, d, att, gb, *after)


def last_heads_kernel(pos_ref, in_ref, d_ref, own_ref, other_ref):
    turned = jnp.concatenate([own_first(pos_ref[1], d_ref[b]) for b in range(3)], axis=1)
    grad = dot(in_ref[...], turned, TN)
    for b in range(3):
        own_ref[b] = grad[:, 2 * b * LANES : (2 * b + 1) * LANES]
        other_ref[b] = grad[:, (2 * b + 1) * LANES : (2 * b + 2) * LANES]


def last_heads(pos, in_one, d, after=()):
    t = in_one.shape[0]
    return call(
        last_heads_kernel,
        "last_heads_grad",
        (1,),
        [whole(t, D), whole(3, t, 2 * LANES)],
        [whole(3, D, LANES)] * 2,
        [shape((3, D, LANES), F32)] * 2,
        prefetch=1,
        us=5,
        after=len(after),
    )(pos, in_one, d, *after)


def input_kernel(x_ref, gm_ref, g_ref, first_ref, last_ref, w_ref, mid_sums, down_sum, up_sums, gt_ref, sums_ref):
    e = 0.0
    split = first_ref.shape[2]
    for b in range(3):
        e = e + dot(first_ref[b], w_ref[:, b * D : b * D + split], NT)
        e = e + dot(last_ref[b], w_ref[:, b * D + split : (b + 1) * D], NT)
    u, inv = unit(x_ref[...].astype(F32))
    gt_ref[...] = (gm_ref[...] + norm_back(e, u, inv, g_ref[...])).astype(BF)
    start = pl.program_id(0) == 0
    sums = []
    for b in (0, 2):
        pair = [column_sum(ref[b].astype(F32)) for ref in (first_ref, last_ref)]
        sums.append(jnp.concatenate(pair, axis=1))
    add_sums(sums_ref, start, sums + [column_sum(e * u), column_sum(e)])

    @pl.when(start)
    def _():
        sums_ref[4:7] = mid_sums[...]
        sums_ref[7:8] = down_sum[...]
        for b in range(FF // D):
            sums_ref[8 + b : 9 + b] = up_sums[b]
        sums_ref[8 + FF // D :] = jnp.zeros((VECTORS - 8 - FF // D, D), F32)


def input_back(x, gm, gain, first, last, w_qkv, mid_sums, down_sum, up_sums, after=()):
    t = x.shape[0]
    row = pl.BlockSpec((QB, D), lambda i: (i, 0))
    part = lambda d: pl.BlockSpec((3, QB, d.shape[2]), lambda i: (0, i, 0))
    return call(
        input_kernel,
        "norm_one_back",
        (t // QB,),
        [
            row,
            row,
            whole(D),
            part(first),
            part(last),
            whole(D, 3 * D),
            whole(3, D),
            whole(1, D),
            whole(FF // D, 1, D),
        ],
        [row, whole(VECTORS, D)],
        [shape((t, D), BF), shape((VECTORS, D), F32)],
        us=10,
        after=len(after),
    )(x, gm, gain, first, last, w_qkv, mid_sums, down_sum, up_sums, *after)


def mix_kernel(mid_ref, act_ref, w_ref, b_ref, out_ref):
    out_ref[...] = (mid_ref[...] + dot(act_ref[...], w_ref[...]) + b_ref[...]).astype(BF)


def mix(mid, act, w_down, b_down, after=()):
    t = mid.shape[0]
    row = pl.BlockSpec((QB, D), lambda i: (i, 0))
    return call(
        mix_kernel,
        "mix",
        (t // QB,),
        [row, pl.BlockSpec((QB, FF), lambda i: (i, 0)), whole(FF, D), whole(D)],
        row,
        shape((t, D), BF),
        us=10,
        after=len(after),
    )(mid, act, w_down, b_down, *after)


def swap_with(x, n_dp, masks):
    pairs = []
    for dp in range(n_dp):
        for core in range(2):
            mask = masks[core]
            target = (dp ^ mask) * 2 + core if mask else dp * 2 + 1 - core
            pairs.append((dp * 2 + core, target))
    return lax.ppermute(x, AXES, pairs)


def in_vmem(x):
    return pltpu.with_memory_space_constraint(x, pltpu.VMEM)


def small_call(kernel, name, pos, arrays, outs, after=(), us=1):
    n = 1 + len(arrays)

    def body(*refs):
        kernel(*refs[:n], *refs[n + len(after) :])

    vmem = pl.BlockSpec(memory_space=pltpu.VMEM)
    return pl.pallas_call(
        body,
        in_specs=[SMEM] + [vmem] * len(arrays) + [pl.BlockSpec(memory_space=pl.ANY)] * len(after),
        out_specs=[vmem] * len(outs),
        out_shape=outs,
        compiler_params=pltpu.CompilerParams(vmem_limit_bytes=SMALL_LIMIT),
        cost_estimate=pl.CostEstimate(flops=SMALL_FLOPS, bytes_accessed=1, transcendentals=0),
        name=name,
    )(pos, *[in_vmem(x) for x in arrays], *[in_hbm(a) if a.dtype == BF or a.ndim < 4 else a for a in after])


class Stream:
    def __init__(self, n_dp, orders, pairs, step=0):
        self.n_dp, self.orders, self.pairs, self.step = n_dp, orders, pairs, step
        self.steps = len(orders[0])

    def __add__(self, other):
        assert self.step == other.step and self.orders == other.orders
        return Stream(self.n_dp, self.orders, self.pairs + other.pairs, self.step)

    @property
    def last(self):
        return self.step == self.steps

    @property
    def dims(self):
        count = 1 if self.last else self.n_dp >> (self.step + 1)
        return (count, sum(p[4] for p in self.pairs)) + self.pairs[0][0].shape[2:]

    def bit(self, core, j):
        a, b = self.orders[0][j], self.orders[1][j]
        return a if a == b else jnp.where(core == 0, a, b)

    def read(self, ref, pair, i, dp, core, mine):
        kind, first, size = pair[2:]
        if self.last:
            return ref[0, pl.ds(first, size)]
        bit = (dp >> self.bit(core, self.step)) & 1
        chosen = bit if mine else 1 - bit
        if kind == "kept":
            return ref[2 * i + chosen, pl.ds(first, size)]
        at = chosen << self.bit(core, 0)
        for j in range(1, self.steps):
            at = at + (((i >> (j - 1)) & 1) << self.bit(core, j))
        if kind == "rows":
            return ref[at, pl.ds(first, size)]
        return ref[pl.ds(first, size), at]


class Vectors:
    def __init__(self, total, n_dp):
        self.n_dp, self.total = n_dp, total
        self.masks = [0] + [1 << b for b in range(n_dp.bit_length() - 1)]
        self.swap()

    def swap(self):
        mask = self.masks.pop(0)
        self.received = swap_with(self.total, self.n_dp, (mask, mask))


def tick(pos, name, streams, after=(), vectors=None):
    arrays, jobs, outs = [], [], []

    def operand(array):
        for n, known in enumerate(arrays):
            if known is array:
                return n
        arrays.append(array)
        return len(arrays) - 1

    for stream in streams:
        pairs = [(operand(p[0]), operand(p[1])) for p in stream.pairs]
        jobs.append((stream, pairs, len(outs)))
        outs += [pltpu.VMEM(stream.dims, F32)] * (1 if stream.last else 2)
    if vectors is not None:
        pair = (operand(vectors.total), operand(vectors.received))
        outs.append(pltpu.VMEM((VECTORS, D), F32))

    def kernel(pos_ref, *refs):
        ins, out_refs = refs[: len(arrays)], refs[len(arrays) :]
        dp, core = pos_ref[0], pos_ref[1]

        def add(stream, pairs, n, mine, i):
            offset = 0
            for pair, (held, received) in zip(stream.pairs, pairs):
                a = stream.read(ins[held], pair, i, dp, core, mine)
                b = stream.read(ins[received], pair, i, dp, core, mine)
                out_refs[n + mine][i, pl.ds(offset, pair[4])] = a + b
                offset += pair[4]

        for stream, pairs, n in jobs:
            for mine in (0,) if stream.last else (0, 1):
                act = functools.partial(add, stream, pairs, n, mine)
                if stream.dims[0] <= 8:
                    for i in range(stream.dims[0]):
                        act(i)
                else:
                    pl.loop(0, stream.dims[0])(act)
        if vectors is not None:
            out_refs[-1][...] = ins[pair[0]][...] + ins[pair[1]][...]

    return small_call(kernel, name, pos, arrays, outs, after)


def advance(pos, name, streams, after=(), vectors=None):
    sent = tick(pos, name, streams, after, vectors)
    if vectors is not None:
        vectors.total = sent[-1]
        if vectors.masks:
            vectors.swap()
    out, n = [], 0
    for stream in streams:
        masks = tuple(1 << order[stream.step] for order in stream.orders)
        received = swap_with(sent[n], stream.n_dp, masks)
        pair = (sent[n + 1], received, "kept", 0, stream.dims[1])
        out.append(Stream(stream.n_dp, stream.orders, [pair], stream.step + 1))
        n += 2
    return out, sent


def place_kernel(pos_ref, *refs, places, blocks, halves):
    core = pos_ref[1]
    for source, b, n, row, cols in places:
        mine, theirs = refs[2 * source][0, b], refs[2 * source + 1][0, b]
        rows, width = mine.shape
        out = refs[len(refs) - blocks + n]
        out[row : row + rows, cols[0] : cols[0] + width] = jnp.where(core == 0, mine, theirs)
        out[row : row + rows, cols[1] : cols[1] + width] = jnp.where(core == 0, theirs, mine)
    if len(refs) > 2 * halves + blocks:
        vectors, singles, wide = refs[2 * halves], refs[2 * halves + 1 : 2 * halves + 9], refs[2 * halves + 9]
        rows, per = singles[0].shape[0], wide.shape[0]
        turned = pltpu.roll(vectors[:8], lax.rem(D - pos_ref[0] * rows, D), 1)
        for n, single in enumerate(singles):
            single[...] = turned[n, :rows]
        at = pos_ref[0] * per
        turned = pltpu.roll(vectors[8:], lax.rem(D - lax.rem(at, D), D), 1)
        line = lax.broadcasted_iota(jnp.int32, turned.shape, 0) == at // D
        wide[...] = jnp.sum(jnp.where(line, turned, 0.0), axis=0)[:per]


def place(pos, pairs, places, outs, after=(), vectors=None):
    given, more = [], []
    if vectors is not None:
        rows = D // vectors.n_dp
        given = [vectors.total]
        more = [(rows,)] * 8 + [(rows * FF // D,)]
    return small_call(
        functools.partial(place_kernel, places=places, blocks=len(outs), halves=len(pairs)),
        "place",
        pos,
        [x for pair in pairs for x in pair] + given,
        [shape(dims, F32) for dims in more + outs],
        after,
    )


def count_rounds(labels, n_dp, window):
    hits = (labels[:, None] == jnp.arange(NTASK, dtype=jnp.int32)[None, :]).astype(jnp.int32)
    counts = [jnp.sum(hits, axis=0) * (2 * window)]
    bit = 1
    while bit < n_dp:
        masks = [bit] if 2 * bit >= n_dp else [bit, 2 * bit, 3 * bit]
        counts.append(counts[-1] + sum(swap_with(counts[-1], n_dp, (m, m)) for m in masks))
        bit *= 4
    return counts[1:]


def per_device(tokens, segments, labels, cotangent, w_qkv, b_query, b_value, w_out, b_out, gamma_one, beta_one, gamma_two, beta_two, w_up, b_up, w_down, b_down, *, n_dp):
    windows, window, width = tokens.shape
    pos = jnp.stack([lax.axis_index("dp"), lax.axis_index("group")]).astype(jnp.int32)
    x = tokens.reshape(window, width)
    cot = cotangent.reshape(window, width)
    counts = count_rounds(labels, n_dp, window)

    steps = n_dp.bit_length() - 1
    plain = list(range(steps))
    wide = (plain, [1, 0] + plain[2:])
    late = (plain[2:] + [0, 1], plain[2:] + [1, 0])
    rows = D // n_dp

    def other_core(value):
        return swap_with(value, n_dp, (0, 0))

    def begin(kind, own, other, late_blocks=0):
        blocks, width = (4, HALF) if kind == "rows" else (own.shape[0], own.shape[2])
        dims = (n_dp, blocks, rows, width) if kind == "rows" else (blocks, n_dp, rows, width)
        own, received = own.reshape(dims), other_core(other.reshape(dims))
        streams = [Stream(n_dp, wide, [(own, received, kind, 0, blocks - late_blocks)])]
        if late_blocks:
            streams.append(Stream(n_dp, late, [(own, received, kind, blocks - late_blocks, late_blocks)]))
        return streams

    go_on = functools.partial(advance, pos)
    proj, in_one = project(x, gamma_one, beta_one, w_qkv, b_query, b_value)
    att, probs = attend(segments, proj, counts[:1])
    mid, in_two = branch(x, att, w_out, b_out, gamma_two, beta_two)
    act, slope, go, own, other, sum_down = up(pos, counts[-1], labels, in_two, cot, w_up, b_up)
    downs = begin("rows", own, other, LATE[0])
    gp, own, other, sum_up = hidden(pos, go, in_two, slope, w_down)
    ups = begin("blocks", own, other, LATE[1])
    downs, sent = go_on("tick_1", downs, (gp,))
    gm, gb, ga, sums_mid = middle_back(go, mid, gamma_two, gp, w_up, w_out, sent[:1])
    ups, sent = go_on("tick_2", ups, (ga,))
    first = attend_back(proj, ga, probs, 0, 4, sent[:1])
    early, sent = go_on("tick_3", [a + b for a, b in zip(downs, ups)], (first,))
    own, other = first_heads(pos, in_one, first, att, gb, sent[:1])
    firsts = begin("blocks", own, other)
    last = attend_back(proj, ga, probs, 4, 2, (own,))
    streams, sent = go_on("tick_4", firsts + early, (last,))
    firsts, early = streams[:1], streams[1:]
    own, other = last_heads(pos, in_one, last, sent[:1])
    lasts = begin("blocks", own, other)
    grad_tokens, vectors = input_back(
        x, gm, gamma_one, first, last, w_qkv, sums_mid, sum_down, sum_up, (own,)
    )
    vectors = Vectors(vectors, n_dp)
    streams, sent = go_on("tick_5", lasts + early, (grad_tokens,), vectors)
    lasts, early = streams[:1], streams[1:]
    mixed = mix(mid, act, w_down, b_down, sent[:1])
    while not early[0].last:
        early, sent = go_on("tick_more", early, sent[:1], vectors)
    firsts, sent = go_on("tick_6", firsts, (mixed,), vectors)
    lasts, sent = go_on("tick_7", lasts, sent[:1], vectors)
    firsts, sent = go_on("tick_8", firsts, sent[:1], vectors)
    sent = tick(pos, "own_early", early, sent[:1], vectors)
    vectors.total = sent[-1]
    mine = sent[:-1]
    theirs = [other_core(v) for v in mine]
    while not lasts[0].last:
        if not firsts[0].last:
            streams, sent = go_on("tick_9", lasts + firsts, sent[:1])
            lasts, firsts = streams[:1], streams[1:]
        else:
            lasts, sent = go_on("tick_9", lasts, sent[:1])
    places = []
    sizes = [(4 - LATE[0], 4 - LATE[1]), (LATE[0], LATE[1])]
    for n, (downs_here, ups_here) in enumerate(sizes[: len(mine)]):
        for b in range(downs_here):
            at = b if n == 0 else 4 - LATE[0] + b
            places.append((n, b, 0, at * rows, (0, HALF)))
        for b in range(ups_here):
            at = b if n == 0 else 4 - LATE[1] + b
            places.append((n, downs_here + b, 1, 0, (at * D, at * D + HALF)))
    *singles, grad_b_up, grad_down, grad_up = place(
        pos, list(zip(mine, theirs)), places, [(4 * rows, D), (rows, FF)], sent[:1], vectors
    )
    mine = tick(pos, "own_late", firsts + lasts, (grad_up,))
    theirs = [other_core(v) for v in mine]
    places = []
    for b in range(3):
        for n in range(2):
            at = b * D + n * LANES
            places.append((0, 3 * b + n, 0, 0, (at, at + 2 * LANES)))
        at = 2 * b * LANES
        places.append((0, 3 * b + 2, 1, 0, (at, at + LANES)))
        at = b * D + 4 * LANES
        places.append((1, b, 0, 0, (at, at + LANES)))
    grad_qkv, grad_out = place(pos, list(zip(mine, theirs)), places, [(rows, 3 * D), (rows, D)])
    query, value, gain_one, shift_one, gain_two, shift_two, out, bias_down = singles
    return (
        mixed.reshape(tokens.shape),
        grad_tokens.reshape(tokens.shape),
        grad_qkv,
        query,
        value,
        grad_out,
        out,
        gain_one,
        shift_one,
        gain_two,
        shift_two,
        grad_up,
        grad_b_up,
        grad_down,
        bias_down,
        counts[-1],
    )


def solution(mesh):
    split = P(("dp", "group"), None, None)
    return jax.shard_map(
        functools.partial(per_device, n_dp=mesh.shape["dp"]),
        mesh=mesh,
        in_specs=(split, P(("dp", "group"), None), P(("dp", "group")), split) + (P(),) * 13,
        out_specs=(split, split, P("dp", None), P("dp"), P("dp"), P("dp", None))
        + (P("dp"),) * 5
        + (P("dp", None), P("dp"), P("dp", None), P("dp"), P()),
        check_vma=False,
    )
```

```python
import functools
import math

import jax
import jax.numpy as jnp
from jax import lax
from jax.experimental import pallas as pl
from jax.experimental.pallas import tpu as pltpu
from jax.sharding import PartitionSpec as P

F32 = jnp.float32
BF = jnp.bfloat16
D = 768
HEADS = 12
HEAD = 64
PAIR = 2 * HEAD
LANES = 128
FF = 3072
NTASK = 3
VECTORS = 16
QB = 256
EPISODE = 256
QUERIES = 128
STAGGER = 2
HALF = D // 2
AXES = ("dp", "group")
NN = (((1,), (0,)), ((), ()))
NT = (((1,), (1,)), ((), ()))
TN = (((0,), (0,)), ((), ()))
PLAN = {'D': [(3, ((1, 2, 3, 0), (0, 2, 3, 1))), (1, ((2, 3, 1, 0), (2, 3, 0, 1)))], 'U': [(3, ((0, 1, 2, 3), (1, 0, 2, 3)))], 'F': [(3, ((1, 2, 0, 3), (0, 2, 1, 3))), (6, ((1, 0, 2, 3), (0, 1, 2, 3)))], 'L': [(3, ((0, 1, 2, 3), (1, 0, 2, 3)))], 'W': [(1, ((2, 0, 1, 3), (2, 1, 0, 3)))]}
SCHEDULE = ['hidden', ('D0', 'D1'), 'hidden last', 'middle', ('U0', 'W0', 'D1'), 'attend first', ('D0',), 'first heads', ('D1',), ('U0',), 'attend last', ('D1', 'W0', 'F0', 'F1'), 'last heads', ('U0',), ('D0',), 'input', ('W0', 'F0', 'L0', 'D1'), ('V',), ('U0', 'W0'), ('F1',), 'mix', ('D0', 'W0', 'F0', 'V'), ('U0', 'F1'), ('D0', 'F0', 'V'), ('L0',), ('L0', 'V', 'F0', 'F1'), ('V', 'L0'), ('F1', 'L0')]
SMALL_FLOPS = 1000000000
SMALL_LIMIT = 20 * 2**20
BIG = 1 << 40
COST = {'first_heads_grad': 0, 'last_heads_grad': 0, 'attend_back_first': 20, 'attend_back_last': 20, 'norm_one_back': 3, 'mix': 20, 'norm_two_back': 3}
FREE = {"hidden_grad": [6], "hidden_grad_last": [3, 4, 6], "norm_two_back": [0, 3, 4], "first_heads_grad": [1, 2], "last_heads_grad": [1, 2], "norm_one_back": [3, 4, 5], "mix": [2]}
OUT = {"up_and_down_grad": [2], "hidden_grad": [0, 4], "hidden_grad_last": [0], "attend_back_first": [0], "attend_back_last": [0]}
VMEM_LIMIT = 34 * 2**20
SCALE = 1
FLOPS = 4e9


def dot(a, b, dims=NN):
    return lax.dot_general(a, b, dims, preferred_element_type=F32)


def in_hbm(x):
    return pltpu.with_memory_space_constraint(x, pltpu.HBM)


def call(kernel, name, grid, in_specs, out_specs, out_shape, scratch=(), prefetch=0, us=3, after=0, free=(), limit=None):
    in_specs = list(in_specs) + [pl.BlockSpec(memory_space=pl.ANY)] * after
    body = kernel
    if after:
        start = prefetch + len(in_specs) - after

        def body(*refs):
            kernel(*refs[:start], *refs[start + after :])

    single = not isinstance(out_shape, list)
    made = [(s if n in OUT.get(name, ()) else pltpu.HBM(s.shape, s.dtype)) if isinstance(s, jax.ShapeDtypeStruct) else s for n, s in enumerate([out_shape] if single else out_shape)]
    run = pl.pallas_call(
        body,
        grid_spec=pltpu.PrefetchScalarGridSpec(
            num_scalar_prefetch=prefetch,
            grid=grid,
            in_specs=in_specs,
            out_specs=[out_specs] if single else out_specs,
            scratch_shapes=list(scratch),
        ),
        out_shape=made,
        compiler_params=pltpu.CompilerParams(vmem_limit_bytes=limit or VMEM_LIMIT),
        cost_estimate=pl.CostEstimate(flops=int(COST.get(name, us) * FLOPS), bytes_accessed=int(us * SCALE), transcendentals=0),
        name=name,
    )

    def apply(*args):
        last = len(args) - after
        table = FREE.get(name, free)
        args = [x if n < prefetch or n >= last or n in table else in_hbm(x) for n, x in enumerate(args)]
        out = run(*args)
        return out[0] if single else out

    return apply


def shape(dims, dtype):
    return jax.ShapeDtypeStruct(dims, dtype)


def whole(*dims):
    return pl.BlockSpec(dims, lambda *_: (0,) * len(dims))


SMEM = pl.BlockSpec(memory_space=pltpu.SMEM)


def unit(x):
    centered = x - jnp.mean(x, axis=-1, keepdims=True)
    inv = lax.rsqrt(jnp.mean(centered * centered, axis=-1, keepdims=True) + 1e-05)
    return centered * inv, inv


def norm_back(e, u, inv, gain):
    scaled = e * gain
    return inv * (
        scaled
        - jnp.mean(scaled, axis=-1, keepdims=True)
        - u * jnp.mean(scaled * u, axis=-1, keepdims=True)
    )


def rows_of(ref):
    return range(0, ref.shape[0], QB)


def column_sum(x):
    return jnp.sum(x, axis=0, keepdims=True)


def bands(t):
    return [(q, max(0, q - EPISODE), min(q + QUERIES, EPISODE + QUERIES)) for q in range(0, t, QUERIES)]


def head_pair(x):
    lane = lax.broadcasted_iota(jnp.int32, (1, PAIR), 1)
    zero = jnp.zeros_like(x)
    return jnp.concatenate([jnp.where(lane < HEAD, x, zero), jnp.where(lane < HEAD, zero, x)], axis=0)


def heads_side_by_side(x):
    return jnp.concatenate([x[:HEAD, :QUERIES], x[HEAD:, QUERIES:]], axis=0).T


def staggered(units, stages):
    waiting = [{} for _ in stages]
    lags = [0, STAGGER, STAGGER + 1]
    for n in range(len(units) + lags[-1]):
        for k, stage in enumerate(stages):
            m = n - lags[k]
            if 0 <= m < len(units):
                given = () if k == 0 else (waiting[k - 1].pop(m),)
                waiting[k][m] = stage(*units[m], *given)


def forward_kernel(x_ref, seg_ref, g1_ref, s1_ref, wq_ref, wk_ref, wv_ref, bq_ref, bv_ref, wo_ref, bo_ref, g2_ref, s2_ref, proj_ref, in_one_ref, att_ref, p_ref, mid_ref, in_two_ref, bias_ref, turned_ref, acc_ref):
    g = pl.program_id(0)
    t = x_ref.shape[0]
    blocks = bands(t)

    @pl.when(g == 0)
    def _():
        for r in rows_of(x_ref):
            u, _ = unit(x_ref[r : r + QB].astype(F32))
            in_one_ref[r : r + QB] = (u * g1_ref[...] + s1_ref[...]).astype(BF)
        hot = (seg_ref[...] == lax.broadcasted_iota(jnp.int32, (8, t), 0)).astype(BF)
        for i, (q0, k0, n) in enumerate(blocks):
            same = dot(hot[:, k0 : k0 + n], hot[:, q0 : q0 + QUERIES], TN)
            col = k0 + lax.broadcasted_iota(jnp.int32, (n, QUERIES), 0)
            row = q0 + lax.broadcasted_iota(jnp.int32, (n, QUERIES), 1)
            bias_ref[i, :n] = jnp.where((same > 0.5) & (col <= row), 0.0, -1e30).astype(F32)

    width = wq_ref.shape[1]
    here = pl.ds(pl.multiple_of(g * width, width), width)
    for r in range(0, t, 2 * QB):
        rows = in_one_ref[r : r + 2 * QB]
        proj_ref[0, r : r + 2 * QB] = ((dot(rows, wq_ref[...]) + bq_ref[here]) * HEAD**-0.5).astype(BF)
        proj_ref[1, r : r + 2 * QB] = dot(rows, wk_ref[...]).astype(BF)
        proj_ref[2, r : r + 2 * QB] = (dot(rows, wv_ref[...]) + bv_ref[here]).astype(BF)
    pairs = width // PAIR
    for w in range(pairs):
        turned_ref[w] = proj_ref[2, :, w * PAIR : (w + 1) * PAIR].T

    def scores(w, i):
        q0, k0, n = blocks[i]
        cols = slice(w * PAIR, (w + 1) * PAIR)
        return dot(proj_ref[1, k0 : k0 + n, cols], head_pair(proj_ref[0, q0 : q0 + QUERIES, cols]), NT)

    def softmax(w, i, values):
        n = blocks[i][2]
        parts = []
        for a in range(2):
            part = values[:, a * QUERIES : (a + 1) * QUERIES] + bias_ref[i, :n]
            e = jnp.exp(part - jnp.max(part, axis=0, keepdims=True))
            probs = (e * (1.0 / jnp.sum(e, axis=0, keepdims=True))).astype(BF)
            p_ref[w, i, :n, a * QUERIES : (a + 1) * QUERIES] = probs
            parts.append(probs)
        return jnp.concatenate(parts, axis=1)

    def attend(w, i, probs):
        q0, k0, n = blocks[i]
        out = dot(turned_ref[w, :, k0 : k0 + n], probs)
        att_ref[q0 : q0 + QUERIES, w * PAIR : (w + 1) * PAIR] = heads_side_by_side(out).astype(BF)

    units = [(w, i) for w in range(pairs) for i in range(len(blocks))]
    staggered(units, (scores, softmax, attend))

    @pl.when(g == 0)
    def _():
        acc_ref[...] = dot(att_ref[...], wo_ref[...])

    @pl.when((g > 0) & (g < pl.num_programs(0) - 1))
    def _():
        acc_ref[...] += dot(att_ref[...], wo_ref[...])

    @pl.when(g == pl.num_programs(0) - 1)
    def _():
        for r in rows_of(x_ref):
            branch = acc_ref[r : r + QB] + dot(att_ref[r : r + QB], wo_ref[...]) + bo_ref[...]
            mid = x_ref[r : r + QB].astype(F32) + branch
            mid_ref[r : r + QB] = mid
            u, _ = unit(mid)
            in_two_ref[r : r + QB] = (u * g2_ref[...] + s2_ref[...]).astype(BF)


def forward(x, seg, gain_one, shift_one, w_qkv, b_query, b_value, w_out, b_out, gain_two, shift_two):
    t = x.shape[0]
    width = 2 * PAIR
    steps = D // width
    count = t // QUERIES
    keys = EPISODE + QUERIES

    def weights(part):
        return pl.BlockSpec((D, width), lambda g: (0, part * steps + g))

    return call(
        forward_kernel,
        "forward",
        (steps,),
        [whole(t, D), whole(1, t), whole(D), whole(D), weights(0), weights(1), weights(2), whole(D), whole(D)]
        + [pl.BlockSpec((width, D), lambda g: (g, 0)), whole(D), whole(D), whole(D)],
        [
            pl.BlockSpec((3, t, width), lambda g: (0, 0, g)),
            whole(t, D),
            pl.BlockSpec((t, width), lambda g: (0, g)),
            pl.BlockSpec((2, count, keys, 2 * QUERIES), lambda g: (g, 0, 0, 0)),
            whole(t, D),
            whole(t, D),
        ],
        [
            shape((3, t, D), BF),
            shape((t, D), BF),
            shape((t, D), BF),
            shape((HEADS // 2, count, keys, 2 * QUERIES), BF),
            shape((t, D), F32),
            shape((t, D), BF),
        ],
        [
            pltpu.VMEM((count, keys, QUERIES), F32),
            pltpu.VMEM((2, PAIR, t), BF),
            pltpu.VMEM((t, D), F32),
        ],
        us=24,
        limit=60 * 2**20,
    )(x, seg, gain_one, shift_one, w_qkv, w_qkv, w_qkv, b_query, b_value, w_out, b_out, gain_two, shift_two)


def gelu_both(v):
    cdf = 0.5 * (1.0 + lax.erf(v * (2.0**-0.5)))
    pdf = jnp.exp(-0.5 * v * v) * (1.0 / math.sqrt(2 * math.pi))
    return v * cdf, cdf + v * pdf


def own_first(core, x):
    half = x.shape[1] // 2
    return jnp.where(core == 0, x, jnp.concatenate([x[:, half:], x[:, :half]], axis=1))


def task_weight(counts_ref, label_ref, width):
    total = (counts_ref[0] + counts_ref[1] + counts_ref[2]).astype(F32)
    here = (NTASK * counts_ref[label_ref[0]]).astype(F32)
    return jnp.full((1, width), total, F32) / jnp.full((1, width), here, F32)


def up_kernel(pos_ref, in_ref, cot_ref, w_ref, b_ref, act_ref, slope_ref, own_ref, other_ref, turned):
    @pl.when(pl.program_id(0) == 0)
    def _():
        turned[...] = own_first(pos_ref[1], cot_ref[...])

    bias = b_ref[pl.ds(pl.multiple_of(pl.program_id(0) * D, D), D)]
    rows = QB // 2
    starts = list(range(0, in_ref.shape[0], rows))
    pre = None
    for r in starts + [None]:
        ready, pre = pre, None if r is None else dot(in_ref[r : r + rows], w_ref[...]) + bias
        if ready is not None:
            act, slope = gelu_both(ready)
            act_ref[last : last + rows] = act.astype(BF)
            slope_ref[last : last + rows] = slope.astype(BF)
        last = r
    grad = dot(act_ref[...], turned[...], TN)
    own_ref[...] = grad[:, :HALF]
    other_ref[...] = grad[:, HALF:]


def up(pos, in_two, cot, w_up, b_up, after=()):
    t = in_two.shape[0]
    cols = pl.BlockSpec((t, D), lambda j, *_: (0, j))
    half = pl.BlockSpec((D, HALF), lambda j, *_: (j, 0))
    return call(
        up_kernel,
        "up_and_down_grad",
        (FF // D,),
        [
            whole(t, D),
            whole(t, D),
            pl.BlockSpec((D, D), lambda j, *_: (0, j)),
            whole(FF),
        ],
        [cols, cols, half, half],
        [shape((t, FF), BF)] * 2 + [shape((FF, HALF), F32)] * 2,
        [pltpu.VMEM((t, D), BF)],
        prefetch=1,
        us=16,
        after=len(after),
    )(pos, in_two, cot, w_up, b_up, *after)


def hidden_kernel(pos_ref, counts_ref, label_ref, cot_ref, in_ref, slope_ref, w_ref, *refs):
    gp_ref, own_ref, other_ref, sum_ref = refs[:4]
    go_ref = cot_ref
    if len(refs) > 4:
        go_ref, down_ref = refs[4:]

        @pl.when(pl.program_id(0) == 0)
        def _():
            go = (cot_ref[...].astype(F32) * task_weight(counts_ref, label_ref, D)).astype(BF)
            go_ref[...] = go
            down_ref[...] = column_sum(go.astype(F32))

    grad = None
    for r in list(rows_of(go_ref)) + [None]:
        ready, grad = grad, None if r is None else dot(go_ref[r : r + QB], w_ref[...], NT)
        if ready is not None:
            gp_ref[last : last + QB] = (ready * slope_ref[last : last + QB].astype(F32)).astype(BF)
        last = r
    sum_ref[0] = column_sum(gp_ref[...].astype(F32))
    grad = dot(in_ref[...], own_first(pos_ref[1], gp_ref[...]), TN)
    own_ref[0] = grad[:, :HALF]
    other_ref[0] = grad[:, HALF:]


def block_half():
    return pl.BlockSpec((1, D, HALF), lambda j, *_: (j, 0, 0))


def hidden(pos, counts, labels, cot, in_two, slope, w_down, first, count, after=()):
    t = in_two.shape[0]
    cols = pl.BlockSpec((t, D), lambda j, *_: (0, j))
    more = [] if first else [(whole(t, D), shape((t, D), BF)), (whole(1, D), shape((1, D), F32))]
    return call(
        hidden_kernel,
        "hidden_grad_last" if first else "hidden_grad",
        (count,),
        [
            whole(t, D),
            whole(t, D),
            pl.BlockSpec((t, D), lambda j, *_: (0, first + j)),
            pl.BlockSpec((D, D), lambda j, *_: (first + j, 0)),
        ],
        [cols, block_half(), block_half(), pl.BlockSpec((1, 1, D), lambda j, *_: (j, 0, 0))]
        + [spec for spec, _ in more],
        [shape((t, count * D), BF)]
        + [shape((count, D, HALF), F32)] * 2
        + [shape((count, 1, D), F32)]
        + [made for _, made in more],
        prefetch=3,
        us=4 * count,
        after=len(after),
    )(pos, counts, labels, cot, in_two, slope, w_down, *after)


def add_sums(ref, first, sums):
    for n, value in enumerate(sums):

        @pl.when(first)
        def _():
            ref[n : n + 1] = value

        @pl.when(jnp.logical_not(first))
        def _():
            ref[n : n + 1] += value


def middle_kernel(go_ref, mid_ref, g_ref, gp_ref, last_ref, wu_ref, wo_ref, gm_ref, gb_ref, ga_ref, sums_ref):
    starts = rows_of(gm_ref)
    split = gp_ref.shape[1]

    def product(r):
        e = dot(gp_ref[r : r + QB], wu_ref[:, :split], NT)
        return e + dot(last_ref[r : r + QB], wu_ref[:, split:], NT)

    following = product(0)
    sums = [0.0, 0.0, 0.0]
    for r in starts:
        e = following
        if r + QB < gm_ref.shape[0]:
            following = product(r + QB)
        u, inv = unit(mid_ref[r : r + QB])
        gm = go_ref[r : r + QB].astype(F32) + norm_back(e, u, inv, g_ref[...])
        gm_ref[r : r + QB] = gm
        gb = gm.astype(BF)
        gb_ref[r : r + QB] = gb
        ga_ref[r : r + QB] = dot(gb, wo_ref[...], NT).astype(BF)
        parts = (column_sum(e * u), column_sum(e), column_sum(gb.astype(F32)))
        sums = [total + part for total, part in zip(sums, parts)]
    add_sums(sums_ref, pl.program_id(0) == 0, sums)


def middle_back(go, mid, gain, gp, gp_last, w_up, w_out, after=()):
    t = go.shape[0]
    rows = 2 * QB
    row = pl.BlockSpec((rows, D), lambda i: (i, 0))
    return call(
        middle_kernel,
        "norm_two_back",
        (t // rows,),
        [row, row, whole(D)]
        + [pl.BlockSpec((rows, part.shape[1]), lambda i: (i, 0)) for part in (gp, gp_last)]
        + [whole(D, FF), whole(D, D)],
        [row, row, row, whole(3, D)],
        [shape((t, D), F32), shape((t, D), BF), shape((t, D), BF), shape((3, D), F32)],
        us=16,
        after=len(after),
    )(go, mid, gain, gp, gp_last, w_up, w_out, *after)


def attend_back_kernel(q_ref, k_ref, v_ref, ga_ref, p_ref, d_ref, dk_ref, dv_ref, turned_ref):
    t = q_ref.shape[1]
    blocks = bands(t)
    pairs = q_ref.shape[2] // PAIR
    for w in range(pairs):
        turned_ref[w] = k_ref[0, :, w * PAIR : (w + 1) * PAIR].T

    def grad_probs(w, i):
        q0, k0, n = blocks[i]
        cols = slice(w * PAIR, (w + 1) * PAIR)
        return dot(v_ref[0, k0 : k0 + n, cols], head_pair(ga_ref[q0 : q0 + QUERIES, cols]), NT)

    def grad_scores(w, i, values):
        probs = p_ref[w, i, : blocks[i][2]].astype(F32)
        prod = probs * values
        return (prod - probs * jnp.sum(prod, axis=0, keepdims=True)).astype(BF)

    def rest(w, i, ds):
        q0, k0, n = blocks[i]
        cols = slice(w * PAIR, (w + 1) * PAIR)
        dq = heads_side_by_side(dot(turned_ref[w, :, k0 : k0 + n], ds))
        d_ref[0, q0 : q0 + QUERIES, cols] = dq.astype(BF) * jnp.asarray(HEAD**-0.5, BF)
        known = n - QUERIES if i else 0
        done = blocks[i + 1][1] if i + 1 < len(blocks) else t
        dk = dot(ds, head_pair(q_ref[0, q0 : q0 + QUERIES, cols]))
        dv = dot(p_ref[w, i, :n], head_pair(ga_ref[q0 : q0 + QUERIES, cols]))
        for part, ref, value in ((1, dk_ref, dk), (2, dv_ref, dv)):
            if known:
                ref[k0 : k0 + known, cols] += value[:known]
            ref[k0 + known : k0 + n, cols] = value[known:]
            if done > k0:
                d_ref[part, k0:done, cols] = ref[k0:done, cols].astype(BF)

    units = [(w, i) for w in range(pairs) for i in range(len(blocks))]
    staggered(units, (grad_probs, grad_scores, rest))


def attend_back(proj, ga, probs, first, pairs, after=()):
    t = proj.shape[1]
    width = 2 * PAIR
    start = first // 2

    def block(part):
        return pl.BlockSpec((1, t, width), lambda h: (part, 0, start + h))

    return call(
        attend_back_kernel,
        "attend_back_last" if first else "attend_back_first",
        (pairs // 2,),
        [
            block(0),
            block(1),
            block(2),
            pl.BlockSpec((t, width), lambda h: (0, start + h)),
            pl.BlockSpec((2,) + probs.shape[1:], lambda h: (start + h, 0, 0, 0)),
        ],
        pl.BlockSpec((3, t, width), lambda h: (0, 0, h)),
        shape((3, t, pairs * PAIR), BF),
        [pltpu.VMEM((t, width), F32)] * 2 + [pltpu.VMEM((2, PAIR, t), BF)],
        us=3 * pairs,
        after=len(after),
    )(proj, proj, proj, ga, probs, *after)


def first_heads_kernel(pos_ref, in_ref, d_ref, att_ref, gb_ref, own_ref, other_ref):
    core = pos_ref[1]
    grad = dot(in_ref[...], own_first(core, d_ref[0]), TN)
    grad_out = dot(att_ref[...], own_first(core, gb_ref[...]), TN)
    columns = [grad[:, n * LANES : (n + 1) * LANES] for n in range(4)]
    columns += [grad_out[:, n * LANES : (n + 1) * LANES] for n in range(2)]
    for n, (own, other) in enumerate([(0, 2), (1, 3), (4, 5)]):
        own_ref[n] = columns[own]
        other_ref[n] = columns[other]


def first_heads(pos, in_one, d, att, gb, after=()):
    t = in_one.shape[0]
    block = pl.BlockSpec((3, D, LANES), lambda j, *_: (j, 0, 0))
    return call(
        first_heads_kernel,
        "first_heads_grad",
        (3,),
        [
            whole(t, D),
            pl.BlockSpec((1, t, 4 * LANES), lambda j, *_: (j, 0, 0)),
            whole(t, D),
            pl.BlockSpec((t, 2 * LANES), lambda j, *_: (0, j)),
        ],
        [block, block],
        [shape((9, D, LANES), F32)] * 2,
        prefetch=1,
        us=10,
        after=len(after),
    )(pos, in_one, d, att, gb, *after)


def last_heads_kernel(pos_ref, in_ref, d_ref, own_ref, other_ref):
    turned = jnp.concatenate([own_first(pos_ref[1], d_ref[b]) for b in range(3)], axis=1)
    grad = dot(in_ref[...], turned, TN)
    for b in range(3):
        own_ref[b] = grad[:, 2 * b * LANES : (2 * b + 1) * LANES]
        other_ref[b] = grad[:, (2 * b + 1) * LANES : (2 * b + 2) * LANES]


def last_heads(pos, in_one, d, after=()):
    t = in_one.shape[0]
    return call(
        last_heads_kernel,
        "last_heads_grad",
        (1,),
        [whole(t, D), whole(3, t, 2 * LANES)],
        [whole(3, D, LANES)] * 2,
        [shape((3, D, LANES), F32)] * 2,
        prefetch=1,
        us=5,
        after=len(after),
    )(pos, in_one, d, *after)


def input_kernel(x_ref, gm_ref, g_ref, first_ref, last_ref, w_ref, mid_sums, down_sum, up_sums, up_last, gt_ref, sums_ref):
    split = first_ref.shape[2]

    def product(r):
        e = 0.0
        for b in range(3):
            e = e + dot(first_ref[b, r : r + QB], w_ref[:, b * D : b * D + split], NT)
            e = e + dot(last_ref[b, r : r + QB], w_ref[:, b * D + split : (b + 1) * D], NT)
        return e

    following = product(0)
    norm_sums = [0.0, 0.0]
    for r in rows_of(gt_ref):
        e = following
        if r + QB < gt_ref.shape[0]:
            following = product(r + QB)
        u, inv = unit(x_ref[r : r + QB].astype(F32))
        gt_ref[r : r + QB] = (gm_ref[r : r + QB] + norm_back(e, u, inv, g_ref[...])).astype(BF)
        norm_sums = [norm_sums[0] + column_sum(e * u), norm_sums[1] + column_sum(e)]
    start = pl.program_id(0) == 0
    sums = []
    for b in (0, 2):
        pair = [column_sum(ref[b].astype(F32)) for ref in (first_ref, last_ref)]
        sums.append(jnp.concatenate(pair, axis=1))
    add_sums(sums_ref, start, sums + norm_sums)

    @pl.when(start)
    def _():
        sums_ref[4:7] = mid_sums[...]
        sums_ref[7:8] = down_sum[...]
        at = 8
        for ref in (up_sums, up_last):
            for b in range(ref.shape[0]):
                sums_ref[at : at + 1] = ref[b]
                at += 1
        sums_ref[8 + FF // D :] = jnp.zeros((VECTORS - 8 - FF // D, D), F32)


def input_back(x, gm, gain, first, last, w_qkv, mid_sums, down_sum, up_sums, up_last, after=()):
    t = x.shape[0]
    rows = 2 * QB
    row = pl.BlockSpec((rows, D), lambda i: (i, 0))
    part = lambda d: pl.BlockSpec((3, rows, d.shape[2]), lambda i: (0, i, 0))
    return call(
        input_kernel,
        "norm_one_back",
        (t // rows,),
        [
            row,
            row,
            whole(D),
            part(first),
            part(last),
            whole(D, 3 * D),
            whole(3, D),
            whole(1, D),
            whole(*up_sums.shape),
            whole(*up_last.shape),
        ],
        [row, whole(VECTORS, D)],
        [shape((t, D), BF), shape((VECTORS, D), F32)],
        us=10,
        after=len(after),
    )(x, gm, gain, first, last, w_qkv, mid_sums, down_sum, up_sums, up_last, *after)


def mix_kernel(mid_ref, act_ref, w_ref, b_ref, out_ref):
    out_ref[...] = (mid_ref[...] + dot(act_ref[...], w_ref[...]) + b_ref[...]).astype(BF)


def mix(mid, act, w_down, b_down, after=()):
    t = mid.shape[0]
    rows = 2 * QB
    row = pl.BlockSpec((rows, D), lambda i: (i, 0))
    return call(
        mix_kernel,
        "mix",
        (t // rows,),
        [row, pl.BlockSpec((rows, FF), lambda i: (i, 0)), whole(FF, D), whole(D)],
        row,
        shape((t, D), BF),
        us=10,
        after=len(after),
    )(mid, act, w_down, b_down, *after)


def swap_with(x, n_dp, masks):
    pairs = []
    for dp in range(n_dp):
        for core in range(2):
            mask = masks[core]
            target = (dp ^ mask) * 2 + core if mask else dp * 2 + 1 - core
            pairs.append((dp * 2 + core, target))
    return lax.ppermute(x, AXES, pairs)


def in_vmem(x):
    return pltpu.with_memory_space_constraint(x, pltpu.VMEM)


def small_call(kernel, name, scalars, arrays, outs, after=()):
    n = len(scalars) + len(arrays)

    def body(*refs):
        kernel(*refs[:n], *refs[n + len(after) :])

    vmem = pl.BlockSpec(memory_space=pltpu.VMEM)
    return pl.pallas_call(
        body,
        in_specs=[SMEM] * len(scalars) + [vmem] * len(arrays) + [pl.BlockSpec(memory_space=pl.ANY)] * len(after),
        out_specs=[vmem] * len(outs),
        out_shape=outs,
        compiler_params=pltpu.CompilerParams(vmem_limit_bytes=SMALL_LIMIT),
        cost_estimate=pl.CostEstimate(flops=SMALL_FLOPS, bytes_accessed=1, transcendentals=0),
        name=name,
    )(*scalars, *[in_vmem(x) if x.size < BIG else x for x in arrays], *[in_hbm(a) if a.dtype == BF or a.ndim < 4 else a for a in after])


class Stream:
    def __init__(self, n_dp, orders, pairs, names, step=0, weighted=False):
        self.n_dp, self.orders, self.pairs, self.step = n_dp, orders, pairs, step
        self.names = names
        self.weighted = weighted
        self.steps = len(orders[0])

    def __add__(self, other):
        assert self.step == other.step and self.orders == other.orders
        return Stream(
            self.n_dp, self.orders, self.pairs + other.pairs, self.names + other.names, self.step, self.weighted
        )

    def key(self):
        return (self.step, self.orders, self.weighted, self.pairs[0][0].shape[2:])

    @property
    def last(self):
        return self.step == self.steps

    @property
    def dims(self):
        count = 1 if self.last else self.n_dp >> (self.step + 1)
        return (count, sum(p[4] for p in self.pairs)) + self.pairs[0][0].shape[2:]

    def bit(self, core, j):
        a, b = self.orders[0][j], self.orders[1][j]
        return a if a == b else jnp.where(core == 0, a, b)

    def read(self, ref, pair, i, dp, core, mine):
        kind, first, size = pair[2:]
        if self.last:
            return ref[0, pl.ds(first, size)]
        bit = (dp >> self.bit(core, self.step)) & 1
        chosen = bit if mine else 1 - bit
        if kind == "kept":
            return ref[2 * i + chosen, pl.ds(first, size)]
        at = chosen << self.bit(core, 0)
        for j in range(1, self.steps):
            at = at + (((i >> (j - 1)) & 1) << self.bit(core, j))
        if kind == "rows":
            return ref[at, pl.ds(first, size)]
        return ref[pl.ds(first, size), at]


class Vectors:
    def __init__(self, total, n_dp):
        self.n_dp, self.total = n_dp, total
        self.masks = [0] + [1 << b for b in range(n_dp.bit_length() - 1)]
        self.swap()

    def swap(self):
        mask = self.masks.pop(0)
        self.received = swap_with(self.total, self.n_dp, (mask, mask))


def tick(pos, task, name, streams, after=(), vectors=None):
    arrays, jobs, outs = [], [], []

    def operand(array):
        for n, known in enumerate(arrays):
            if known is array:
                return n
        arrays.append(array)
        return len(arrays) - 1

    for stream in streams:
        pairs = [(operand(p[0]), operand(p[1])) for p in stream.pairs]
        jobs.append((stream, pairs, len(outs)))
        outs += [pltpu.VMEM(stream.dims, F32)] * (1 if stream.last else 2)
    if vectors is not None:
        pair = (operand(vectors.total), operand(vectors.received))
        outs.append(pltpu.VMEM((VECTORS, D), F32))

    scalars = [pos] + (list(task) if any(stream.weighted for stream in streams) else [])

    def kernel(pos_ref, *refs):
        task_refs, refs = refs[: len(scalars) - 1], refs[len(scalars) - 1 :]
        ins, out_refs = refs[: len(arrays)], refs[len(arrays) :]
        dp, core = pos_ref[0], pos_ref[1]

        def add(stream, pairs, n, mine, i):
            offset = 0
            for pair, (held, received) in zip(stream.pairs, pairs):
                a = stream.read(ins[held], pair, i, dp, core, mine)
                b = stream.read(ins[received], pair, i, dp, core, mine)
                total = a + b
                if stream.weighted:
                    total = total * task_weight(*task_refs, total.shape[-1])
                out_refs[n + mine][i, pl.ds(offset, pair[4])] = total
                offset += pair[4]

        for stream, pairs, n in jobs:
            for mine in (0,) if stream.last else (0, 1):
                act = functools.partial(add, stream, pairs, n, mine)
                if stream.dims[0] <= 8:
                    for i in range(stream.dims[0]):
                        act(i)
                else:
                    pl.loop(0, stream.dims[0])(act)
        if vectors is not None:
            out_refs[-1][...] = ins[pair[0]][...] + ins[pair[1]][...]

    return small_call(kernel, name, scalars, arrays, outs, after)


class Transfers:
    def __init__(self, pos, task, n_dp):
        self.pos, self.task, self.n_dp, self.ticks = pos, task, n_dp, 0
        self.streams, self.vectors, self.mine = [], None, []

    def other_core(self, value):
        return swap_with(value, self.n_dp, (0, 0))

    def order(self, pattern):
        return tuple(b for p in pattern for b in ([p] if p < 3 else range(3, self.n_dp.bit_length() - 1)))

    def begin(self, kind, own, other, names, plan, weighted):
        rows = D // self.n_dp
        blocks, width = len(names), own.shape[-1]
        dims = (self.n_dp, blocks, rows, width) if kind == "rows" else (blocks, self.n_dp, rows, width)
        own, received = own.reshape(dims), self.other_core(other.reshape(dims))
        first = 0
        for count, patterns in plan:
            orders = tuple(self.order(p) for p in patterns)
            pair = (own, received, kind, first, count)
            self.streams.append(Stream(self.n_dp, orders, [pair], names[first : first + count], weighted=weighted))
            first += count

    def named(self, name):
        return next((s for s in self.streams if name in s.names), None)

    def tick(self, wanted, after):
        vectors = None
        streams = []
        for name in wanted:
            if name == "vectors":
                vectors = self.vectors
                continue
            stream = self.named(name)
            if stream is not None and stream not in streams:
                streams.append(stream)
        merged = {}
        for stream in streams:
            self.streams.remove(stream)
            key = stream.key()
            merged[key] = merged[key] + stream if key in merged else stream
        streams = list(merged.values())
        self.ticks += 1
        sent = tick(self.pos, self.task, "tick_%d" % self.ticks, streams, after, vectors)
        n = 0
        for stream in streams:
            if stream.last:
                self.mine.append((sent[n], self.other_core(sent[n]), stream.names))
                n += 1
                continue
            masks = tuple(1 << order[stream.step] for order in stream.orders)
            received = swap_with(sent[n], self.n_dp, masks)
            pair = (sent[n + 1], received, "kept", 0, stream.dims[1])
            self.streams.append(Stream(self.n_dp, stream.orders, [pair], stream.names, stream.step + 1))
            n += 2
        if vectors is not None:
            vectors.total = sent[-1]
            if vectors.masks:
                vectors.swap()
            else:
                vectors.received = None
        return [sent[0]]

    def finish(self, after):
        while self.streams or self.vectors.received is not None:
            wanted = [s.names[0] for s in self.streams]
            after = self.tick(wanted + ["vectors"] * (self.vectors.received is not None), after)
        return after


def place_kernel(pos_ref, *refs, places, blocks, halves):
    core = pos_ref[1]
    for source, b, n, row, cols in places:
        mine, theirs = refs[2 * source][0, b], refs[2 * source + 1][0, b]
        rows, width = mine.shape
        out = refs[len(refs) - blocks + n]
        out[row : row + rows, cols[0] : cols[0] + width] = jnp.where(core == 0, mine, theirs)
        out[row : row + rows, cols[1] : cols[1] + width] = jnp.where(core == 0, theirs, mine)
    vectors, singles, wide = refs[2 * halves], refs[2 * halves + 1 : 2 * halves + 9], refs[2 * halves + 9]
    rows, per = singles[0].shape[0], wide.shape[0]
    turned = pltpu.roll(vectors[:8], lax.rem(D - pos_ref[0] * rows, D), 1)
    for n, single in enumerate(singles):
        single[...] = turned[n, :rows]
    at = pos_ref[0] * per
    turned = pltpu.roll(vectors[8:], lax.rem(D - lax.rem(at, D), D), 1)
    line = lax.broadcasted_iota(jnp.int32, turned.shape, 0) == at // D
    wide[...] = jnp.sum(jnp.where(line, turned, 0.0), axis=0)[:per]


def place(pos, sums, outs, after, vectors):
    places = [(k, b) + name for k, (_, _, names) in enumerate(sums) for b, name in enumerate(names)]
    rows = D // vectors.n_dp
    more = [(rows,)] * 8 + [(rows * FF // D,)]
    return small_call(
        functools.partial(place_kernel, places=places, blocks=len(outs), halves=len(sums)),
        "place",
        [pos],
        [x for mine, theirs, _ in sums for x in (mine, theirs)] + [vectors.total],
        [shape(dims, F32) for dims in more + outs],
        after,
    )


def count_rounds(labels, n_dp, window):
    hits = (labels[:, None] == jnp.arange(NTASK, dtype=jnp.int32)[None, :]).astype(jnp.int32)
    counts = [jnp.sum(hits, axis=0) * (2 * window)]
    bit = 1
    while bit < n_dp:
        masks = [bit] if 2 * bit >= n_dp else [bit, 2 * bit, 3 * bit]
        counts.append(counts[-1] + sum(swap_with(counts[-1], n_dp, (m, m)) for m in masks))
        bit *= 4
    return counts[1:]


def per_device(tokens, segments, labels, cotangent, w_qkv, b_query, b_value, w_out, b_out, gamma_one, beta_one, gamma_two, beta_two, w_up, b_up, w_down, b_down, *, n_dp):
    windows, window, width = tokens.shape
    pos = jnp.stack([lax.axis_index("dp"), lax.axis_index("group")]).astype(jnp.int32)
    x = tokens.reshape(window, width)
    cot = cotangent.reshape(window, width)
    counts = count_rounds(labels, n_dp, window)

    rows = D // n_dp
    moving = Transfers(pos, (counts[-1], labels), n_dp)

    down_names = [(0, b * rows, (0, HALF)) for b in range(4)]
    up_names = [(1, 0, (b * D, b * D + HALF)) for b in range(4)]
    first_names, last_names = [], []
    for b in range(3):
        for at in (b * D, b * D + LANES):
            first_names.append((2, 0, (at, at + 2 * LANES)))
        first_names.append((3, 0, (2 * b * LANES, (2 * b + 1) * LANES)))
        last_names.append((2, 0, (b * D + 4 * LANES, b * D + 5 * LANES)))
    chunks = {"D": down_names, "U": up_names[:3], "W": up_names[3:], "F": first_names, "L": last_names}

    def begin(chunk, kind, own, other):
        moving.begin(kind, own, other, chunks[chunk], PLAN[chunk], chunk == "D")

    proj, in_one, att, probs, mid, in_two = forward(
        x, segments, gamma_one, beta_one, w_qkv, b_query, b_value, w_out, b_out, gamma_two, beta_two
    )
    act, slope, own, other = up(pos, in_two, cot, w_up, b_up, counts[:1])
    begin("D", "rows", own, other)
    after = []
    for step in SCHEDULE:
        if step == "hidden":
            gp, own, other, sum_up, go, sum_down = hidden(
                pos, counts[-1], labels, cot, in_two, slope, w_down, 0, 3, after
            )
            begin("U", "blocks", own, other)
            after = [gp]
        elif step == "hidden last":
            gp_last, own, other, sum_up_last = hidden(
                pos, counts[-1], labels, go, in_two, slope, w_down, 3, 1, after
            )
            begin("W", "blocks", own, other)
            after = [gp_last]
        elif step == "middle":
            gm, gb, ga, sums_mid = middle_back(go, mid, gamma_two, gp, gp_last, w_up, w_out, after)
            after = [ga]
        elif step == "attend first":
            first = attend_back(proj, ga, probs, 0, 4, after)
            after = [first]
        elif step == "first heads":
            own, other = first_heads(pos, in_one, first, att, gb, after)
            begin("F", "blocks", own, other)
            after = [own]
        elif step == "attend last":
            last = attend_back(proj, ga, probs, 4, 2, after)
            after = [last]
        elif step == "last heads":
            own, other = last_heads(pos, in_one, last, after)
            begin("L", "blocks", own, other)
            after = [own]
        elif step == "input":
            grad_tokens, vectors = input_back(
                x, gm, gamma_one, first, last, w_qkv, sums_mid, sum_down, sum_up, sum_up_last, after
            )
            moving.vectors = Vectors(vectors, n_dp)
            after = [grad_tokens]
        elif step == "mix":
            mixed = mix(mid, act, w_down, b_down, after)
            after = [mixed]
        else:
            wanted = []
            for item in step:
                if item == "V":
                    wanted.append("vectors")
                else:
                    first_block = sum(count for count, _ in PLAN[item[0]][: int(item[1])])
                    wanted.append(chunks[item[0]][first_block])
            after = moving.tick(wanted, after)
    after = moving.finish(after)
    *singles, grad_b_up, grad_down, grad_up, grad_qkv, grad_out = place(
        pos, moving.mine, [(4 * rows, D), (rows, FF), (rows, 3 * D), (rows, D)], after, moving.vectors
    )
    query, value, gain_one, shift_one, gain_two, shift_two, out, bias_down = singles
    return (
        mixed.reshape(tokens.shape),
        grad_tokens.reshape(tokens.shape),
        grad_qkv,
        query,
        value,
        grad_out,
        out,
        gain_one,
        shift_one,
        gain_two,
        shift_two,
        grad_up,
        grad_b_up,
        grad_down,
        bias_down,
        counts[-1],
    )


def solution(mesh):
    split = P(("dp", "group"), None, None)
    return jax.shard_map(
        functools.partial(per_device, n_dp=mesh.shape["dp"]),
        mesh=mesh,
        in_specs=(split, P(("dp", "group"), None), P(("dp", "group")), split) + (P(),) * 13,
        out_specs=(split, split, P("dp", None), P("dp"), P("dp"), P("dp", None))
        + (P("dp"),) * 5
        + (P("dp", None), P("dp"), P("dp", None), P("dp"), P()),
        check_vma=False,
    )
```

```python
import functools
import math

import jax
import jax.numpy as jnp
from jax import lax
from jax.experimental import pallas as pl
from jax.experimental.pallas import tpu as pltpu
from jax.sharding import PartitionSpec as P

F32 = jnp.float32
BF = jnp.bfloat16
D = 768
HEADS = 12
HEAD = 64
PAIR = 2 * HEAD
LANES = 128
FF = 3072
NTASK = 3
VECTORS = 16
QB = 256
EPISODE = 256
QUERIES = 128
STAGGER = 2
HALF = D // 2
AXES = ("dp", "group")
NN = (((1,), (0,)), ((), ()))
NT = (((1,), (1,)), ((), ()))
TN = (((0,), (0,)), ((), ()))
PLAN = {'D': [(3, ((1, 2, 3, 0), (0, 2, 3, 1))), (1, ((2, 3, 1, 0), (2, 3, 0, 1)))], 'U': [(3, ((0, 1, 2, 3), (1, 0, 2, 3))), (1, ((2, 0, 1, 3), (2, 1, 0, 3)))], 'F': [(3, ((1, 2, 0, 3), (0, 2, 1, 3))), (6, ((1, 0, 2, 3), (0, 1, 2, 3)))], 'L': [(3, ((0, 1, 2, 3), (1, 0, 2, 3)))]}
SCHEDULE = ['hidden', ('D0', 'D1'), 'middle', ('U0', 'U1', 'D1'), 'attend first', ('D0',), 'first heads', ('D1',), ('U0',), 'attend last', ('D1', 'U1', 'F0', 'F1'), 'last heads', ('U0',), ('D0',), 'input', ('U1', 'F0', 'L0', 'D1'), ('V',), ('U0', 'U1'), ('F1',), 'mix', ('D0', 'U1', 'F0', 'V'), ('U0', 'F1'), ('D0', 'F0', 'V'), ('L0',), ('L0', 'V', 'F0', 'F1'), ('V', 'L0'), ('F1', 'L0')]
SMALL_FLOPS = 1000000000
SMALL_LIMIT = 20 * 2**20
BIG = 1 << 40
COST = {'first_heads_grad': 0, 'last_heads_grad': 0, 'attend_back_first': 20, 'attend_back_last': 20, 'norm_one_back': 3, 'mix': 20, 'norm_two_back': 3}
FREE = {"hidden_grad": [6], "norm_two_back": [0, 3], "first_heads_grad": [1, 2], "last_heads_grad": [1, 2], "norm_one_back": [3, 4, 5], "mix": [2]}
OUT = {"up_and_down_grad": [2], "hidden_grad": [0, 1], "attend_back_first": [0], "attend_back_last": [0]}
VMEM_LIMIT = 34 * 2**20
SCALE = 1
FLOPS = 4e9


def dot(a, b, dims=NN):
    return lax.dot_general(a, b, dims, preferred_element_type=F32)


def in_hbm(x):
    return pltpu.with_memory_space_constraint(x, pltpu.HBM)


def call(kernel, name, grid, in_specs, out_specs, out_shape, scratch=(), prefetch=0, us=3, after=0, free=(), limit=None):
    in_specs = list(in_specs) + [pl.BlockSpec(memory_space=pl.ANY)] * after
    body = kernel
    if after:
        start = prefetch + len(in_specs) - after

        def body(*refs):
            kernel(*refs[:start], *refs[start + after :])

    single = not isinstance(out_shape, list)
    made = [(s if n in OUT.get(name, ()) else pltpu.HBM(s.shape, s.dtype)) if isinstance(s, jax.ShapeDtypeStruct) else s for n, s in enumerate([out_shape] if single else out_shape)]
    run = pl.pallas_call(
        body,
        grid_spec=pltpu.PrefetchScalarGridSpec(
            num_scalar_prefetch=prefetch,
            grid=grid,
            in_specs=in_specs,
            out_specs=[out_specs] if single else out_specs,
            scratch_shapes=list(scratch),
        ),
        out_shape=made,
        compiler_params=pltpu.CompilerParams(vmem_limit_bytes=limit or VMEM_LIMIT),
        cost_estimate=pl.CostEstimate(flops=int(COST.get(name, us) * FLOPS), bytes_accessed=int(us * SCALE), transcendentals=0),
        name=name,
    )

    def apply(*args):
        last = len(args) - after
        table = FREE.get(name, free)
        args = [x if n < prefetch or n >= last or n in table else in_hbm(x) for n, x in enumerate(args)]
        out = run(*args)
        return out[0] if single else out

    return apply


def shape(dims, dtype):
    return jax.ShapeDtypeStruct(dims, dtype)


def whole(*dims):
    return pl.BlockSpec(dims, lambda *_: (0,) * len(dims))


SMEM = pl.BlockSpec(memory_space=pltpu.SMEM)


def unit(x):
    centered = x - jnp.mean(x, axis=-1, keepdims=True)
    inv = lax.rsqrt(jnp.mean(centered * centered, axis=-1, keepdims=True) + 1e-05)
    return centered * inv, inv


def norm_back(e, u, inv, gain):
    scaled = e * gain
    return inv * (
        scaled
        - jnp.mean(scaled, axis=-1, keepdims=True)
        - u * jnp.mean(scaled * u, axis=-1, keepdims=True)
    )


def rows_of(ref):
    return range(0, ref.shape[0], QB)


def column_sum(x):
    return jnp.sum(x, axis=0, keepdims=True)


def bands(t):
    return [(q, max(0, q - EPISODE), min(q + QUERIES, EPISODE + QUERIES)) for q in range(0, t, QUERIES)]


def head_pair(x):
    lane = lax.broadcasted_iota(jnp.int32, (1, PAIR), 1)
    zero = jnp.zeros_like(x)
    return jnp.concatenate([jnp.where(lane < HEAD, x, zero), jnp.where(lane < HEAD, zero, x)], axis=0)


def heads_side_by_side(x):
    return jnp.concatenate([x[:HEAD, :QUERIES], x[HEAD:, QUERIES:]], axis=0).T


def staggered(units, stages):
    waiting = [{} for _ in stages]
    lags = [0, STAGGER, STAGGER + 1]
    for n in range(len(units) + lags[-1]):
        for k, stage in enumerate(stages):
            m = n - lags[k]
            if 0 <= m < len(units):
                given = () if k == 0 else (waiting[k - 1].pop(m),)
                waiting[k][m] = stage(*units[m], *given)


def forward_kernel(x_ref, seg_ref, g1_ref, s1_ref, wq_ref, wk_ref, wv_ref, bq_ref, bv_ref, wo_ref, bo_ref, g2_ref, s2_ref, proj_ref, in_one_ref, att_ref, p_ref, mid_ref, in_two_ref, bias_ref, turned_ref, acc_ref):
    g = pl.program_id(0)
    t = x_ref.shape[0]
    blocks = bands(t)

    @pl.when(g == 0)
    def _():
        for r in rows_of(x_ref):
            u, _ = unit(x_ref[r : r + QB].astype(F32))
            in_one_ref[r : r + QB] = (u * g1_ref[...] + s1_ref[...]).astype(BF)
            acc_ref[r : r + QB] = x_ref[r : r + QB].astype(F32) + bo_ref[...]
        hot = (seg_ref[...] == lax.broadcasted_iota(jnp.int32, (8, t), 0)).astype(BF)
        for i, (q0, k0, n) in enumerate(blocks):
            same = dot(hot[:, k0 : k0 + n], hot[:, q0 : q0 + QUERIES], TN)
            col = k0 + lax.broadcasted_iota(jnp.int32, (n, QUERIES), 0)
            row = q0 + lax.broadcasted_iota(jnp.int32, (n, QUERIES), 1)
            bias_ref[i, :n] = jnp.where((same > 0.5) & (col <= row), 0.0, -1e30).astype(F32)

    width = wq_ref.shape[1]
    here = pl.ds(pl.multiple_of(g * width, width), width)
    for r in range(0, t, 2 * QB):
        rows = in_one_ref[r : r + 2 * QB]
        proj_ref[0, r : r + 2 * QB] = ((dot(rows, wq_ref[...]) + bq_ref[here]) * HEAD**-0.5).astype(BF)
        proj_ref[1, r : r + 2 * QB] = dot(rows, wk_ref[...]).astype(BF)
        proj_ref[2, r : r + 2 * QB] = (dot(rows, wv_ref[...]) + bv_ref[here]).astype(BF)
    pairs = width // PAIR
    for w in range(pairs):
        turned_ref[w] = proj_ref[2, :, w * PAIR : (w + 1) * PAIR].T

    def scores(w, i):
        q0, k0, n = blocks[i]
        cols = slice(w * PAIR, (w + 1) * PAIR)
        return dot(proj_ref[1, k0 : k0 + n, cols], head_pair(proj_ref[0, q0 : q0 + QUERIES, cols]), NT)

    def softmax(w, i, values):
        n = blocks[i][2]
        parts = []
        for a in range(2):
            part = values[:, a * QUERIES : (a + 1) * QUERIES] + bias_ref[i, :n]
            e = jnp.exp(part - jnp.max(part, axis=0, keepdims=True))
            probs = (e * (1.0 / jnp.sum(e, axis=0, keepdims=True))).astype(BF)
            p_ref[w, i, :n, a * QUERIES : (a + 1) * QUERIES] = probs
            parts.append(probs)
        return jnp.concatenate(parts, axis=1)

    def attend(w, i, probs):
        q0, k0, n = blocks[i]
        out = dot(turned_ref[w, :, k0 : k0 + n], probs)
        att_ref[q0 : q0 + QUERIES, w * PAIR : (w + 1) * PAIR] = heads_side_by_side(out).astype(BF)

    units = [(w, i) for w in range(pairs) for i in range(len(blocks))]
    staggered(units, (scores, softmax, attend))

    acc_ref[...] += dot(att_ref[...], wo_ref[...])

    @pl.when(g == pl.num_programs(0) - 1)
    def _():
        for r in rows_of(x_ref):
            mid = acc_ref[r : r + QB]
            mid_ref[r : r + QB] = mid
            u, _ = unit(mid)
            in_two_ref[r : r + QB] = (u * g2_ref[...] + s2_ref[...]).astype(BF)


def forward(x, seg, gain_one, shift_one, w_qkv, b_query, b_value, w_out, b_out, gain_two, shift_two):
    t = x.shape[0]
    width = 2 * PAIR
    steps = D // width
    count = t // QUERIES
    keys = EPISODE + QUERIES

    def weights(part):
        return pl.BlockSpec((D, width), lambda g: (0, part * steps + g))

    return call(
        forward_kernel,
        "forward",
        (steps,),
        [whole(t, D), whole(1, t), whole(D), whole(D), weights(0), weights(1), weights(2), whole(D), whole(D)]
        + [pl.BlockSpec((width, D), lambda g: (g, 0)), whole(D), whole(D), whole(D)],
        [
            pl.BlockSpec((3, t, width), lambda g: (0, 0, g)),
            whole(t, D),
            pl.BlockSpec((t, width), lambda g: (0, g)),
            pl.BlockSpec((2, count, keys, 2 * QUERIES), lambda g: (g, 0, 0, 0)),
            whole(t, D),
            whole(t, D),
        ],
        [
            shape((3, t, D), BF),
            shape((t, D), BF),
            shape((t, D), BF),
            shape((HEADS // 2, count, keys, 2 * QUERIES), BF),
            shape((t, D), F32),
            shape((t, D), BF),
        ],
        [
            pltpu.VMEM((count, keys, QUERIES), F32),
            pltpu.VMEM((2, PAIR, t), BF),
            pltpu.VMEM((t, D), F32),
        ],
        us=24,
        limit=60 * 2**20,
    )(x, seg, gain_one, shift_one, w_qkv, w_qkv, w_qkv, b_query, b_value, w_out, b_out, gain_two, shift_two)


def gelu_both(v):
    cdf = 0.5 * (1.0 + lax.erf(v * (2.0**-0.5)))
    pdf = jnp.exp(-0.5 * v * v) * (1.0 / math.sqrt(2 * math.pi))
    return v * cdf, cdf + v * pdf


def own_first(core, x):
    half = x.shape[1] // 2
    return jnp.where(core == 0, x, jnp.concatenate([x[:, half:], x[:, :half]], axis=1))


def task_weight(counts_ref, label_ref, width):
    total = (counts_ref[0] + counts_ref[1] + counts_ref[2]).astype(F32)
    here = (NTASK * counts_ref[label_ref[0]]).astype(F32)
    return jnp.full((1, width), total, F32) / jnp.full((1, width), here, F32)


def up_kernel(pos_ref, in_ref, cot_ref, w_ref, b_ref, act_ref, slope_ref, own_ref, other_ref, turned):
    @pl.when(pl.program_id(0) == 0)
    def _():
        turned[...] = own_first(pos_ref[1], cot_ref[...])

    bias = b_ref[pl.ds(pl.multiple_of(pl.program_id(0) * D, D), D)]
    rows = QB // 2
    starts = list(range(0, in_ref.shape[0], rows))
    pre = None
    for r in starts + [None]:
        ready, pre = pre, None if r is None else dot(in_ref[r : r + rows], w_ref[...]) + bias
        if ready is not None:
            act, slope = gelu_both(ready)
            act_ref[last : last + rows] = act.astype(BF)
            slope_ref[last : last + rows] = slope.astype(BF)
        last = r
    grad = dot(act_ref[...], turned[...], TN)
    own_ref[...] = grad[:, :HALF]
    other_ref[...] = grad[:, HALF:]


def up(pos, in_two, cot, w_up, b_up, after=()):
    t = in_two.shape[0]
    cols = pl.BlockSpec((t, D), lambda j, *_: (0, j))
    half = pl.BlockSpec((D, HALF), lambda j, *_: (j, 0))
    return call(
        up_kernel,
        "up_and_down_grad",
        (FF // D,),
        [
            whole(t, D),
            whole(t, D),
            pl.BlockSpec((D, D), lambda j, *_: (0, j)),
            whole(FF),
        ],
        [cols, cols, half, half],
        [shape((t, FF), BF)] * 2 + [shape((FF, HALF), F32)] * 2,
        [pltpu.VMEM((t, D), BF)],
        prefetch=1,
        us=16,
        after=len(after),
    )(pos, in_two, cot, w_up, b_up, *after)


def hidden_kernel(pos_ref, counts_ref, label_ref, cot_ref, in_ref, slope_ref, w_ref, gp_ref, go_ref, own_ref, other_ref, sum_ref, down_ref):
    @pl.when(pl.program_id(0) == 0)
    def _():
        go = (cot_ref[...].astype(F32) * task_weight(counts_ref, label_ref, D)).astype(BF)
        go_ref[...] = go
        down_ref[...] = column_sum(go.astype(F32))

    grad = None
    for r in list(rows_of(go_ref)) + [None]:
        ready, grad = grad, None if r is None else dot(go_ref[r : r + QB], w_ref[...], NT)
        if ready is not None:
            gp_ref[last : last + QB] = (ready * slope_ref[last : last + QB].astype(F32)).astype(BF)
        last = r
    sum_ref[0] = column_sum(gp_ref[...].astype(F32))
    grad = dot(in_ref[...], own_first(pos_ref[1], gp_ref[...]), TN)
    own_ref[0] = grad[:, :HALF]
    other_ref[0] = grad[:, HALF:]


def block_half():
    return pl.BlockSpec((1, D, HALF), lambda j, *_: (j, 0, 0))


def hidden(pos, counts, labels, cot, in_two, slope, w_down):
    t = in_two.shape[0]
    cols = pl.BlockSpec((t, D), lambda j, *_: (0, j))
    return call(
        hidden_kernel,
        "hidden_grad",
        (FF // D,),
        [whole(t, D), whole(t, D), cols, pl.BlockSpec((D, D), lambda j, *_: (j, 0))],
        [
            cols,
            whole(t, D),
            block_half(),
            block_half(),
            pl.BlockSpec((1, 1, D), lambda j, *_: (j, 0, 0)),
            whole(1, D),
        ],
        [shape((t, FF), BF), shape((t, D), BF)]
        + [shape((FF // D, D, HALF), F32)] * 2
        + [shape((FF // D, 1, D), F32), shape((1, D), F32)],
        prefetch=3,
        us=14,
    )(pos, counts, labels, cot, in_two, slope, w_down)


def add_sums(ref, first, sums):
    for n, value in enumerate(sums):

        @pl.when(first)
        def _():
            ref[n : n + 1] = value

        @pl.when(jnp.logical_not(first))
        def _():
            ref[n : n + 1] += value


def middle_kernel(go_ref, mid_ref, g_ref, gp_ref, wu_ref, wo_ref, gm_ref, gb_ref, ga_ref, sums_ref):
    starts = rows_of(gm_ref)
    following = dot(gp_ref[:QB], wu_ref[...], NT)
    sums = [0.0, 0.0, 0.0]
    for r in starts:
        e = following
        if r + QB < gm_ref.shape[0]:
            following = dot(gp_ref[r + QB : r + 2 * QB], wu_ref[...], NT)
        u, inv = unit(mid_ref[r : r + QB])
        gm = go_ref[r : r + QB].astype(F32) + norm_back(e, u, inv, g_ref[...])
        gm_ref[r : r + QB] = gm
        gb = gm.astype(BF)
        gb_ref[r : r + QB] = gb
        ga_ref[r : r + QB] = dot(gb, wo_ref[...], NT).astype(BF)
        parts = (column_sum(e * u), column_sum(e), column_sum(gb.astype(F32)))
        sums = [total + part for total, part in zip(sums, parts)]
    add_sums(sums_ref, pl.program_id(0) == 0, sums)


def middle_back(go, mid, gain, gp, w_up, w_out, after=()):
    t = go.shape[0]
    rows = 2 * QB
    row = pl.BlockSpec((rows, D), lambda i: (i, 0))
    return call(
        middle_kernel,
        "norm_two_back",
        (t // rows,),
        [row, row, whole(D), pl.BlockSpec((rows, FF), lambda i: (i, 0)), whole(D, FF), whole(D, D)],
        [row, row, row, whole(3, D)],
        [shape((t, D), F32), shape((t, D), BF), shape((t, D), BF), shape((3, D), F32)],
        us=16,
        after=len(after),
    )(go, mid, gain, gp, w_up, w_out, *after)


def attend_back_kernel(q_ref, k_ref, v_ref, ga_ref, p_ref, d_ref, dk_ref, dv_ref, turned_ref):
    t = q_ref.shape[1]
    blocks = bands(t)

    @pl.loop(0, q_ref.shape[2] // PAIR)
    def _(w):
        cols = pl.ds(pl.multiple_of(w * PAIR, PAIR), PAIR)
        turned_ref[...] = k_ref[0, :, cols].T

        def grad_probs(i):
            q0, k0, n = blocks[i]
            return dot(v_ref[0, k0 : k0 + n, cols], head_pair(ga_ref[q0 : q0 + QUERIES, cols]), NT)

        def grad_scores(i, values):
            probs = p_ref[w, i, : blocks[i][2]].astype(F32)
            prod = probs * values
            return (prod - probs * jnp.sum(prod, axis=0, keepdims=True)).astype(BF)

        def rest(i, ds):
            q0, k0, n = blocks[i]
            dq = heads_side_by_side(dot(turned_ref[:, k0 : k0 + n], ds))
            d_ref[0, q0 : q0 + QUERIES, cols] = dq.astype(BF) * jnp.asarray(HEAD**-0.5, BF)
            known = n - QUERIES if i else 0
            done = blocks[i + 1][1] if i + 1 < len(blocks) else t
            dk = dot(ds, head_pair(q_ref[0, q0 : q0 + QUERIES, cols]))
            dv = dot(p_ref[w, i, :n], head_pair(ga_ref[q0 : q0 + QUERIES, cols]))
            for part, ref, value in ((1, dk_ref, dk), (2, dv_ref, dv)):
                if known:
                    ref[k0 : k0 + known] += value[:known]
                ref[k0 + known : k0 + n] = value[known:]
                if done > k0:
                    d_ref[part, k0:done, cols] = ref[k0:done].astype(BF)

        staggered([(i,) for i in range(len(blocks))], (grad_probs, grad_scores, rest))


def attend_back(proj, ga, probs, first, pairs, after=()):
    t = proj.shape[1]
    width = 2 * PAIR
    start = first // 2

    def block(part):
        return pl.BlockSpec((1, t, width), lambda h: (part, 0, start + h))

    return call(
        attend_back_kernel,
        "attend_back_last" if first else "attend_back_first",
        (pairs // 2,),
        [
            block(0),
            block(1),
            block(2),
            pl.BlockSpec((t, width), lambda h: (0, start + h)),
            pl.BlockSpec((2,) + probs.shape[1:], lambda h: (start + h, 0, 0, 0)),
        ],
        pl.BlockSpec((3, t, width), lambda h: (0, 0, h)),
        shape((3, t, pairs * PAIR), BF),
        [pltpu.VMEM((t, PAIR), F32)] * 2 + [pltpu.VMEM((PAIR, t), BF)],
        us=3 * pairs,
        after=len(after),
    )(proj, proj, proj, ga, probs, *after)


def first_heads_kernel(pos_ref, in_ref, d_ref, att_ref, gb_ref, own_ref, other_ref):
    core = pos_ref[1]
    grad = dot(in_ref[...], own_first(core, d_ref[0]), TN)
    grad_out = dot(att_ref[...], own_first(core, gb_ref[...]), TN)
    columns = [grad[:, n * LANES : (n + 1) * LANES] for n in range(4)]
    columns += [grad_out[:, n * LANES : (n + 1) * LANES] for n in range(2)]
    for n, (own, other) in enumerate([(0, 2), (1, 3), (4, 5)]):
        own_ref[n] = columns[own]
        other_ref[n] = columns[other]


def first_heads(pos, in_one, d, att, gb, after=()):
    t = in_one.shape[0]
    block = pl.BlockSpec((3, D, LANES), lambda j, *_: (j, 0, 0))
    return call(
        first_heads_kernel,
        "first_heads_grad",
        (3,),
        [
            whole(t, D),
            pl.BlockSpec((1, t, 4 * LANES), lambda j, *_: (j, 0, 0)),
            whole(t, D),
            pl.BlockSpec((t, 2 * LANES), lambda j, *_: (0, j)),
        ],
        [block, block],
        [shape((9, D, LANES), F32)] * 2,
        prefetch=1,
        us=10,
        after=len(after),
    )(pos, in_one, d, att, gb, *after)


def last_heads_kernel(pos_ref, in_ref, d_ref, own_ref, other_ref):
    turned = jnp.concatenate([own_first(pos_ref[1], d_ref[b]) for b in range(3)], axis=1)
    grad = dot(in_ref[...], turned, TN)
    for b in range(3):
        own_ref[b] = grad[:, 2 * b * LANES : (2 * b + 1) * LANES]
        other_ref[b] = grad[:, (2 * b + 1) * LANES : (2 * b + 2) * LANES]


def last_heads(pos, in_one, d, after=()):
    t = in_one.shape[0]
    return call(
        last_heads_kernel,
        "last_heads_grad",
        (1,),
        [whole(t, D), whole(3, t, 2 * LANES)],
        [whole(3, D, LANES)] * 2,
        [shape((3, D, LANES), F32)] * 2,
        prefetch=1,
        us=5,
        after=len(after),
    )(pos, in_one, d, *after)


def input_kernel(x_ref, gm_ref, g_ref, first_ref, last_ref, w_ref, mid_sums, down_sum, up_sums, gt_ref, sums_ref):
    e = 0.0
    split = first_ref.shape[2]
    for b in range(3):
        e = e + dot(first_ref[b], w_ref[:, b * D : b * D + split], NT)
        e = e + dot(last_ref[b], w_ref[:, b * D + split : (b + 1) * D], NT)
    u, inv = unit(x_ref[...].astype(F32))
    gt_ref[...] = (gm_ref[...] + norm_back(e, u, inv, g_ref[...])).astype(BF)
    start = pl.program_id(0) == 0
    sums = []
    for b in (0, 2):
        pair = [column_sum(ref[b].astype(F32)) for ref in (first_ref, last_ref)]
        sums.append(jnp.concatenate(pair, axis=1))
    add_sums(sums_ref, start, sums + [column_sum(e * u), column_sum(e)])

    @pl.when(start)
    def _():
        sums_ref[4:7] = mid_sums[...]
        sums_ref[7:8] = down_sum[...]
        for b in range(FF // D):
            sums_ref[8 + b : 9 + b] = up_sums[b]
        sums_ref[8 + FF // D :] = jnp.zeros((VECTORS - 8 - FF // D, D), F32)


def input_back(x, gm, gain, first, last, w_qkv, mid_sums, down_sum, up_sums, after=()):
    t = x.shape[0]
    row = pl.BlockSpec((QB, D), lambda i: (i, 0))
    part = lambda d: pl.BlockSpec((3, QB, d.shape[2]), lambda i: (0, i, 0))
    return call(
        input_kernel,
        "norm_one_back",
        (t // QB,),
        [
            row,
            row,
            whole(D),
            part(first),
            part(last),
            whole(D, 3 * D),
            whole(3, D),
            whole(1, D),
            whole(FF // D, 1, D),
        ],
        [row, whole(VECTORS, D)],
        [shape((t, D), BF), shape((VECTORS, D), F32)],
        us=10,
        after=len(after),
    )(x, gm, gain, first, last, w_qkv, mid_sums, down_sum, up_sums, *after)


def mix_kernel(mid_ref, act_ref, w_ref, b_ref, out_ref):
    out_ref[...] = (mid_ref[...] + dot(act_ref[...], w_ref[...]) + b_ref[...]).astype(BF)


def mix(mid, act, w_down, b_down, after=()):
    t = mid.shape[0]
    row = pl.BlockSpec((QB, D), lambda i: (i, 0))
    return call(
        mix_kernel,
        "mix",
        (t // QB,),
        [row, pl.BlockSpec((QB, FF), lambda i: (i, 0)), whole(FF, D), whole(D)],
        row,
        shape((t, D), BF),
        us=10,
        after=len(after),
    )(mid, act, w_down, b_down, *after)


def swap_with(x, n_dp, masks):
    pairs = []
    for dp in range(n_dp):
        for core in range(2):
            mask = masks[core]
            target = (dp ^ mask) * 2 + core if mask else dp * 2 + 1 - core
            pairs.append((dp * 2 + core, target))
    return lax.ppermute(x, AXES, pairs)


def in_vmem(x):
    return pltpu.with_memory_space_constraint(x, pltpu.VMEM)


def small_call(kernel, name, scalars, arrays, outs, after=()):
    n = len(scalars) + len(arrays)

    def body(*refs):
        kernel(*refs[:n], *refs[n + len(after) :])

    vmem = pl.BlockSpec(memory_space=pltpu.VMEM)
    return pl.pallas_call(
        body,
        in_specs=[SMEM] * len(scalars) + [vmem] * len(arrays) + [pl.BlockSpec(memory_space=pl.ANY)] * len(after),
        out_specs=[vmem] * len(outs),
        out_shape=outs,
        compiler_params=pltpu.CompilerParams(vmem_limit_bytes=SMALL_LIMIT),
        cost_estimate=pl.CostEstimate(flops=SMALL_FLOPS, bytes_accessed=1, transcendentals=0),
        name=name,
    )(*scalars, *[in_vmem(x) if x.size < BIG else x for x in arrays], *[in_hbm(a) if a.dtype == BF or a.ndim < 4 else a for a in after])


class Stream:
    def __init__(self, n_dp, orders, pairs, names, step=0, weighted=False):
        self.n_dp, self.orders, self.pairs, self.step = n_dp, orders, pairs, step
        self.names = names
        self.weighted = weighted
        self.steps = len(orders[0])

    def __add__(self, other):
        assert self.step == other.step and self.orders == other.orders
        return Stream(
            self.n_dp, self.orders, self.pairs + other.pairs, self.names + other.names, self.step, self.weighted
        )

    def key(self):
        return (self.step, self.orders, self.weighted, self.pairs[0][0].shape[2:])

    @property
    def last(self):
        return self.step == self.steps

    @property
    def dims(self):
        count = 1 if self.last else self.n_dp >> (self.step + 1)
        return (count, sum(p[4] for p in self.pairs)) + self.pairs[0][0].shape[2:]

    def bit(self, core, j):
        a, b = self.orders[0][j], self.orders[1][j]
        return a if a == b else jnp.where(core == 0, a, b)

    def read(self, ref, pair, i, dp, core, mine):
        kind, first, size = pair[2:]
        if self.last:
            return ref[0, pl.ds(first, size)]
        bit = (dp >> self.bit(core, self.step)) & 1
        chosen = bit if mine else 1 - bit
        if kind == "kept":
            return ref[2 * i + chosen, pl.ds(first, size)]
        at = chosen << self.bit(core, 0)
        for j in range(1, self.steps):
            at = at + (((i >> (j - 1)) & 1) << self.bit(core, j))
        if kind == "rows":
            return ref[at, pl.ds(first, size)]
        return ref[pl.ds(first, size), at]


class Vectors:
    def __init__(self, total, n_dp):
        self.n_dp, self.total = n_dp, total
        self.masks = [0] + [1 << b for b in range(n_dp.bit_length() - 1)]
        self.swap()

    def swap(self):
        mask = self.masks.pop(0)
        self.received = swap_with(self.total, self.n_dp, (mask, mask))


def tick(pos, task, name, streams, after=(), vectors=None):
    arrays, jobs, outs = [], [], []

    def operand(array):
        for n, known in enumerate(arrays):
            if known is array:
                return n
        arrays.append(array)
        return len(arrays) - 1

    for stream in streams:
        pairs = [(operand(p[0]), operand(p[1])) for p in stream.pairs]
        jobs.append((stream, pairs, len(outs)))
        outs += [pltpu.VMEM(stream.dims, F32)] * (1 if stream.last else 2)
    if vectors is not None:
        pair = (operand(vectors.total), operand(vectors.received))
        outs.append(pltpu.VMEM((VECTORS, D), F32))

    scalars = [pos] + (list(task) if any(stream.weighted for stream in streams) else [])

    def kernel(pos_ref, *refs):
        task_refs, refs = refs[: len(scalars) - 1], refs[len(scalars) - 1 :]
        ins, out_refs = refs[: len(arrays)], refs[len(arrays) :]
        dp, core = pos_ref[0], pos_ref[1]

        def add(stream, pairs, n, mine, i):
            offset = 0
            for pair, (held, received) in zip(stream.pairs, pairs):
                a = stream.read(ins[held], pair, i, dp, core, mine)
                b = stream.read(ins[received], pair, i, dp, core, mine)
                total = a + b
                if stream.weighted:
                    total = total * task_weight(*task_refs, total.shape[-1])
                out_refs[n + mine][i, pl.ds(offset, pair[4])] = total
                offset += pair[4]

        for stream, pairs, n in jobs:
            for mine in (0,) if stream.last else (0, 1):
                act = functools.partial(add, stream, pairs, n, mine)
                if stream.dims[0] <= 8:
                    for i in range(stream.dims[0]):
                        act(i)
                else:
                    pl.loop(0, stream.dims[0])(act)
        if vectors is not None:
            out_refs[-1][...] = ins[pair[0]][...] + ins[pair[1]][...]

    return small_call(kernel, name, scalars, arrays, outs, after)


class Transfers:
    def __init__(self, pos, task, n_dp):
        self.pos, self.task, self.n_dp, self.ticks = pos, task, n_dp, 0
        self.streams, self.vectors, self.mine = [], None, []

    def other_core(self, value):
        return swap_with(value, self.n_dp, (0, 0))

    def order(self, pattern):
        return tuple(b for p in pattern for b in ([p] if p < 3 else range(3, self.n_dp.bit_length() - 1)))

    def begin(self, kind, own, other, names, plan, weighted):
        rows = D // self.n_dp
        blocks, width = len(names), own.shape[-1]
        dims = (self.n_dp, blocks, rows, width) if kind == "rows" else (blocks, self.n_dp, rows, width)
        own, received = own.reshape(dims), self.other_core(other.reshape(dims))
        first = 0
        for count, patterns in plan:
            orders = tuple(self.order(p) for p in patterns)
            pair = (own, received, kind, first, count)
            self.streams.append(Stream(self.n_dp, orders, [pair], names[first : first + count], weighted=weighted))
            first += count

    def named(self, name):
        return next((s for s in self.streams if name in s.names), None)

    def tick(self, wanted, after):
        vectors = None
        streams = []
        for name in wanted:
            if name == "vectors":
                vectors = self.vectors
                continue
            stream = self.named(name)
            if stream is not None and stream not in streams:
                streams.append(stream)
        merged = {}
        for stream in streams:
            self.streams.remove(stream)
            key = stream.key()
            merged[key] = merged[key] + stream if key in merged else stream
        streams = list(merged.values())
        self.ticks += 1
        sent = tick(self.pos, self.task, "tick_%d" % self.ticks, streams, after, vectors)
        n = 0
        for stream in streams:
            if stream.last:
                self.mine.append((sent[n], self.other_core(sent[n]), stream.names))
                n += 1
                continue
            masks = tuple(1 << order[stream.step] for order in stream.orders)
            received = swap_with(sent[n], self.n_dp, masks)
            pair = (sent[n + 1], received, "kept", 0, stream.dims[1])
            self.streams.append(Stream(self.n_dp, stream.orders, [pair], stream.names, stream.step + 1))
            n += 2
        if vectors is not None:
            vectors.total = sent[-1]
            if vectors.masks:
                vectors.swap()
            else:
                vectors.received = None
        return [sent[0]]

    def finish(self, after):
        while self.streams or self.vectors.received is not None:
            wanted = [s.names[0] for s in self.streams]
            after = self.tick(wanted + ["vectors"] * (self.vectors.received is not None), after)
        return after


def place_kernel(pos_ref, *refs, places, blocks, halves):
    core = pos_ref[1]
    for source, b, n, row, cols in places:
        mine, theirs = refs[2 * source][0, b], refs[2 * source + 1][0, b]
        rows, width = mine.shape
        out = refs[len(refs) - blocks + n]
        out[row : row + rows, cols[0] : cols[0] + width] = jnp.where(core == 0, mine, theirs)
        out[row : row + rows, cols[1] : cols[1] + width] = jnp.where(core == 0, theirs, mine)
    vectors, singles, wide = refs[2 * halves], refs[2 * halves + 1 : 2 * halves + 9], refs[2 * halves + 9]
    rows, per = singles[0].shape[0], wide.shape[0]
    turned = pltpu.roll(vectors[:8], lax.rem(D - pos_ref[0] * rows, D), 1)
    for n, single in enumerate(singles):
        single[...] = turned[n, :rows]
    at = pos_ref[0] * per
    turned = pltpu.roll(vectors[8:], lax.rem(D - lax.rem(at, D), D), 1)
    line = lax.broadcasted_iota(jnp.int32, turned.shape, 0) == at // D
    wide[...] = jnp.sum(jnp.where(line, turned, 0.0), axis=0)[:per]


def place(pos, sums, outs, after, vectors):
    places = [(k, b) + name for k, (_, _, names) in enumerate(sums) for b, name in enumerate(names)]
    rows = D // vectors.n_dp
    more = [(rows,)] * 8 + [(rows * FF // D,)]
    return small_call(
        functools.partial(place_kernel, places=places, blocks=len(outs), halves=len(sums)),
        "place",
        [pos],
        [x for mine, theirs, _ in sums for x in (mine, theirs)] + [vectors.total],
        [shape(dims, F32) for dims in more + outs],
        after,
    )


def count_rounds(labels, n_dp, window):
    hits = (labels[:, None] == jnp.arange(NTASK, dtype=jnp.int32)[None, :]).astype(jnp.int32)
    counts = [jnp.sum(hits, axis=0) * (2 * window)]
    bit = 1
    while bit < n_dp:
        masks = [bit] if 2 * bit >= n_dp else [bit, 2 * bit, 3 * bit]
        counts.append(counts[-1] + sum(swap_with(counts[-1], n_dp, (m, m)) for m in masks))
        bit *= 4
    return counts[1:]


def per_device(tokens, segments, labels, cotangent, w_qkv, b_query, b_value, w_out, b_out, gamma_one, beta_one, gamma_two, beta_two, w_up, b_up, w_down, b_down, *, n_dp):
    windows, window, width = tokens.shape
    pos = jnp.stack([lax.axis_index("dp"), lax.axis_index("group")]).astype(jnp.int32)
    x = tokens.reshape(window, width)
    cot = cotangent.reshape(window, width)
    counts = count_rounds(labels, n_dp, window)

    rows = D // n_dp
    moving = Transfers(pos, (counts[-1], labels), n_dp)

    down_names = [(0, b * rows, (0, HALF)) for b in range(4)]
    up_names = [(1, 0, (b * D, b * D + HALF)) for b in range(4)]
    first_names, last_names = [], []
    for b in range(3):
        for at in (b * D, b * D + LANES):
            first_names.append((2, 0, (at, at + 2 * LANES)))
        first_names.append((3, 0, (2 * b * LANES, (2 * b + 1) * LANES)))
        last_names.append((2, 0, (b * D + 4 * LANES, b * D + 5 * LANES)))
    chunks = {"D": down_names, "U": up_names, "F": first_names, "L": last_names}

    def begin(chunk, kind, own, other):
        moving.begin(kind, own, other, chunks[chunk], PLAN[chunk], chunk == "D")

    proj, in_one, att, probs, mid, in_two = forward(
        x, segments, gamma_one, beta_one, w_qkv, b_query, b_value, w_out, b_out, gamma_two, beta_two
    )
    act, slope, own, other = up(pos, in_two, cot, w_up, b_up, counts[:1])
    begin("D", "rows", own, other)
    after = []
    for step in SCHEDULE:
        if step == "hidden":
            gp, go, own, other, sum_up, sum_down = hidden(pos, counts[-1], labels, cot, in_two, slope, w_down)
            begin("U", "blocks", own, other)
            after = [gp]
        elif step == "middle":
            gm, gb, ga, sums_mid = middle_back(go, mid, gamma_two, gp, w_up, w_out, after)
            after = [ga]
        elif step == "attend first":
            first = attend_back(proj, ga, probs, 0, 4, after)
            after = [first]
        elif step == "first heads":
            own, other = first_heads(pos, in_one, first, att, gb, after)
            begin("F", "blocks", own, other)
            after = [own]
        elif step == "attend last":
            last = attend_back(proj, ga, probs, 4, 2, after)
            after = [last]
        elif step == "last heads":
            own, other = last_heads(pos, in_one, last, after)
            begin("L", "blocks", own, other)
            after = [own]
        elif step == "input":
            grad_tokens, vectors = input_back(
                x, gm, gamma_one, first, last, w_qkv, sums_mid, sum_down, sum_up, after
            )
            moving.vectors = Vectors(vectors, n_dp)
            after = [grad_tokens]
        elif step == "mix":
            mixed = mix(mid, act, w_down, b_down, after)
            after = [mixed]
        else:
            wanted = []
            for item in step:
                if item == "V":
                    wanted.append("vectors")
                else:
                    first_block = sum(count for count, _ in PLAN[item[0]][: int(item[1])])
                    wanted.append(chunks[item[0]][first_block])
            after = moving.tick(wanted, after)
    after = moving.finish(after)
    *singles, grad_b_up, grad_down, grad_up, grad_qkv, grad_out = place(
        pos, moving.mine, [(4 * rows, D), (rows, FF), (rows, 3 * D), (rows, D)], after, moving.vectors
    )
    query, value, gain_one, shift_one, gain_two, shift_two, out, bias_down = singles
    return (
        mixed.reshape(tokens.shape),
        grad_tokens.reshape(tokens.shape),
        grad_qkv,
        query,
        value,
        grad_out,
        out,
        gain_one,
        shift_one,
        gain_two,
        shift_two,
        grad_up,
        grad_b_up,
        grad_down,
        bias_down,
        counts[-1],
    )


def solution(mesh):
    split = P(("dp", "group"), None, None)
    return jax.shard_map(
        functools.partial(per_device, n_dp=mesh.shape["dp"]),
        mesh=mesh,
        in_specs=(split, P(("dp", "group"), None), P(("dp", "group")), split) + (P(),) * 13,
        out_specs=(split, split, P("dp", None), P("dp"), P("dp"), P("dp", None))
        + (P("dp"),) * 5
        + (P("dp", None), P("dp"), P("dp", None), P("dp"), P()),
        check_vma=False,
    )
```

```python
import functools
import math

import jax
import jax.numpy as jnp
from jax import lax
from jax.experimental import pallas as pl
from jax.experimental.pallas import tpu as pltpu
from jax.sharding import PartitionSpec as P

F32 = jnp.float32
BF = jnp.bfloat16
D = 768
HEADS = 12
HEAD = 64
PAIR = 2 * HEAD
LANES = 128
FF = 3072
NTASK = 3
VECTORS = 16
QB = 256
EPISODE = 256
QUERIES = 128
STAGGER = 2
HALF = D // 2
AXES = ("dp", "group")
NN = (((1,), (0,)), ((), ()))
NT = (((1,), (1,)), ((), ()))
TN = (((0,), (0,)), ((), ()))
PLAN = {'D': [(3, ((1, 2, 3, 0), (0, 2, 3, 1))), (1, ((2, 3, 1, 0), (2, 3, 0, 1)))],
 'U': [(3, ((0, 1, 2, 3), (1, 0, 2, 3))), (1, ((2, 0, 1, 3), (2, 1, 0, 3)))],
 'F': [(3, ((1, 2, 0, 3), (0, 2, 1, 3))), (6, ((1, 0, 2, 3), (0, 1, 2, 3)))],
 'L': [(3, ((0, 1, 2, 3), (1, 0, 2, 3)))]}
SCHEDULE = ['hidden',
 ('D0', 'D1'),
 'middle',
 ('U0', 'U1', 'D1'),
 'attend first',
 'first heads',
 ('D0',),
 ('D1',),
 ('U0',),
 'attend last',
 ('D1', 'U1', 'F0', 'F1'),
 'last heads',
 ('U0',),
 ('D0',),
 'input',
 ('U1', 'F0', 'L0', 'D1'),
 ('V',),
 ('U0', 'U1'),
 ('F1',),
 'mix',
 ('D0', 'U1', 'F0', 'V'),
 ('U0', 'F1'),
 ('D0', 'F0', 'V'),
 ('L0',),
 ('L0', 'V', 'F0', 'F1'),
 ('V', 'L0'),
 ('F1', 'L0')]
COST = {'first_heads_grad': 0,
 'last_heads_grad': 0,
 'attend_back_first': 20,
 'attend_back_last': 20,
 'norm_one_back': 3,
 'mix': 20,
 'norm_two_back': 3,
 'hidden_grad': 60}
FLOPS = 4e9
TICK_FLOPS = 1000000000
FREE = {'hidden_grad': [6],
 'norm_two_back': [0, 3],
 'first_heads_grad': [1, 2],
 'last_heads_grad': [1, 2],
 'norm_one_back': [3, 4, 5],
 'mix': [2]}
OUT = {'up_and_down_grad': [2], 'hidden_grad': [0, 1], 'attend_back_first': [0], 'attend_back_last': [0]}
VMEM_LIMIT = 34 * 2**20
TICK_LIMIT = 20 * 2**20


def dot(a, b, dims=NN):
    return lax.dot_general(a, b, dims, preferred_element_type=F32)


def in_hbm(x):
    return pltpu.with_memory_space_constraint(x, pltpu.HBM)


def call(kernel, name, grid, in_specs, out_specs, out_shape, scratch=(), prefetch=0, us=3, after=0, limit=None):
    in_specs = list(in_specs) + [pl.BlockSpec(memory_space=pl.ANY)] * after
    body = kernel
    if after:
        start = prefetch + len(in_specs) - after

        def body(*refs):
            kernel(*refs[:start], *refs[start + after :])

    single = not isinstance(out_shape, list)
    made = [(s if n in OUT.get(name, ()) else pltpu.HBM(s.shape, s.dtype)) if isinstance(s, jax.ShapeDtypeStruct) else s for n, s in enumerate([out_shape] if single else out_shape)]
    run = pl.pallas_call(
        body,
        grid_spec=pltpu.PrefetchScalarGridSpec(
            num_scalar_prefetch=prefetch,
            grid=grid,
            in_specs=in_specs,
            out_specs=[out_specs] if single else out_specs,
            scratch_shapes=list(scratch),
        ),
        out_shape=made,
        compiler_params=pltpu.CompilerParams(vmem_limit_bytes=limit or VMEM_LIMIT),
        cost_estimate=pl.CostEstimate(flops=int(COST.get(name, us) * FLOPS), bytes_accessed=us, transcendentals=0),
        name=name,
    )

    def apply(*args):
        last = len(args) - after
        table = FREE.get(name, ())
        args = [x if n < prefetch or n >= last or n in table else in_hbm(x) for n, x in enumerate(args)]
        out = run(*args)
        return out[0] if single else out

    return apply


def shape(dims, dtype):
    return jax.ShapeDtypeStruct(dims, dtype)


def whole(*dims):
    return pl.BlockSpec(dims, lambda *_: (0,) * len(dims))


SMEM = pl.BlockSpec(memory_space=pltpu.SMEM)


def unit(x):
    centered = x - jnp.mean(x, axis=-1, keepdims=True)
    inv = lax.rsqrt(jnp.mean(centered * centered, axis=-1, keepdims=True) + 1e-05)
    return centered * inv, inv


def norm_back(e, u, inv, gain):
    scaled = e * gain
    return inv * (
        scaled
        - jnp.mean(scaled, axis=-1, keepdims=True)
        - u * jnp.mean(scaled * u, axis=-1, keepdims=True)
    )


def rows_of(ref):
    return range(0, ref.shape[0], QB)


def column_sum(x):
    return jnp.sum(x, axis=0, keepdims=True)


def bands(t):
    return [(q, max(0, q - EPISODE), min(q + QUERIES, EPISODE + QUERIES)) for q in range(0, t, QUERIES)]


def head_pair(x):
    lane = lax.broadcasted_iota(jnp.int32, (1, PAIR), 1)
    zero = jnp.zeros_like(x)
    return jnp.concatenate([jnp.where(lane < HEAD, x, zero), jnp.where(lane < HEAD, zero, x)], axis=0)


def heads_side_by_side(x):
    return jnp.concatenate([x[:HEAD, :QUERIES], x[HEAD:, QUERIES:]], axis=0).T


def staggered(units, stages):
    waiting = [{} for _ in stages]
    lags = [0, STAGGER, STAGGER + 1]
    for n in range(len(units) + lags[-1]):
        for k, stage in enumerate(stages):
            m = n - lags[k]
            if 0 <= m < len(units):
                given = () if k == 0 else (waiting[k - 1].pop(m),)
                waiting[k][m] = stage(*units[m], *given)


def forward_kernel(x_ref, seg_ref, g1_ref, s1_ref, wq_ref, wk_ref, wv_ref, bq_ref, bv_ref, wo_ref, bo_ref, g2_ref, s2_ref, proj_ref, in_one_ref, att_ref, p_ref, mid_ref, in_two_ref, bias_ref, turned_ref, acc_ref):
    g = pl.program_id(0)
    t = x_ref.shape[0]
    blocks = bands(t)

    @pl.when(g == 0)
    def _():
        for r in rows_of(x_ref):
            u, _ = unit(x_ref[r : r + QB].astype(F32))
            in_one_ref[r : r + QB] = (u * g1_ref[...] + s1_ref[...]).astype(BF)
            acc_ref[r : r + QB] = x_ref[r : r + QB].astype(F32) + bo_ref[...]
        hot = (seg_ref[...] == lax.broadcasted_iota(jnp.int32, (8, t), 0)).astype(BF)
        for i, (q0, k0, n) in enumerate(blocks):
            same = dot(hot[:, k0 : k0 + n], hot[:, q0 : q0 + QUERIES], TN)
            col = k0 + lax.broadcasted_iota(jnp.int32, (n, QUERIES), 0)
            row = q0 + lax.broadcasted_iota(jnp.int32, (n, QUERIES), 1)
            bias_ref[i, :n] = jnp.where((same > 0.5) & (col <= row), 0.0, -1e30).astype(F32)

    width = wq_ref.shape[1]
    here = pl.ds(pl.multiple_of(g * width, width), width)
    for r in range(0, t, 2 * QB):
        rows = in_one_ref[r : r + 2 * QB]
        proj_ref[0, r : r + 2 * QB] = ((dot(rows, wq_ref[...]) + bq_ref[here]) * HEAD**-0.5).astype(BF)
        proj_ref[1, r : r + 2 * QB] = dot(rows, wk_ref[...]).astype(BF)
        proj_ref[2, r : r + 2 * QB] = (dot(rows, wv_ref[...]) + bv_ref[here]).astype(BF)
    pairs = width // PAIR
    for w in range(pairs):
        turned_ref[w] = proj_ref[2, :, w * PAIR : (w + 1) * PAIR].T

    def scores(w, i):
        q0, k0, n = blocks[i]
        cols = slice(w * PAIR, (w + 1) * PAIR)
        return dot(proj_ref[1, k0 : k0 + n, cols], head_pair(proj_ref[0, q0 : q0 + QUERIES, cols]), NT)

    def softmax(w, i, values):
        n = blocks[i][2]
        parts = []
        for a in range(2):
            part = values[:, a * QUERIES : (a + 1) * QUERIES] + bias_ref[i, :n]
            e = jnp.exp(part - jnp.max(part, axis=0, keepdims=True))
            probs = (e * (1.0 / jnp.sum(e, axis=0, keepdims=True))).astype(BF)
            p_ref[w, i, :n, a * QUERIES : (a + 1) * QUERIES] = probs
            parts.append(probs)
        return jnp.concatenate(parts, axis=1)

    def attend(w, i, probs):
        q0, k0, n = blocks[i]
        out = dot(turned_ref[w, :, k0 : k0 + n], probs)
        att_ref[q0 : q0 + QUERIES, w * PAIR : (w + 1) * PAIR] = heads_side_by_side(out).astype(BF)

    units = [(w, i) for w in range(pairs) for i in range(len(blocks))]
    staggered(units, (scores, softmax, attend))

    acc_ref[...] += dot(att_ref[...], wo_ref[...])

    @pl.when(g == pl.num_programs(0) - 1)
    def _():
        for r in rows_of(x_ref):
            mid = acc_ref[r : r + QB]
            mid_ref[r : r + QB] = mid
            u, _ = unit(mid)
            in_two_ref[r : r + QB] = (u * g2_ref[...] + s2_ref[...]).astype(BF)


def forward(x, seg, gain_one, shift_one, w_qkv, b_query, b_value, w_out, b_out, gain_two, shift_two):
    t = x.shape[0]
    width = 2 * PAIR
    steps = D // width
    count = t // QUERIES
    keys = EPISODE + QUERIES

    def weights(part):
        return pl.BlockSpec((D, width), lambda g: (0, part * steps + g))

    return call(
        forward_kernel,
        "forward",
        (steps,),
        [whole(t, D), whole(1, t), whole(D), whole(D), weights(0), weights(1), weights(2), whole(D), whole(D)]
        + [pl.BlockSpec((width, D), lambda g: (g, 0)), whole(D), whole(D), whole(D)],
        [
            pl.BlockSpec((3, t, width), lambda g: (0, 0, g)),
            whole(t, D),
            pl.BlockSpec((t, width), lambda g: (0, g)),
            pl.BlockSpec((2, count, keys, 2 * QUERIES), lambda g: (g, 0, 0, 0)),
            whole(t, D),
            whole(t, D),
        ],
        [
            shape((3, t, D), BF),
            shape((t, D), BF),
            shape((t, D), BF),
            shape((HEADS // 2, count, keys, 2 * QUERIES), BF),
            shape((t, D), F32),
            shape((t, D), BF),
        ],
        [
            pltpu.VMEM((count, keys, QUERIES), F32),
            pltpu.VMEM((2, PAIR, t), BF),
            pltpu.VMEM((t, D), F32),
        ],
        us=24,
        limit=60 * 2**20,
    )(x, seg, gain_one, shift_one, w_qkv, w_qkv, w_qkv, b_query, b_value, w_out, b_out, gain_two, shift_two)


def gelu_both(v):
    cdf = 0.5 * (1.0 + lax.erf(v * (2.0**-0.5)))
    pdf = jnp.exp(-0.5 * v * v) * (1.0 / math.sqrt(2 * math.pi))
    return v * cdf, cdf + v * pdf


def own_first(core, x):
    half = x.shape[1] // 2
    return jnp.where(core == 0, x, jnp.concatenate([x[:, half:], x[:, :half]], axis=1))


def task_weight(counts_ref, label_ref, width):
    total = (counts_ref[0] + counts_ref[1] + counts_ref[2]).astype(F32)
    here = (NTASK * counts_ref[label_ref[0]]).astype(F32)
    return jnp.full((1, width), total, F32) / jnp.full((1, width), here, F32)


def up_kernel(pos_ref, in_ref, cot_ref, w_ref, b_ref, act_ref, slope_ref, own_ref, other_ref, turned):
    @pl.when(pl.program_id(0) == 0)
    def _():
        turned[...] = own_first(pos_ref[1], cot_ref[...])

    bias = b_ref[pl.ds(pl.multiple_of(pl.program_id(0) * D, D), D)]
    rows = QB // 2
    starts = list(range(0, in_ref.shape[0], rows))
    pre = None
    for r in starts + [None]:
        ready, pre = pre, None if r is None else dot(in_ref[r : r + rows], w_ref[...]) + bias
        if ready is not None:
            act, slope = gelu_both(ready)
            act_ref[last : last + rows] = act.astype(BF)
            slope_ref[last : last + rows] = slope.astype(BF)
        last = r
    grad = dot(act_ref[...], turned[...], TN)
    own_ref[...] = grad[:, :HALF]
    other_ref[...] = grad[:, HALF:]


def up(pos, in_two, cot, w_up, b_up, after=()):
    t = in_two.shape[0]
    cols = pl.BlockSpec((t, D), lambda j, *_: (0, j))
    half = pl.BlockSpec((D, HALF), lambda j, *_: (j, 0))
    return call(
        up_kernel,
        "up_and_down_grad",
        (FF // D,),
        [
            whole(t, D),
            whole(t, D),
            pl.BlockSpec((D, D), lambda j, *_: (0, j)),
            whole(FF),
        ],
        [cols, cols, half, half],
        [shape((t, FF), BF)] * 2 + [shape((FF, HALF), F32)] * 2,
        [pltpu.VMEM((t, D), BF)],
        prefetch=1,
        us=16,
        after=len(after),
    )(pos, in_two, cot, w_up, b_up, *after)


def hidden_kernel(pos_ref, counts_ref, label_ref, cot_ref, in_ref, slope_ref, w_ref, gp_ref, go_ref, own_ref, other_ref, sum_ref, down_ref):
    @pl.when(pl.program_id(0) == 0)
    def _():
        go = (cot_ref[...].astype(F32) * task_weight(counts_ref, label_ref, D)).astype(BF)
        go_ref[...] = go
        down_ref[...] = column_sum(go.astype(F32))

    grad = None
    for r in list(rows_of(go_ref)) + [None]:
        ready, grad = grad, None if r is None else dot(go_ref[r : r + QB], w_ref[...], NT)
        if ready is not None:
            gp_ref[last : last + QB] = (ready * slope_ref[last : last + QB].astype(F32)).astype(BF)
        last = r
    sum_ref[0] = column_sum(gp_ref[...].astype(F32))
    grad = dot(in_ref[...], own_first(pos_ref[1], gp_ref[...]), TN)
    own_ref[0] = grad[:, :HALF]
    other_ref[0] = grad[:, HALF:]


def block_half():
    return pl.BlockSpec((1, D, HALF), lambda j, *_: (j, 0, 0))


def hidden(pos, counts, labels, cot, in_two, slope, w_down):
    t = in_two.shape[0]
    cols = pl.BlockSpec((t, D), lambda j, *_: (0, j))
    return call(
        hidden_kernel,
        "hidden_grad",
        (FF // D,),
        [whole(t, D), whole(t, D), cols, pl.BlockSpec((D, D), lambda j, *_: (j, 0))],
        [
            cols,
            whole(t, D),
            block_half(),
            block_half(),
            pl.BlockSpec((1, 1, D), lambda j, *_: (j, 0, 0)),
            whole(1, D),
        ],
        [shape((t, FF), BF), shape((t, D), BF)]
        + [shape((FF // D, D, HALF), F32)] * 2
        + [shape((FF // D, 1, D), F32), shape((1, D), F32)],
        prefetch=3,
        us=14,
    )(pos, counts, labels, cot, in_two, slope, w_down)


def add_sums(ref, first, sums):
    for n, value in enumerate(sums):

        @pl.when(first)
        def _():
            ref[n : n + 1] = value

        @pl.when(jnp.logical_not(first))
        def _():
            ref[n : n + 1] += value


def middle_kernel(go_ref, mid_ref, g_ref, gp_ref, wu_ref, wo_ref, gm_ref, gb_ref, ga_ref, sums_ref):
    starts = rows_of(gm_ref)
    following = dot(gp_ref[:QB], wu_ref[...], NT)
    sums = [0.0, 0.0, 0.0]
    for r in starts:
        e = following
        if r + QB < gm_ref.shape[0]:
            following = dot(gp_ref[r + QB : r + 2 * QB], wu_ref[...], NT)
        u, inv = unit(mid_ref[r : r + QB])
        gm = go_ref[r : r + QB].astype(F32) + norm_back(e, u, inv, g_ref[...])
        gm_ref[r : r + QB] = gm
        gb = gm.astype(BF)
        gb_ref[r : r + QB] = gb
        ga_ref[r : r + QB] = dot(gb, wo_ref[...], NT).astype(BF)
        parts = (column_sum(e * u), column_sum(e), column_sum(gb.astype(F32)))
        sums = [total + part for total, part in zip(sums, parts)]
    add_sums(sums_ref, pl.program_id(0) == 0, sums)


def middle_back(go, mid, gain, gp, w_up, w_out, after=()):
    t = go.shape[0]
    rows = 2 * QB
    row = pl.BlockSpec((rows, D), lambda i: (i, 0))
    return call(
        middle_kernel,
        "norm_two_back",
        (t // rows,),
        [row, row, whole(D), pl.BlockSpec((rows, FF), lambda i: (i, 0)), whole(D, FF), whole(D, D)],
        [row, row, row, whole(3, D)],
        [shape((t, D), F32), shape((t, D), BF), shape((t, D), BF), shape((3, D), F32)],
        us=16,
        after=len(after),
    )(go, mid, gain, gp, w_up, w_out, *after)


def attend_back_kernel(q_ref, k_ref, v_ref, ga_ref, p_ref, d_ref, dk_ref, dv_ref, turned_ref):
    t = q_ref.shape[1]
    blocks = bands(t)

    @pl.loop(0, q_ref.shape[2] // PAIR)
    def _(w):
        cols = pl.ds(pl.multiple_of(w * PAIR, PAIR), PAIR)
        turned_ref[...] = k_ref[0, :, cols].T

        def grad_probs(i):
            q0, k0, n = blocks[i]
            return dot(v_ref[0, k0 : k0 + n, cols], head_pair(ga_ref[q0 : q0 + QUERIES, cols]), NT)

        def grad_scores(i, values):
            probs = p_ref[w, i, : blocks[i][2]].astype(F32)
            prod = probs * values
            return (prod - probs * jnp.sum(prod, axis=0, keepdims=True)).astype(BF)

        def rest(i, ds):
            q0, k0, n = blocks[i]
            dq = heads_side_by_side(dot(turned_ref[:, k0 : k0 + n], ds))
            d_ref[0, q0 : q0 + QUERIES, cols] = dq.astype(BF) * jnp.asarray(HEAD**-0.5, BF)
            known = n - QUERIES if i else 0
            done = blocks[i + 1][1] if i + 1 < len(blocks) else t
            dk = dot(ds, head_pair(q_ref[0, q0 : q0 + QUERIES, cols]))
            dv = dot(p_ref[w, i, :n], head_pair(ga_ref[q0 : q0 + QUERIES, cols]))
            for part, ref, value in ((1, dk_ref, dk), (2, dv_ref, dv)):
                if known:
                    ref[k0 : k0 + known] += value[:known]
                ref[k0 + known : k0 + n] = value[known:]
                if done > k0:
                    d_ref[part, k0:done, cols] = ref[k0:done].astype(BF)

        staggered([(i,) for i in range(len(blocks))], (grad_probs, grad_scores, rest))


def attend_back(proj, ga, probs, first, pairs, after=()):
    t = proj.shape[1]
    width = 2 * PAIR
    start = first // 2

    def block(part):
        return pl.BlockSpec((1, t, width), lambda h: (part, 0, start + h))

    return call(
        attend_back_kernel,
        "attend_back_last" if first else "attend_back_first",
        (pairs // 2,),
        [
            block(0),
            block(1),
            block(2),
            pl.BlockSpec((t, width), lambda h: (0, start + h)),
            pl.BlockSpec((2,) + probs.shape[1:], lambda h: (start + h, 0, 0, 0)),
        ],
        pl.BlockSpec((3, t, width), lambda h: (0, 0, h)),
        shape((3, t, pairs * PAIR), BF),
        [pltpu.VMEM((t, PAIR), F32)] * 2 + [pltpu.VMEM((PAIR, t), BF)],
        us=3 * pairs,
        after=len(after),
    )(proj, proj, proj, ga, probs, *after)


def first_heads_kernel(pos_ref, in_ref, d_ref, att_ref, gb_ref, own_ref, other_ref):
    core = pos_ref[1]
    grad = dot(in_ref[...], own_first(core, d_ref[0]), TN)
    grad_out = dot(att_ref[...], own_first(core, gb_ref[...]), TN)
    columns = [grad[:, n * LANES : (n + 1) * LANES] for n in range(4)]
    columns += [grad_out[:, n * LANES : (n + 1) * LANES] for n in range(2)]
    for n, (own, other) in enumerate([(0, 2), (1, 3), (4, 5)]):
        own_ref[n] = columns[own]
        other_ref[n] = columns[other]


def first_heads(pos, in_one, d, att, gb, after=()):
    t = in_one.shape[0]
    block = pl.BlockSpec((3, D, LANES), lambda j, *_: (j, 0, 0))
    return call(
        first_heads_kernel,
        "first_heads_grad",
        (3,),
        [
            whole(t, D),
            pl.BlockSpec((1, t, 4 * LANES), lambda j, *_: (j, 0, 0)),
            whole(t, D),
            pl.BlockSpec((t, 2 * LANES), lambda j, *_: (0, j)),
        ],
        [block, block],
        [shape((9, D, LANES), F32)] * 2,
        prefetch=1,
        us=10,
        after=len(after),
    )(pos, in_one, d, att, gb, *after)


def last_heads_kernel(pos_ref, in_ref, d_ref, own_ref, other_ref):
    turned = jnp.concatenate([own_first(pos_ref[1], d_ref[b]) for b in range(3)], axis=1)
    grad = dot(in_ref[...], turned, TN)
    for b in range(3):
        own_ref[b] = grad[:, 2 * b * LANES : (2 * b + 1) * LANES]
        other_ref[b] = grad[:, (2 * b + 1) * LANES : (2 * b + 2) * LANES]


def last_heads(pos, in_one, d, after=()):
    t = in_one.shape[0]
    return call(
        last_heads_kernel,
        "last_heads_grad",
        (1,),
        [whole(t, D), whole(3, t, 2 * LANES)],
        [whole(3, D, LANES)] * 2,
        [shape((3, D, LANES), F32)] * 2,
        prefetch=1,
        us=5,
        after=len(after),
    )(pos, in_one, d, *after)


def input_kernel(x_ref, gm_ref, g_ref, first_ref, last_ref, w_ref, mid_sums, down_sum, up_sums, gt_ref, sums_ref):
    e = 0.0
    split = first_ref.shape[2]
    for b in range(3):
        e = e + dot(first_ref[b], w_ref[:, b * D : b * D + split], NT)
        e = e + dot(last_ref[b], w_ref[:, b * D + split : (b + 1) * D], NT)
    u, inv = unit(x_ref[...].astype(F32))
    gt_ref[...] = (gm_ref[...] + norm_back(e, u, inv, g_ref[...])).astype(BF)
    start = pl.program_id(0) == 0
    sums = []
    for b in (0, 2):
        pair = [column_sum(ref[b].astype(F32)) for ref in (first_ref, last_ref)]
        sums.append(jnp.concatenate(pair, axis=1))
    add_sums(sums_ref, start, sums + [column_sum(e * u), column_sum(e)])

    @pl.when(start)
    def _():
        sums_ref[4:7] = mid_sums[...]
        sums_ref[7:8] = down_sum[...]
        for b in range(FF // D):
            sums_ref[8 + b : 9 + b] = up_sums[b]
        sums_ref[8 + FF // D :] = jnp.zeros((VECTORS - 8 - FF // D, D), F32)


def input_back(x, gm, gain, first, last, w_qkv, mid_sums, down_sum, up_sums, after=()):
    t = x.shape[0]
    row = pl.BlockSpec((QB, D), lambda i: (i, 0))
    part = lambda d: pl.BlockSpec((3, QB, d.shape[2]), lambda i: (0, i, 0))
    return call(
        input_kernel,
        "norm_one_back",
        (t // QB,),
        [
            row,
            row,
            whole(D),
            part(first),
            part(last),
            whole(D, 3 * D),
            whole(3, D),
            whole(1, D),
            whole(FF // D, 1, D),
        ],
        [row, whole(VECTORS, D)],
        [shape((t, D), BF), shape((VECTORS, D), F32)],
        us=10,
        after=len(after),
    )(x, gm, gain, first, last, w_qkv, mid_sums, down_sum, up_sums, *after)


def mix_kernel(mid_ref, act_ref, w_ref, b_ref, out_ref):
    out_ref[...] = (mid_ref[...] + dot(act_ref[...], w_ref[...]) + b_ref[...]).astype(BF)


def mix(mid, act, w_down, b_down, after=()):
    t = mid.shape[0]
    row = pl.BlockSpec((QB, D), lambda i: (i, 0))
    return call(
        mix_kernel,
        "mix",
        (t // QB,),
        [row, pl.BlockSpec((QB, FF), lambda i: (i, 0)), whole(FF, D), whole(D)],
        row,
        shape((t, D), BF),
        us=10,
        after=len(after),
    )(mid, act, w_down, b_down, *after)


def swap_with(x, n_dp, masks):
    pairs = []
    for dp in range(n_dp):
        for core in range(2):
            mask = masks[core]
            target = (dp ^ mask) * 2 + core if mask else dp * 2 + 1 - core
            pairs.append((dp * 2 + core, target))
    return lax.ppermute(x, AXES, pairs)


def in_vmem(x):
    return pltpu.with_memory_space_constraint(x, pltpu.VMEM)


def small_call(kernel, name, scalars, arrays, outs, after=()):
    n = len(scalars) + len(arrays)

    def body(*refs):
        kernel(*refs[:n], *refs[n + len(after) :])

    vmem = pl.BlockSpec(memory_space=pltpu.VMEM)
    return pl.pallas_call(
        body,
        in_specs=[SMEM] * len(scalars) + [vmem] * len(arrays) + [pl.BlockSpec(memory_space=pl.ANY)] * len(after),
        out_specs=[vmem] * len(outs),
        out_shape=outs,
        compiler_params=pltpu.CompilerParams(vmem_limit_bytes=TICK_LIMIT),
        cost_estimate=pl.CostEstimate(flops=TICK_FLOPS, bytes_accessed=1, transcendentals=0),
        name=name,
    )(*scalars, *[in_vmem(x) for x in arrays], *[in_hbm(a) if a.dtype == BF or a.ndim < 4 else a for a in after])


class Stream:
    def __init__(self, n_dp, orders, pairs, names, step=0, weighted=False):
        self.n_dp, self.orders, self.pairs, self.step = n_dp, orders, pairs, step
        self.names = names
        self.weighted = weighted
        self.steps = len(orders[0])

    def __add__(self, other):
        assert self.step == other.step and self.orders == other.orders
        return Stream(
            self.n_dp, self.orders, self.pairs + other.pairs, self.names + other.names, self.step, self.weighted
        )

    def key(self):
        return (self.step, self.orders, self.weighted, self.pairs[0][0].shape[2:])

    @property
    def last(self):
        return self.step == self.steps

    @property
    def dims(self):
        count = 1 if self.last else self.n_dp >> (self.step + 1)
        return (count, sum(p[4] for p in self.pairs)) + self.pairs[0][0].shape[2:]

    def bit(self, core, j):
        a, b = self.orders[0][j], self.orders[1][j]
        return a if a == b else jnp.where(core == 0, a, b)

    def read(self, ref, pair, i, dp, core, mine):
        kind, first, size = pair[2:]
        if self.last:
            return ref[0, pl.ds(first, size)]
        bit = (dp >> self.bit(core, self.step)) & 1
        chosen = bit if mine else 1 - bit
        if kind == "kept":
            return ref[2 * i + chosen, pl.ds(first, size)]
        at = chosen << self.bit(core, 0)
        for j in range(1, self.steps):
            at = at + (((i >> (j - 1)) & 1) << self.bit(core, j))
        if kind == "rows":
            return ref[at, pl.ds(first, size)]
        return ref[pl.ds(first, size), at]


class Vectors:
    def __init__(self, total, n_dp):
        self.n_dp, self.total = n_dp, total
        self.masks = [0] + [1 << b for b in range(n_dp.bit_length() - 1)]
        self.swap()

    def swap(self):
        mask = self.masks.pop(0)
        self.received = swap_with(self.total, self.n_dp, (mask, mask))


def tick(pos, task, name, streams, after=(), vectors=None):
    arrays, jobs, outs = [], [], []

    def operand(array):
        for n, known in enumerate(arrays):
            if known is array:
                return n
        arrays.append(array)
        return len(arrays) - 1

    for stream in streams:
        pairs = [(operand(p[0]), operand(p[1])) for p in stream.pairs]
        jobs.append((stream, pairs, len(outs)))
        outs += [pltpu.VMEM(stream.dims, F32)] * (1 if stream.last else 2)
    if vectors is not None:
        pair = (operand(vectors.total), operand(vectors.received))
        outs.append(pltpu.VMEM((VECTORS, D), F32))

    scalars = [pos] + (list(task) if any(stream.weighted for stream in streams) else [])

    def kernel(pos_ref, *refs):
        task_refs, refs = refs[: len(scalars) - 1], refs[len(scalars) - 1 :]
        ins, out_refs = refs[: len(arrays)], refs[len(arrays) :]
        dp, core = pos_ref[0], pos_ref[1]

        def add(stream, pairs, n, mine, i):
            offset = 0
            for pair, (held, received) in zip(stream.pairs, pairs):
                a = stream.read(ins[held], pair, i, dp, core, mine)
                b = stream.read(ins[received], pair, i, dp, core, mine)
                total = a + b
                if stream.weighted:
                    total = total * task_weight(*task_refs, total.shape[-1])
                out_refs[n + mine][i, pl.ds(offset, pair[4])] = total
                offset += pair[4]

        for stream, pairs, n in jobs:
            for mine in (0,) if stream.last else (0, 1):
                act = functools.partial(add, stream, pairs, n, mine)
                if stream.dims[0] <= 8:
                    for i in range(stream.dims[0]):
                        act(i)
                else:
                    pl.loop(0, stream.dims[0])(act)
        if vectors is not None:
            out_refs[-1][...] = ins[pair[0]][...] + ins[pair[1]][...]

    return small_call(kernel, name, scalars, arrays, outs, after)


class Transfers:
    def __init__(self, pos, task, n_dp):
        self.pos, self.task, self.n_dp, self.ticks = pos, task, n_dp, 0
        self.streams, self.vectors, self.mine = [], None, []

    def other_core(self, value):
        return swap_with(value, self.n_dp, (0, 0))

    def order(self, pattern):
        return tuple(b for p in pattern for b in ([p] if p < 3 else range(3, self.n_dp.bit_length() - 1)))

    def begin(self, kind, own, other, names, plan, weighted):
        rows = D // self.n_dp
        blocks, width = len(names), own.shape[-1]
        dims = (self.n_dp, blocks, rows, width) if kind == "rows" else (blocks, self.n_dp, rows, width)
        own, received = own.reshape(dims), self.other_core(other.reshape(dims))
        first = 0
        for count, patterns in plan:
            orders = tuple(self.order(p) for p in patterns)
            pair = (own, received, kind, first, count)
            self.streams.append(Stream(self.n_dp, orders, [pair], names[first : first + count], weighted=weighted))
            first += count

    def named(self, name):
        return next((s for s in self.streams if name in s.names), None)

    def tick(self, wanted, after):
        vectors = None
        streams = []
        for name in wanted:
            if name == "vectors":
                vectors = self.vectors
                continue
            stream = self.named(name)
            if stream is not None and stream not in streams:
                streams.append(stream)
        merged = {}
        for stream in streams:
            self.streams.remove(stream)
            key = stream.key()
            merged[key] = merged[key] + stream if key in merged else stream
        streams = list(merged.values())
        self.ticks += 1
        sent = tick(self.pos, self.task, "tick_%d" % self.ticks, streams, after, vectors)
        n = 0
        for stream in streams:
            if stream.last:
                self.mine.append((sent[n], self.other_core(sent[n]), stream.names))
                n += 1
                continue
            masks = tuple(1 << order[stream.step] for order in stream.orders)
            received = swap_with(sent[n], self.n_dp, masks)
            pair = (sent[n + 1], received, "kept", 0, stream.dims[1])
            self.streams.append(Stream(self.n_dp, stream.orders, [pair], stream.names, stream.step + 1))
            n += 2
        if vectors is not None:
            vectors.total = sent[-1]
            if vectors.masks:
                vectors.swap()
            else:
                vectors.received = None
        return [sent[0]]

    def finish(self, after):
        while self.streams or self.vectors.received is not None:
            wanted = [s.names[0] for s in self.streams]
            after = self.tick(wanted + ["vectors"] * (self.vectors.received is not None), after)
        return after


def place_kernel(pos_ref, *refs, places, blocks, halves):
    core = pos_ref[1]
    for source, b, n, row, cols in places:
        mine, theirs = refs[2 * source][0, b], refs[2 * source + 1][0, b]
        rows, width = mine.shape
        out = refs[len(refs) - blocks + n]
        out[row : row + rows, cols[0] : cols[0] + width] = jnp.where(core == 0, mine, theirs)
        out[row : row + rows, cols[1] : cols[1] + width] = jnp.where(core == 0, theirs, mine)
    vectors, singles, wide = refs[2 * halves], refs[2 * halves + 1 : 2 * halves + 9], refs[2 * halves + 9]
    rows, per = singles[0].shape[0], wide.shape[0]
    turned = pltpu.roll(vectors[:8], lax.rem(D - pos_ref[0] * rows, D), 1)
    for n, single in enumerate(singles):
        single[...] = turned[n, :rows]
    at = pos_ref[0] * per
    turned = pltpu.roll(vectors[8:], lax.rem(D - lax.rem(at, D), D), 1)
    line = lax.broadcasted_iota(jnp.int32, turned.shape, 0) == at // D
    wide[...] = jnp.sum(jnp.where(line, turned, 0.0), axis=0)[:per]


def place(pos, sums, outs, after, vectors):
    places = [(k, b) + name for k, (_, _, names) in enumerate(sums) for b, name in enumerate(names)]
    rows = D // vectors.n_dp
    more = [(rows,)] * 8 + [(rows * FF // D,)]
    return small_call(
        functools.partial(place_kernel, places=places, blocks=len(outs), halves=len(sums)),
        "place",
        [pos],
        [x for mine, theirs, _ in sums for x in (mine, theirs)] + [vectors.total],
        [shape(dims, F32) for dims in more + outs],
        after,
    )


def count_rounds(labels, n_dp, window):
    hits = (labels[:, None] == jnp.arange(NTASK, dtype=jnp.int32)[None, :]).astype(jnp.int32)
    counts = [jnp.sum(hits, axis=0) * (2 * window)]
    bit = 1
    while bit < n_dp:
        masks = [bit] if 2 * bit >= n_dp else [bit, 2 * bit, 3 * bit]
        counts.append(counts[-1] + sum(swap_with(counts[-1], n_dp, (m, m)) for m in masks))
        bit *= 4
    return counts[1:]


def per_device(tokens, segments, labels, cotangent, w_qkv, b_query, b_value, w_out, b_out, gamma_one, beta_one, gamma_two, beta_two, w_up, b_up, w_down, b_down, *, n_dp):
    windows, window, width = tokens.shape
    pos = jnp.stack([lax.axis_index("dp"), lax.axis_index("group")]).astype(jnp.int32)
    x = tokens.reshape(window, width)
    cot = cotangent.reshape(window, width)
    counts = count_rounds(labels, n_dp, window)

    rows = D // n_dp
    moving = Transfers(pos, (counts[-1], labels), n_dp)

    down_names = [(0, b * rows, (0, HALF)) for b in range(4)]
    up_names = [(1, 0, (b * D, b * D + HALF)) for b in range(4)]
    first_names, last_names = [], []
    for b in range(3):
        for at in (b * D, b * D + LANES):
            first_names.append((2, 0, (at, at + 2 * LANES)))
        first_names.append((3, 0, (2 * b * LANES, (2 * b + 1) * LANES)))
        last_names.append((2, 0, (b * D + 4 * LANES, b * D + 5 * LANES)))
    chunks = {"D": down_names, "U": up_names, "F": first_names, "L": last_names}

    def begin(chunk, kind, own, other):
        moving.begin(kind, own, other, chunks[chunk], PLAN[chunk], chunk == "D")

    proj, in_one, att, probs, mid, in_two = forward(
        x, segments, gamma_one, beta_one, w_qkv, b_query, b_value, w_out, b_out, gamma_two, beta_two
    )
    act, slope, own, other = up(pos, in_two, cot, w_up, b_up, counts[:1])
    begin("D", "rows", own, other)
    after = []
    for step in SCHEDULE:
        if step == "hidden":
            gp, go, own, other, sum_up, sum_down = hidden(pos, counts[-1], labels, cot, in_two, slope, w_down)
            begin("U", "blocks", own, other)
            after = [gp]
        elif step == "middle":
            gm, gb, ga, sums_mid = middle_back(go, mid, gamma_two, gp, w_up, w_out, after)
            after = [ga]
        elif step == "attend first":
            first = attend_back(proj, ga, probs, 0, 4, after)
            after = [first]
        elif step == "first heads":
            own, other = first_heads(pos, in_one, first, att, gb, after)
            begin("F", "blocks", own, other)
            after = [own]
        elif step == "attend last":
            last = attend_back(proj, ga, probs, 4, 2, after)
            after = [last]
        elif step == "last heads":
            own, other = last_heads(pos, in_one, last, after)
            begin("L", "blocks", own, other)
            after = [own]
        elif step == "input":
            grad_tokens, vectors = input_back(
                x, gm, gamma_one, first, last, w_qkv, sums_mid, sum_down, sum_up, after
            )
            moving.vectors = Vectors(vectors, n_dp)
            after = [grad_tokens]
        elif step == "mix":
            mixed = mix(mid, act, w_down, b_down, after)
            after = [mixed]
        else:
            wanted = []
            for item in step:
                if item == "V":
                    wanted.append("vectors")
                else:
                    first_block = sum(count for count, _ in PLAN[item[0]][: int(item[1])])
                    wanted.append(chunks[item[0]][first_block])
            after = moving.tick(wanted, after)
    after = moving.finish(after)
    *singles, grad_b_up, grad_down, grad_up, grad_qkv, grad_out = place(
        pos, moving.mine, [(4 * rows, D), (rows, FF), (rows, 3 * D), (rows, D)], after, moving.vectors
    )
    query, value, gain_one, shift_one, gain_two, shift_two, out, bias_down = singles
    return (
        mixed.reshape(tokens.shape),
        grad_tokens.reshape(tokens.shape),
        grad_qkv,
        query,
        value,
        grad_out,
        out,
        gain_one,
        shift_one,
        gain_two,
        shift_two,
        grad_up,
        grad_b_up,
        grad_down,
        bias_down,
        counts[-1],
    )


def solution(mesh):
    split = P(("dp", "group"), None, None)
    return jax.shard_map(
        functools.partial(per_device, n_dp=mesh.shape["dp"]),
        mesh=mesh,
        in_specs=(split, P(("dp", "group"), None), P(("dp", "group")), split) + (P(),) * 13,
        out_specs=(split, split, P("dp", None), P("dp"), P("dp"), P("dp", None))
        + (P("dp"),) * 5
        + (P("dp", None), P("dp"), P("dp", None), P("dp"), P()),
        check_vma=False,
    )
```

```python
import functools
import math

import jax
import jax.numpy as jnp
from jax import lax
from jax.experimental import pallas as pl
from jax.experimental.pallas import tpu as pltpu
from jax.sharding import PartitionSpec as P

F32 = jnp.float32
BF = jnp.bfloat16
D = 768
HEADS = 12
HEAD = 64
PAIR = 2 * HEAD
LANES = 128
FF = 3072
NTASK = 3
VECTORS = 16
QB = 256
EPISODE = 256
QUERIES = 128
STAGGER = 2
HALF = D // 2
AXES = ("dp", "group")
NN = (((1,), (0,)), ((), ()))
NT = (((1,), (1,)), ((), ()))
TN = (((0,), (0,)), ((), ()))
PLAN = {'D': [(3, ((1, 2, 3, 0), (0, 2, 3, 1))), (1, ((2, 3, 1, 0), (2, 3, 0, 1)))],
 'U': [(3, ((0, 1, 2, 3), (1, 0, 2, 3))), (1, ((2, 0, 1, 3), (2, 1, 0, 3)))],
 'F': [(3, ((1, 2, 0, 3), (0, 2, 1, 3))), (6, ((1, 0, 2, 3), (0, 1, 2, 3)))],
 'L': [(3, ((0, 1, 2, 3), (1, 0, 2, 3)))]}
SCHEDULE = ['hidden', ('D0', 'D1'), 'middle', ('U0', 'U1', 'D1'), 'attend first', 'first heads', ('D0',), ('D1',), ('U0',), 'attend last', ('D1', 'U1', 'F0', 'F1'), 'last heads', ('U0',), ('D0',), 'input', ('U1', 'F0', 'L0', 'D1'), ('U0', 'U1', 'V'), ('F1',), 'mix', ('D0', 'U1', 'F0', 'V'), ('U0', 'F1'), ('D0', 'F0', 'V'), ('L0',), ('L0', 'F0', 'F1'), ('L0',), ('F1', 'L0')]
COST = {'first_heads_grad': 0,
 'last_heads_grad': 0,
 'attend_back_first': 20,
 'attend_back_last': 20,
 'norm_one_back': 3,
 'mix': 20,
 'norm_two_back': 3,
 'hidden_grad': 60}
FLOPS = 4e9
TICK_FLOPS = 1000000000
FREE = {'hidden_grad': [6],
 'norm_two_back': [0, 3],
 'first_heads_grad': [1, 2],
 'last_heads_grad': [1, 2],
 'norm_one_back': [3, 4, 5],
 'mix': [2]}
OUT = {'up_and_down_grad': [2], 'hidden_grad': [0, 1], 'attend_back_first': [0], 'attend_back_last': [0]}
VMEM_LIMIT = 34 * 2**20
TICK_LIMIT = 20 * 2**20


def dot(a, b, dims=NN):
    return lax.dot_general(a, b, dims, preferred_element_type=F32)


def in_hbm(x):
    return pltpu.with_memory_space_constraint(x, pltpu.HBM)


def call(kernel, name, grid, in_specs, out_specs, out_shape, scratch=(), prefetch=0, us=3, after=0, limit=None):
    in_specs = list(in_specs) + [pl.BlockSpec(memory_space=pl.ANY)] * after
    body = kernel
    if after:
        start = prefetch + len(in_specs) - after

        def body(*refs):
            kernel(*refs[:start], *refs[start + after :])

    single = not isinstance(out_shape, list)
    made = [(s if n in OUT.get(name, ()) else pltpu.HBM(s.shape, s.dtype)) if isinstance(s, jax.ShapeDtypeStruct) else s for n, s in enumerate([out_shape] if single else out_shape)]
    run = pl.pallas_call(
        body,
        grid_spec=pltpu.PrefetchScalarGridSpec(
            num_scalar_prefetch=prefetch,
            grid=grid,
            in_specs=in_specs,
            out_specs=[out_specs] if single else out_specs,
            scratch_shapes=list(scratch),
        ),
        out_shape=made,
        compiler_params=pltpu.CompilerParams(vmem_limit_bytes=limit or VMEM_LIMIT),
        cost_estimate=pl.CostEstimate(flops=int(COST.get(name, us) * FLOPS), bytes_accessed=us, transcendentals=0),
        name=name,
    )

    def apply(*args):
        last = len(args) - after
        table = FREE.get(name, ())
        args = [x if n < prefetch or n >= last or n in table else in_hbm(x) for n, x in enumerate(args)]
        out = run(*args)
        return out[0] if single else out

    return apply


def shape(dims, dtype):
    return jax.ShapeDtypeStruct(dims, dtype)


def whole(*dims):
    return pl.BlockSpec(dims, lambda *_: (0,) * len(dims))


SMEM = pl.BlockSpec(memory_space=pltpu.SMEM)


def unit(x):
    centered = x - jnp.mean(x, axis=-1, keepdims=True)
    inv = lax.rsqrt(jnp.mean(centered * centered, axis=-1, keepdims=True) + 1e-05)
    return centered * inv, inv


def norm_back(e, u, inv, gain):
    scaled = e * gain
    return inv * (
        scaled
        - jnp.mean(scaled, axis=-1, keepdims=True)
        - u * jnp.mean(scaled * u, axis=-1, keepdims=True)
    )


def rows_of(ref):
    return range(0, ref.shape[0], QB)


def column_sum(x):
    return jnp.sum(x, axis=0, keepdims=True)


def bands(t):
    return [(q, max(0, q - EPISODE), min(q + QUERIES, EPISODE + QUERIES)) for q in range(0, t, QUERIES)]


def head_pair(x):
    lane = lax.broadcasted_iota(jnp.int32, (1, PAIR), 1)
    zero = jnp.zeros_like(x)
    return jnp.concatenate([jnp.where(lane < HEAD, x, zero), jnp.where(lane < HEAD, zero, x)], axis=0)


def heads_side_by_side(x):
    return jnp.concatenate([x[:HEAD, :QUERIES], x[HEAD:, QUERIES:]], axis=0).T


def staggered(units, stages):
    waiting = [{} for _ in stages]
    lags = [0, STAGGER, STAGGER + 1]
    for n in range(len(units) + lags[-1]):
        for k, stage in enumerate(stages):
            m = n - lags[k]
            if 0 <= m < len(units):
                given = () if k == 0 else (waiting[k - 1].pop(m),)
                waiting[k][m] = stage(*units[m], *given)


def forward_kernel(x_ref, seg_ref, g1_ref, s1_ref, wq_ref, wk_ref, wv_ref, bq_ref, bv_ref, wo_ref, bo_ref, g2_ref, s2_ref, proj_ref, in_one_ref, att_ref, p_ref, mid_ref, in_two_ref, bias_ref, turned_ref, acc_ref):
    g = pl.program_id(0)
    t = x_ref.shape[0]
    blocks = bands(t)

    @pl.when(g == 0)
    def _():
        for r in rows_of(x_ref):
            u, _ = unit(x_ref[r : r + QB].astype(F32))
            in_one_ref[r : r + QB] = (u * g1_ref[...] + s1_ref[...]).astype(BF)
            acc_ref[r : r + QB] = x_ref[r : r + QB].astype(F32) + bo_ref[...]
        hot = (seg_ref[...] == lax.broadcasted_iota(jnp.int32, (8, t), 0)).astype(BF)
        for i, (q0, k0, n) in enumerate(blocks):
            same = dot(hot[:, k0 : k0 + n], hot[:, q0 : q0 + QUERIES], TN)
            col = k0 + lax.broadcasted_iota(jnp.int32, (n, QUERIES), 0)
            row = q0 + lax.broadcasted_iota(jnp.int32, (n, QUERIES), 1)
            bias_ref[i, :n] = jnp.where((same > 0.5) & (col <= row), 0.0, -1e30).astype(F32)

    width = wq_ref.shape[1]
    here = pl.ds(pl.multiple_of(g * width, width), width)
    for r in range(0, t, 2 * QB):
        rows = in_one_ref[r : r + 2 * QB]
        proj_ref[0, r : r + 2 * QB] = ((dot(rows, wq_ref[...]) + bq_ref[here]) * HEAD**-0.5).astype(BF)
        proj_ref[1, r : r + 2 * QB] = dot(rows, wk_ref[...]).astype(BF)
        proj_ref[2, r : r + 2 * QB] = (dot(rows, wv_ref[...]) + bv_ref[here]).astype(BF)
    pairs = width // PAIR
    for w in range(pairs):
        turned_ref[w] = proj_ref[2, :, w * PAIR : (w + 1) * PAIR].T

    def scores(w, i):
        q0, k0, n = blocks[i]
        cols = slice(w * PAIR, (w + 1) * PAIR)
        return dot(proj_ref[1, k0 : k0 + n, cols], head_pair(proj_ref[0, q0 : q0 + QUERIES, cols]), NT)

    def softmax(w, i, values):
        n = blocks[i][2]
        parts = []
        for a in range(2):
            part = values[:, a * QUERIES : (a + 1) * QUERIES] + bias_ref[i, :n]
            e = jnp.exp(part - jnp.max(part, axis=0, keepdims=True))
            probs = (e * (1.0 / jnp.sum(e, axis=0, keepdims=True))).astype(BF)
            p_ref[w, i, :n, a * QUERIES : (a + 1) * QUERIES] = probs
            parts.append(probs)
        return jnp.concatenate(parts, axis=1)

    def attend(w, i, probs):
        q0, k0, n = blocks[i]
        out = dot(turned_ref[w, :, k0 : k0 + n], probs)
        att_ref[q0 : q0 + QUERIES, w * PAIR : (w + 1) * PAIR] = heads_side_by_side(out).astype(BF)

    units = [(w, i) for w in range(pairs) for i in range(len(blocks))]
    staggered(units, (scores, softmax, attend))

    acc_ref[...] += dot(att_ref[...], wo_ref[...])

    @pl.when(g == pl.num_programs(0) - 1)
    def _():
        for r in rows_of(x_ref):
            mid = acc_ref[r : r + QB]
            mid_ref[r : r + QB] = mid
            u, _ = unit(mid)
            in_two_ref[r : r + QB] = (u * g2_ref[...] + s2_ref[...]).astype(BF)


def forward(x, seg, gain_one, shift_one, w_qkv, b_query, b_value, w_out, b_out, gain_two, shift_two):
    t = x.shape[0]
    width = 2 * PAIR
    steps = D // width
    count = t // QUERIES
    keys = EPISODE + QUERIES

    def weights(part):
        return pl.BlockSpec((D, width), lambda g: (0, part * steps + g))

    return call(
        forward_kernel,
        "forward",
        (steps,),
        [whole(t, D), whole(1, t), whole(D), whole(D), weights(0), weights(1), weights(2), whole(D), whole(D)]
        + [pl.BlockSpec((width, D), lambda g: (g, 0)), whole(D), whole(D), whole(D)],
        [
            pl.BlockSpec((3, t, width), lambda g: (0, 0, g)),
            whole(t, D),
            pl.BlockSpec((t, width), lambda g: (0, g)),
            pl.BlockSpec((2, count, keys, 2 * QUERIES), lambda g: (g, 0, 0, 0)),
            whole(t, D),
            whole(t, D),
        ],
        [
            shape((3, t, D), BF),
            shape((t, D), BF),
            shape((t, D), BF),
            shape((HEADS // 2, count, keys, 2 * QUERIES), BF),
            shape((t, D), F32),
            shape((t, D), BF),
        ],
        [
            pltpu.VMEM((count, keys, QUERIES), F32),
            pltpu.VMEM((2, PAIR, t), BF),
            pltpu.VMEM((t, D), F32),
        ],
        us=24,
        limit=60 * 2**20,
    )(x, seg, gain_one, shift_one, w_qkv, w_qkv, w_qkv, b_query, b_value, w_out, b_out, gain_two, shift_two)


def gelu_both(v):
    cdf = 0.5 * (1.0 + lax.erf(v * (2.0**-0.5)))
    pdf = jnp.exp(-0.5 * v * v) * (1.0 / math.sqrt(2 * math.pi))
    return v * cdf, cdf + v * pdf


def own_first(core, x):
    half = x.shape[1] // 2
    return jnp.where(core == 0, x, jnp.concatenate([x[:, half:], x[:, :half]], axis=1))


def task_weight(counts_ref, label_ref, width):
    total = (counts_ref[0] + counts_ref[1] + counts_ref[2]).astype(F32)
    here = (NTASK * counts_ref[label_ref[0]]).astype(F32)
    return jnp.full((1, width), total, F32) / jnp.full((1, width), here, F32)


def up_kernel(pos_ref, in_ref, cot_ref, w_ref, b_ref, act_ref, slope_ref, own_ref, other_ref, turned):
    @pl.when(pl.program_id(0) == 0)
    def _():
        turned[...] = own_first(pos_ref[1], cot_ref[...])

    bias = b_ref[pl.ds(pl.multiple_of(pl.program_id(0) * D, D), D)]
    rows = QB // 2
    starts = list(range(0, in_ref.shape[0], rows))
    pre = None
    for r in starts + [None]:
        ready, pre = pre, None if r is None else dot(in_ref[r : r + rows], w_ref[...]) + bias
        if ready is not None:
            act, slope = gelu_both(ready)
            act_ref[last : last + rows] = act.astype(BF)
            slope_ref[last : last + rows] = slope.astype(BF)
        last = r
    grad = dot(act_ref[...], turned[...], TN)
    own_ref[...] = grad[:, :HALF]
    other_ref[...] = grad[:, HALF:]


def up(pos, in_two, cot, w_up, b_up, after=()):
    t = in_two.shape[0]
    cols = pl.BlockSpec((t, D), lambda j, *_: (0, j))
    half = pl.BlockSpec((D, HALF), lambda j, *_: (j, 0))
    return call(
        up_kernel,
        "up_and_down_grad",
        (FF // D,),
        [
            whole(t, D),
            whole(t, D),
            pl.BlockSpec((D, D), lambda j, *_: (0, j)),
            whole(FF),
        ],
        [cols, cols, half, half],
        [shape((t, FF), BF)] * 2 + [shape((FF, HALF), F32)] * 2,
        [pltpu.VMEM((t, D), BF)],
        prefetch=1,
        us=16,
        after=len(after),
    )(pos, in_two, cot, w_up, b_up, *after)


def hidden_kernel(pos_ref, counts_ref, label_ref, cot_ref, in_ref, slope_ref, w_ref, gp_ref, go_ref, own_ref, other_ref, sum_ref, down_ref):
    @pl.when(pl.program_id(0) == 0)
    def _():
        go = (cot_ref[...].astype(F32) * task_weight(counts_ref, label_ref, D)).astype(BF)
        go_ref[...] = go
        down_ref[...] = column_sum(go.astype(F32))

    grad = None
    for r in list(rows_of(go_ref)) + [None]:
        ready, grad = grad, None if r is None else dot(go_ref[r : r + QB], w_ref[...], NT)
        if ready is not None:
            gp_ref[last : last + QB] = (ready * slope_ref[last : last + QB].astype(F32)).astype(BF)
        last = r
    sum_ref[0] = column_sum(gp_ref[...].astype(F32))
    grad = dot(in_ref[...], own_first(pos_ref[1], gp_ref[...]), TN)
    own_ref[0] = grad[:, :HALF]
    other_ref[0] = grad[:, HALF:]


def block_half():
    return pl.BlockSpec((1, D, HALF), lambda j, *_: (j, 0, 0))


def hidden(pos, counts, labels, cot, in_two, slope, w_down):
    t = in_two.shape[0]
    cols = pl.BlockSpec((t, D), lambda j, *_: (0, j))
    return call(
        hidden_kernel,
        "hidden_grad",
        (FF // D,),
        [whole(t, D), whole(t, D), cols, pl.BlockSpec((D, D), lambda j, *_: (j, 0))],
        [
            cols,
            whole(t, D),
            block_half(),
            block_half(),
            pl.BlockSpec((1, 1, D), lambda j, *_: (j, 0, 0)),
            whole(1, D),
        ],
        [shape((t, FF), BF), shape((t, D), BF)]
        + [shape((FF // D, D, HALF), F32)] * 2
        + [shape((FF // D, 1, D), F32), shape((1, D), F32)],
        prefetch=3,
        us=14,
    )(pos, counts, labels, cot, in_two, slope, w_down)


def add_sums(ref, first, sums):
    for n, value in enumerate(sums):

        @pl.when(first)
        def _():
            ref[n : n + 1] = value

        @pl.when(jnp.logical_not(first))
        def _():
            ref[n : n + 1] += value


def middle_kernel(go_ref, mid_ref, g_ref, gp_ref, wu_ref, wo_ref, gm_ref, gb_ref, ga_ref, sums_ref):
    starts = rows_of(gm_ref)
    following = dot(gp_ref[:QB], wu_ref[...], NT)
    sums = [0.0, 0.0, 0.0]
    for r in starts:
        e = following
        if r + QB < gm_ref.shape[0]:
            following = dot(gp_ref[r + QB : r + 2 * QB], wu_ref[...], NT)
        u, inv = unit(mid_ref[r : r + QB])
        gm = go_ref[r : r + QB].astype(F32) + norm_back(e, u, inv, g_ref[...])
        gm_ref[r : r + QB] = gm
        gb = gm.astype(BF)
        gb_ref[r : r + QB] = gb
        ga_ref[r : r + QB] = dot(gb, wo_ref[...], NT).astype(BF)
        parts = (column_sum(e * u), column_sum(e), column_sum(gb.astype(F32)))
        sums = [total + part for total, part in zip(sums, parts)]
    add_sums(sums_ref, pl.program_id(0) == 0, sums)


def middle_back(go, mid, gain, gp, w_up, w_out, after=()):
    t = go.shape[0]
    rows = 2 * QB
    row = pl.BlockSpec((rows, D), lambda i: (i, 0))
    return call(
        middle_kernel,
        "norm_two_back",
        (t // rows,),
        [row, row, whole(D), pl.BlockSpec((rows, FF), lambda i: (i, 0)), whole(D, FF), whole(D, D)],
        [row, row, row, whole(3, D)],
        [shape((t, D), F32), shape((t, D), BF), shape((t, D), BF), shape((3, D), F32)],
        us=16,
        after=len(after),
    )(go, mid, gain, gp, w_up, w_out, *after)


def attend_back_kernel(q_ref, k_ref, v_ref, ga_ref, p_ref, d_ref, dk_ref, dv_ref, turned_ref):
    t = q_ref.shape[1]
    blocks = bands(t)

    @pl.loop(0, q_ref.shape[2] // PAIR)
    def _(w):
        cols = pl.ds(pl.multiple_of(w * PAIR, PAIR), PAIR)
        turned_ref[...] = k_ref[0, :, cols].T

        def grad_probs(i):
            q0, k0, n = blocks[i]
            return dot(v_ref[0, k0 : k0 + n, cols], head_pair(ga_ref[q0 : q0 + QUERIES, cols]), NT)

        def grad_scores(i, values):
            probs = p_ref[w, i, : blocks[i][2]].astype(F32)
            prod = probs * values
            return (prod - probs * jnp.sum(prod, axis=0, keepdims=True)).astype(BF)

        def rest(i, ds):
            q0, k0, n = blocks[i]
            dq = heads_side_by_side(dot(turned_ref[:, k0 : k0 + n], ds))
            d_ref[0, q0 : q0 + QUERIES, cols] = dq.astype(BF) * jnp.asarray(HEAD**-0.5, BF)
            known = n - QUERIES if i else 0
            done = blocks[i + 1][1] if i + 1 < len(blocks) else t
            dk = dot(ds, head_pair(q_ref[0, q0 : q0 + QUERIES, cols]))
            dv = dot(p_ref[w, i, :n], head_pair(ga_ref[q0 : q0 + QUERIES, cols]))
            for part, ref, value in ((1, dk_ref, dk), (2, dv_ref, dv)):
                if known:
                    ref[k0 : k0 + known] += value[:known]
                ref[k0 + known : k0 + n] = value[known:]
                if done > k0:
                    d_ref[part, k0:done, cols] = ref[k0:done].astype(BF)

        staggered([(i,) for i in range(len(blocks))], (grad_probs, grad_scores, rest))


def attend_back(proj, ga, probs, first, pairs, after=()):
    t = proj.shape[1]
    width = 2 * PAIR
    start = first // 2

    def block(part):
        return pl.BlockSpec((1, t, width), lambda h: (part, 0, start + h))

    return call(
        attend_back_kernel,
        "attend_back_last" if first else "attend_back_first",
        (pairs // 2,),
        [
            block(0),
            block(1),
            block(2),
            pl.BlockSpec((t, width), lambda h: (0, start + h)),
            pl.BlockSpec((2,) + probs.shape[1:], lambda h: (start + h, 0, 0, 0)),
        ],
        pl.BlockSpec((3, t, width), lambda h: (0, 0, h)),
        shape((3, t, pairs * PAIR), BF),
        [pltpu.VMEM((t, PAIR), F32)] * 2 + [pltpu.VMEM((PAIR, t), BF)],
        us=3 * pairs,
        after=len(after),
    )(proj, proj, proj, ga, probs, *after)


def first_heads_kernel(pos_ref, in_ref, d_ref, att_ref, gb_ref, own_ref, other_ref):
    core = pos_ref[1]
    grad = dot(in_ref[...], own_first(core, d_ref[0]), TN)
    grad_out = dot(att_ref[...], own_first(core, gb_ref[...]), TN)
    columns = [grad[:, n * LANES : (n + 1) * LANES] for n in range(4)]
    columns += [grad_out[:, n * LANES : (n + 1) * LANES] for n in range(2)]
    for n, (own, other) in enumerate([(0, 2), (1, 3), (4, 5)]):
        own_ref[n] = columns[own]
        other_ref[n] = columns[other]


def first_heads(pos, in_one, d, att, gb, after=()):
    t = in_one.shape[0]
    block = pl.BlockSpec((3, D, LANES), lambda j, *_: (j, 0, 0))
    return call(
        first_heads_kernel,
        "first_heads_grad",
        (3,),
        [
            whole(t, D),
            pl.BlockSpec((1, t, 4 * LANES), lambda j, *_: (j, 0, 0)),
            whole(t, D),
            pl.BlockSpec((t, 2 * LANES), lambda j, *_: (0, j)),
        ],
        [block, block],
        [shape((9, D, LANES), F32)] * 2,
        prefetch=1,
        us=10,
        after=len(after),
    )(pos, in_one, d, att, gb, *after)


def last_heads_kernel(pos_ref, in_ref, d_ref, own_ref, other_ref):
    turned = jnp.concatenate([own_first(pos_ref[1], d_ref[b]) for b in range(3)], axis=1)
    grad = dot(in_ref[...], turned, TN)
    for b in range(3):
        own_ref[b] = grad[:, 2 * b * LANES : (2 * b + 1) * LANES]
        other_ref[b] = grad[:, (2 * b + 1) * LANES : (2 * b + 2) * LANES]


def last_heads(pos, in_one, d, after=()):
    t = in_one.shape[0]
    return call(
        last_heads_kernel,
        "last_heads_grad",
        (1,),
        [whole(t, D), whole(3, t, 2 * LANES)],
        [whole(3, D, LANES)] * 2,
        [shape((3, D, LANES), F32)] * 2,
        prefetch=1,
        us=5,
        after=len(after),
    )(pos, in_one, d, *after)


def input_kernel(x_ref, gm_ref, g_ref, first_ref, last_ref, w_ref, mid_sums, down_sum, up_sums, gt_ref, sums_ref):
    e = 0.0
    split = first_ref.shape[2]
    for b in range(3):
        e = e + dot(first_ref[b], w_ref[:, b * D : b * D + split], NT)
        e = e + dot(last_ref[b], w_ref[:, b * D + split : (b + 1) * D], NT)
    u, inv = unit(x_ref[...].astype(F32))
    gt_ref[...] = (gm_ref[...] + norm_back(e, u, inv, g_ref[...])).astype(BF)
    start = pl.program_id(0) == 0
    sums = []
    for b in (0, 2):
        pair = [column_sum(ref[b].astype(F32)) for ref in (first_ref, last_ref)]
        sums.append(jnp.concatenate(pair, axis=1))
    add_sums(sums_ref, start, sums + [column_sum(e * u), column_sum(e)])

    @pl.when(start)
    def _():
        sums_ref[4:7] = mid_sums[...]
        sums_ref[7:8] = down_sum[...]
        for b in range(FF // D):
            sums_ref[8 + b : 9 + b] = up_sums[b]
        sums_ref[8 + FF // D :] = jnp.zeros((VECTORS - 8 - FF // D, D), F32)


def input_back(x, gm, gain, first, last, w_qkv, mid_sums, down_sum, up_sums, after=()):
    t = x.shape[0]
    row = pl.BlockSpec((QB, D), lambda i: (i, 0))
    part = lambda d: pl.BlockSpec((3, QB, d.shape[2]), lambda i: (0, i, 0))
    return call(
        input_kernel,
        "norm_one_back",
        (t // QB,),
        [
            row,
            row,
            whole(D),
            part(first),
            part(last),
            whole(D, 3 * D),
            whole(3, D),
            whole(1, D),
            whole(FF // D, 1, D),
        ],
        [row, whole(VECTORS, D)],
        [shape((t, D), BF), shape((VECTORS, D), F32)],
        us=10,
        after=len(after),
    )(x, gm, gain, first, last, w_qkv, mid_sums, down_sum, up_sums, *after)


def mix_kernel(mid_ref, act_ref, w_ref, b_ref, out_ref):
    out_ref[...] = (mid_ref[...] + dot(act_ref[...], w_ref[...]) + b_ref[...]).astype(BF)


def mix(mid, act, w_down, b_down, after=()):
    t = mid.shape[0]
    row = pl.BlockSpec((QB, D), lambda i: (i, 0))
    return call(
        mix_kernel,
        "mix",
        (t // QB,),
        [row, pl.BlockSpec((QB, FF), lambda i: (i, 0)), whole(FF, D), whole(D)],
        row,
        shape((t, D), BF),
        us=10,
        after=len(after),
    )(mid, act, w_down, b_down, *after)


def swap_with(x, n_dp, masks):
    pairs = []
    for dp in range(n_dp):
        for core in range(2):
            mask = masks[core]
            target = (dp ^ mask) * 2 + core if mask else dp * 2 + 1 - core
            pairs.append((dp * 2 + core, target))
    return lax.ppermute(x, AXES, pairs)


def in_vmem(x):
    return pltpu.with_memory_space_constraint(x, pltpu.VMEM)


def small_call(kernel, name, scalars, arrays, outs, after=()):
    n = len(scalars) + len(arrays)

    def body(*refs):
        kernel(*refs[:n], *refs[n + len(after) :])

    vmem = pl.BlockSpec(memory_space=pltpu.VMEM)
    return pl.pallas_call(
        body,
        in_specs=[SMEM] * len(scalars) + [vmem] * len(arrays) + [pl.BlockSpec(memory_space=pl.ANY)] * len(after),
        out_specs=[vmem] * len(outs),
        out_shape=outs,
        compiler_params=pltpu.CompilerParams(vmem_limit_bytes=TICK_LIMIT),
        cost_estimate=pl.CostEstimate(flops=TICK_FLOPS, bytes_accessed=1, transcendentals=0),
        name=name,
    )(*scalars, *[in_vmem(x) for x in arrays], *[in_hbm(a) if a.dtype == BF or a.ndim < 4 else a for a in after])


class Stream:
    def __init__(self, n_dp, orders, pairs, names, step=0, weighted=False):
        self.n_dp, self.orders, self.pairs, self.step = n_dp, orders, pairs, step
        self.names = names
        self.weighted = weighted
        self.steps = len(orders[0])

    def __add__(self, other):
        assert self.step == other.step and self.orders == other.orders
        return Stream(
            self.n_dp, self.orders, self.pairs + other.pairs, self.names + other.names, self.step, self.weighted
        )

    def key(self):
        return (self.step, self.orders, self.weighted, self.pairs[0][0].shape[2:])

    @property
    def last(self):
        return self.step == self.steps

    @property
    def dims(self):
        count = 1 if self.last else self.n_dp >> (self.step + 1)
        return (count, sum(p[4] for p in self.pairs)) + self.pairs[0][0].shape[2:]

    def bit(self, core, j):
        a, b = self.orders[0][j], self.orders[1][j]
        return a if a == b else jnp.where(core == 0, a, b)

    def read(self, ref, pair, i, dp, core, mine):
        kind, first, size = pair[2:]
        if self.last:
            return ref[0, pl.ds(first, size)]
        bit = (dp >> self.bit(core, self.step)) & 1
        chosen = bit if mine else 1 - bit
        if kind == "kept":
            return ref[2 * i + chosen, pl.ds(first, size)]
        at = chosen << self.bit(core, 0)
        for j in range(1, self.steps):
            at = at + (((i >> (j - 1)) & 1) << self.bit(core, j))
        if kind == "rows":
            return ref[at, pl.ds(first, size)]
        return ref[pl.ds(first, size), at]


class Vectors:
    def __init__(self, total, n_dp):
        self.n_dp, self.total = n_dp, total
        self.rounds = [(0,)]
        for bit in range(0, n_dp.bit_length() - 1, 2):
            mask = 1 << bit
            self.rounds.append((mask,) if 2 * mask >= n_dp else (mask, 2 * mask, 3 * mask))
        self.swap()

    def swap(self):
        self.received = [swap_with(self.total, self.n_dp, (mask, mask)) for mask in self.rounds.pop(0)]


def tick(pos, task, name, streams, after=(), vectors=None):
    arrays, jobs, outs = [], [], []

    def operand(array):
        for n, known in enumerate(arrays):
            if known is array:
                return n
        arrays.append(array)
        return len(arrays) - 1

    for stream in streams:
        pairs = [(operand(p[0]), operand(p[1])) for p in stream.pairs]
        jobs.append((stream, pairs, len(outs)))
        outs += [pltpu.VMEM(stream.dims, F32)] * (1 if stream.last else 2)
    if vectors is not None:
        parts = [operand(v) for v in [vectors.total] + vectors.received]
        outs.append(pltpu.VMEM((VECTORS, D), F32))

    scalars = [pos] + (list(task) if any(stream.weighted for stream in streams) else [])

    def kernel(pos_ref, *refs):
        task_refs, refs = refs[: len(scalars) - 1], refs[len(scalars) - 1 :]
        ins, out_refs = refs[: len(arrays)], refs[len(arrays) :]
        dp, core = pos_ref[0], pos_ref[1]

        def add(stream, pairs, n, mine, i):
            offset = 0
            for pair, (held, received) in zip(stream.pairs, pairs):
                a = stream.read(ins[held], pair, i, dp, core, mine)
                b = stream.read(ins[received], pair, i, dp, core, mine)
                total = a + b
                if stream.weighted:
                    total = total * task_weight(*task_refs, total.shape[-1])
                out_refs[n + mine][i, pl.ds(offset, pair[4])] = total
                offset += pair[4]

        for stream, pairs, n in jobs:
            for mine in (0,) if stream.last else (0, 1):
                act = functools.partial(add, stream, pairs, n, mine)
                if stream.dims[0] <= 8:
                    for i in range(stream.dims[0]):
                        act(i)
                else:
                    pl.loop(0, stream.dims[0])(act)
        if vectors is not None:
            out_refs[-1][...] = sum((ins[n][...] for n in parts[1:]), ins[parts[0]][...])

    return small_call(kernel, name, scalars, arrays, outs, after)


class Transfers:
    def __init__(self, pos, task, n_dp):
        self.pos, self.task, self.n_dp, self.ticks = pos, task, n_dp, 0
        self.streams, self.vectors, self.mine = [], None, []

    def other_core(self, value):
        return swap_with(value, self.n_dp, (0, 0))

    def order(self, pattern):
        return tuple(b for p in pattern for b in ([p] if p < 3 else range(3, self.n_dp.bit_length() - 1)))

    def begin(self, kind, own, other, names, plan, weighted):
        rows = D // self.n_dp
        blocks, width = len(names), own.shape[-1]
        dims = (self.n_dp, blocks, rows, width) if kind == "rows" else (blocks, self.n_dp, rows, width)
        own, received = own.reshape(dims), self.other_core(other.reshape(dims))
        first = 0
        for count, patterns in plan:
            orders = tuple(self.order(p) for p in patterns)
            pair = (own, received, kind, first, count)
            self.streams.append(Stream(self.n_dp, orders, [pair], names[first : first + count], weighted=weighted))
            first += count

    def named(self, name):
        return next((s for s in self.streams if name in s.names), None)

    def tick(self, wanted, after):
        vectors = None
        streams = []
        for name in wanted:
            if name == "vectors":
                vectors = self.vectors
                continue
            stream = self.named(name)
            if stream is not None and stream not in streams:
                streams.append(stream)
        merged = {}
        for stream in streams:
            self.streams.remove(stream)
            key = stream.key()
            merged[key] = merged[key] + stream if key in merged else stream
        streams = list(merged.values())
        self.ticks += 1
        sent = tick(self.pos, self.task, "tick_%d" % self.ticks, streams, after, vectors)
        n = 0
        for stream in streams:
            if stream.last:
                self.mine.append((sent[n], self.other_core(sent[n]), stream.names))
                n += 1
                continue
            masks = tuple(1 << order[stream.step] for order in stream.orders)
            received = swap_with(sent[n], self.n_dp, masks)
            pair = (sent[n + 1], received, "kept", 0, stream.dims[1])
            self.streams.append(Stream(self.n_dp, stream.orders, [pair], stream.names, stream.step + 1))
            n += 2
        if vectors is not None:
            vectors.total = sent[-1]
            if vectors.rounds:
                vectors.swap()
            else:
                vectors.received = None
        return [sent[0]]

    def finish(self, after):
        while self.streams or self.vectors.received is not None:
            wanted = [s.names[0] for s in self.streams]
            after = self.tick(wanted + ["vectors"] * (self.vectors.received is not None), after)
        return after


def place_kernel(pos_ref, *refs, places, blocks, halves):
    core = pos_ref[1]
    for source, b, n, row, cols in places:
        mine, theirs = refs[2 * source][0, b], refs[2 * source + 1][0, b]
        rows, width = mine.shape
        out = refs[len(refs) - blocks + n]
        out[row : row + rows, cols[0] : cols[0] + width] = jnp.where(core == 0, mine, theirs)
        out[row : row + rows, cols[1] : cols[1] + width] = jnp.where(core == 0, theirs, mine)
    vectors, singles, wide = refs[2 * halves], refs[2 * halves + 1 : 2 * halves + 9], refs[2 * halves + 9]
    rows, per = singles[0].shape[0], wide.shape[0]
    turned = pltpu.roll(vectors[:8], lax.rem(D - pos_ref[0] * rows, D), 1)
    for n, single in enumerate(singles):
        single[...] = turned[n, :rows]
    at = pos_ref[0] * per
    turned = pltpu.roll(vectors[8:], lax.rem(D - lax.rem(at, D), D), 1)
    line = lax.broadcasted_iota(jnp.int32, turned.shape, 0) == at // D
    wide[...] = jnp.sum(jnp.where(line, turned, 0.0), axis=0)[:per]


def place(pos, sums, outs, after, vectors):
    places = [(k, b) + name for k, (_, _, names) in enumerate(sums) for b, name in enumerate(names)]
    rows = D // vectors.n_dp
    more = [(rows,)] * 8 + [(rows * FF // D,)]
    return small_call(
        functools.partial(place_kernel, places=places, blocks=len(outs), halves=len(sums)),
        "place",
        [pos],
        [x for mine, theirs, _ in sums for x in (mine, theirs)] + [vectors.total],
        [shape(dims, F32) for dims in more + outs],
        after,
    )


def count_rounds(labels, n_dp, window):
    hits = (labels[:, None] == jnp.arange(NTASK, dtype=jnp.int32)[None, :]).astype(jnp.int32)
    counts = [jnp.sum(hits, axis=0) * (2 * window)]
    bit = 1
    while bit < n_dp:
        masks = [bit] if 2 * bit >= n_dp else [bit, 2 * bit, 3 * bit]
        counts.append(counts[-1] + sum(swap_with(counts[-1], n_dp, (m, m)) for m in masks))
        bit *= 4
    return counts[1:]


def per_device(tokens, segments, labels, cotangent, w_qkv, b_query, b_value, w_out, b_out, gamma_one, beta_one, gamma_two, beta_two, w_up, b_up, w_down, b_down, *, n_dp):
    windows, window, width = tokens.shape
    pos = jnp.stack([lax.axis_index("dp"), lax.axis_index("group")]).astype(jnp.int32)
    x = tokens.reshape(window, width)
    cot = cotangent.reshape(window, width)
    counts = count_rounds(labels, n_dp, window)

    rows = D // n_dp
    moving = Transfers(pos, (counts[-1], labels), n_dp)

    down_names = [(0, b * rows, (0, HALF)) for b in range(4)]
    up_names = [(1, 0, (b * D, b * D + HALF)) for b in range(4)]
    first_names, last_names = [], []
    for b in range(3):
        for at in (b * D, b * D + LANES):
            first_names.append((2, 0, (at, at + 2 * LANES)))
        first_names.append((3, 0, (2 * b * LANES, (2 * b + 1) * LANES)))
        last_names.append((2, 0, (b * D + 4 * LANES, b * D + 5 * LANES)))
    chunks = {"D": down_names, "U": up_names, "F": first_names, "L": last_names}

    def begin(chunk, kind, own, other):
        moving.begin(kind, own, other, chunks[chunk], PLAN[chunk], chunk == "D")

    proj, in_one, att, probs, mid, in_two = forward(
        x, segments, gamma_one, beta_one, w_qkv, b_query, b_value, w_out, b_out, gamma_two, beta_two
    )
    act, slope, own, other = up(pos, in_two, cot, w_up, b_up, counts[:1])
    begin("D", "rows", own, other)
    after = []
    for step in SCHEDULE:
        if step == "hidden":
            gp, go, own, other, sum_up, sum_down = hidden(pos, counts[-1], labels, cot, in_two, slope, w_down)
            begin("U", "blocks", own, other)
            after = [gp]
        elif step == "middle":
            gm, gb, ga, sums_mid = middle_back(go, mid, gamma_two, gp, w_up, w_out, after)
            after = [ga]
        elif step == "attend first":
            first = attend_back(proj, ga, probs, 0, 4, after)
            after = [first]
        elif step == "first heads":
            own, other = first_heads(pos, in_one, first, att, gb, after)
            begin("F", "blocks", own, other)
            after = [own]
        elif step == "attend last":
            last = attend_back(proj, ga, probs, 4, 2, after)
            after = [last]
        elif step == "last heads":
            own, other = last_heads(pos, in_one, last, after)
            begin("L", "blocks", own, other)
            after = [own]
        elif step == "input":
            grad_tokens, vectors = input_back(
                x, gm, gamma_one, first, last, w_qkv, sums_mid, sum_down, sum_up, after
            )
            moving.vectors = Vectors(vectors, n_dp)
            after = [grad_tokens]
        elif step == "mix":
            mixed = mix(mid, act, w_down, b_down, after)
            after = [mixed]
        else:
            wanted = []
            for item in step:
                if item == "V":
                    wanted.append("vectors")
                else:
                    first_block = sum(count for count, _ in PLAN[item[0]][: int(item[1])])
                    wanted.append(chunks[item[0]][first_block])
            after = moving.tick(wanted, after)
    after = moving.finish(after)
    *singles, grad_b_up, grad_down, grad_up, grad_qkv, grad_out = place(
        pos, moving.mine, [(4 * rows, D), (rows, FF), (rows, 3 * D), (rows, D)], after, moving.vectors
    )
    query, value, gain_one, shift_one, gain_two, shift_two, out, bias_down = singles
    return (
        mixed.reshape(tokens.shape),
        grad_tokens.reshape(tokens.shape),
        grad_qkv,
        query,
        value,
        grad_out,
        out,
        gain_one,
        shift_one,
        gain_two,
        shift_two,
        grad_up,
        grad_b_up,
        grad_down,
        bias_down,
        counts[-1],
    )


def solution(mesh):
    split = P(("dp", "group"), None, None)
    return jax.shard_map(
        functools.partial(per_device, n_dp=mesh.shape["dp"]),
        mesh=mesh,
        in_specs=(split, P(("dp", "group"), None), P(("dp", "group")), split) + (P(),) * 13,
        out_specs=(split, split, P("dp", None), P("dp"), P("dp"), P("dp", None))
        + (P("dp"),) * 5
        + (P("dp", None), P("dp"), P("dp", None), P("dp"), P()),
        check_vma=False,
    )
```
